128 devices in a mesh: dp: 32 (over z, y, x_lo), tensor: 4 (over x_hi, core).
Axes of the slice: x: 4 (x_hi: 2, x_lo: 2; x = x_hi * 2 + x_lo), y: 4, z: 4, core: 2. Of those that a mesh axis runs over, the one named last changes fastest.
Arguments:
- tokens: bfloat16 [32, 1024, 1024], P('dp', 'tensor'), may hold values from -6 to 6
- doc_starts: int32 [32, 4], P('dp'), may hold values from 0 to 1023, as said below
- cotangent: bfloat16 [32, 1024, 1024], P('dp', 'tensor'), may hold values from -12 to 12
- w_query: bfloat16 [1024, 2048], P(None, 'tensor'), may hold values from -0.1875 to 0.1875
- key_matrix: bfloat16 [1024, 1024], P(None, 'tensor'), may hold values from -0.1875 to 0.1875
- value_matrix: bfloat16 [1024, 1024], P(None, 'tensor'), may hold values from -0.1875 to 0.1875
- w_out: bfloat16 [2048, 1024], P('tensor'), may hold values from -0.75 to 0.75
- w_gate: bfloat16 [1024, 3072], P(None, 'tensor'), may hold values from -0.1875 to 0.1875
- w_up: bfloat16 [1024, 3072], P(None, 'tensor'), may hold values from -0.1875 to 0.1875
- w_down: bfloat16 [3072, 1024], P('tensor'), may hold values from -0.21875 to 0.21875
- gain_attn: float32 [1024], replicated, may hold values from 0.5 to 1.5
- gain_mlp: float32 [1024], replicated, may hold values from 0.5 to 1.5
- gain_query: float32 [128], replicated, may hold values from 0.5 to 1.5
- gain_key: float32 [128], replicated, may hold values from 0.5 to 1.5
Outputs:
- layer_out: bfloat16 [32, 1024, 1024], P('dp', 'tensor')
- grad_tokens: float32 [32, 1024, 1024], P('dp', 'tensor')
- grad_w_query: float32 [1024, 2048], P('dp', 'tensor')
- grad_w_key: float32 [1024, 1024], P('dp', 'tensor')
- grad_w_value: float32 [1024, 1024], P('dp', 'tensor')
- grad_w_out: float32 [2048, 1024], P('tensor', 'dp')
- grad_w_gate: float32 [1024, 3072], P('dp', 'tensor')
- grad_w_up: float32 [1024, 3072], P('dp', 'tensor')
- grad_w_down: float32 [3072, 1024], P('tensor', 'dp')
- grad_gain_attn: float32 [1024], replicated
- grad_gain_mlp: float32 [1024], replicated
- grad_gain_query: float32 [128], replicated
- grad_gain_key: float32 [128], replicated
The draws below stay inside these ranges and needn't reach their ends.
Inputs may be any that keep to these rules, and one draw needn't show every extreme that they name: `doc_starts`: each row lists the first tokens of 4 documents that tile a sequence of 1024 tokens in order: the first is 0 and they rise strictly. In each sequence one document, at a place drawn from the seed, starts before token 193 and reaches token 831; each other document has at most 64 tokens.
All inputs are finite; a program needn't handle non-finite values.
Results may differ from the reference program's by a relative error of at most 0.03.
Values may be sent and summed in bfloat16 or wider, within the bound.
A program may use at most 128 MiB of HBM per device.

```python
import jax
import jax.numpy as jnp
from jax import lax

MODEL_DIM = 1024
QUERY_HEADS = 16
KEY_VALUE_HEADS = 8
HEAD_DIM = 128
FF = 3072
SEQ_LEN = 1024
NDOC = 4
SEQUENCES = 32


def draw_doc_starts(key, part):
    key = jax.random.fold_in(key, 11)
    key_length, key_choose = jax.random.split(key)
    shorts = jax.random.randint(key_length, (SEQUENCES, NDOC), 1, SEQ_LEN // 16 + 1)
    long_index = jax.random.randint(key_choose, (SEQUENCES, 1), 0, NDOC)
    slot_index = jnp.arange(NDOC, dtype=jnp.int32)[None, :]
    is_long = slot_index == long_index
    shorts = jnp.where(is_long, 0, shorts)
    long_length = SEQ_LEN - jnp.sum(shorts, axis=1, keepdims=True)
    lengths = jnp.where(is_long, long_length, shorts)
    starts = jnp.cumsum(lengths, axis=1) - lengths
    return starts.astype(jnp.int32)


def raised(array, own_key, source, target, blocks, factor):
    owner, partner = [(jnp.arange(array.shape[dim]) // (array.shape[dim] // blocks)).reshape([-1 if axis == dim else 1 for axis in range(array.ndim)]) for dim in (source, target)]
    chosen = jax.random.permutation(own_key, blocks)[partner]
    strong = (owner == chosen) | (owner == (partner + blocks // 2) % blocks)
    return jnp.where(strong, factor * array, array)


def steps_of(key, extent, cuts, low, high):
    level, own = 1.0, jax.random.fold_in(key, 6)
    for axis_at, parts in cuts:
        steps = jnp.exp(jax.random.uniform(jax.random.fold_in(own, axis_at), (parts,), jnp.float32, low / len(cuts), high / len(cuts)))
        level = level * jnp.repeat(steps, extent[axis_at] // parts).reshape([-1 if axis == axis_at else 1 for axis in range(len(extent))])
    return level


def centred(own_key, extent, width, limit, shards=(), kind=jnp.bfloat16):
    entries = jax.random.normal(own_key, extent, jnp.float32) * width
    if len(shards) > 0:
        entries = steps_of(own_key, extent, shards, -0.22, 0.18) * entries
    return jnp.clip(entries, min=-limit, max=limit).astype(kind)


def bell_draw_with(own_key, shape, deviation, reach, cuts, heavy, kind=jnp.bfloat16):
    values = deviation * jax.random.normal(own_key, shape, jnp.float32)
    if cuts:
        values = values * steps_of(own_key, shape, cuts, -0.22, 0.18)
    return jnp.clip(raised(values, jax.random.fold_in(own_key, 3), *heavy), -reach, reach).astype(kind)


def setup_inputs(seed: int = 0) -> dict:
    streams_of = jax.random.split(jax.random.key(seed), 15)
    tokens = centred(streams_of[0], (SEQUENCES, SEQ_LEN, MODEL_DIM), 1.0, 6.0, ((0, 32), (1, 4)))
    doc_starts = draw_doc_starts(jax.random.fold_in(streams_of[14], 71), 0)
    cotangent = bell_draw_with(streams_of[2], (SEQUENCES, SEQ_LEN, MODEL_DIM), 1.0, 12.0, ((0, 32), (1, 4)), (0, 2, 32, 2.75))
    w_query = centred(streams_of[3], (MODEL_DIM, QUERY_HEADS * HEAD_DIM), MODEL_DIM ** -0.5, 0.1875, ((1, 4),))
    key_matrix = centred(streams_of[4], (MODEL_DIM, KEY_VALUE_HEADS * HEAD_DIM), MODEL_DIM ** -0.5, 0.1875, ((1, 4),))
    value_matrix = centred(streams_of[5], (MODEL_DIM, KEY_VALUE_HEADS * HEAD_DIM), MODEL_DIM ** -0.5, 0.1875, ((1, 4),))
    w_out = centred(streams_of[6], (QUERY_HEADS * HEAD_DIM, MODEL_DIM), (QUERY_HEADS * HEAD_DIM // 32) ** -0.5, 0.75, ((0, 4),))
    w_gate = centred(streams_of[7], (MODEL_DIM, FF), MODEL_DIM ** -0.5, 0.1875, ((1, 4),))
    w_up = centred(streams_of[8], (MODEL_DIM, FF), MODEL_DIM ** -0.5, 0.1875, ((1, 4),))
    w_down = centred(streams_of[9], (FF, MODEL_DIM), (FF // 4) ** -0.5, 0.21875, ((0, 4),))
    gain_attn = jnp.clip(1.0 + 0.1 * jax.random.normal(streams_of[10], (MODEL_DIM,), jnp.float32), 0.5, 1.5)
    gain_mlp = jnp.clip(1.0 + 0.1 * jax.random.normal(streams_of[11], (MODEL_DIM,), jnp.float32), 0.5, 1.5)
    gain_query = jnp.clip(1.0 + 0.1 * jax.random.normal(streams_of[12], (HEAD_DIM,), jnp.float32), 0.5, 1.5)
    gain_key = jnp.clip(1.0 + 0.1 * jax.random.normal(streams_of[13], (HEAD_DIM,), jnp.float32), 0.5, 1.5)
    return dict(tokens=tokens, doc_starts=doc_starts, cotangent=cotangent, w_query=w_query, key_matrix=key_matrix, value_matrix=value_matrix, w_out=w_out, w_gate=w_gate, w_up=w_up, w_down=w_down, gain_attn=gain_attn, gain_mlp=gain_mlp, gain_query=gain_query, gain_key=gain_key)


@jax.custom_vjp
def lowered_rows(v):
    return lax.optimization_barrier(v.astype(jnp.bfloat16)).astype(jnp.float32)

@jax.custom_vjp
def lowered_backward(v):
    return v

def low_keep(v):
    return (lowered_rows(v), None)

def low_pass(kept, grad):
    return (grad,)

def back_keep(v):
    return (v, None)

def back_low(kept, grad):
    return (lowered_rows(grad),)
lowered_rows.defvjp(low_keep, low_pass)
lowered_backward.defvjp(back_keep, back_low)
epsilon = 1e-06
rope_base = 1000000.0
masked_fill = -1e+30
highest = lax.Precision.HIGHEST

def rms_scale(values, scale_gain):
    return values * lax.rsqrt(lax.optimization_barrier(jnp.mean(values * values, axis=-1, keepdims=True)) + epsilon) * scale_gain

def doc_layout(starts, token_length):
    place_index = jnp.arange(token_length, dtype=jnp.int32)
    started = place_index[:, None] >= starts[..., None, :]
    doc_index = lax.optimization_barrier(jnp.sum(started.astype(jnp.int32), axis=-1))
    doc_first = lax.optimization_barrier(jnp.max(jnp.where(started, starts[..., None, :], 0), axis=-1))
    return (doc_index, place_index - doc_first)

def rope_tables(position, head_width):
    half_width = head_width // 2
    frequency = rope_base ** (-(jnp.arange(half_width, dtype=jnp.float32) * 2.0) / head_width)
    angles = position.astype(jnp.float32)[..., None] * frequency
    return (jnp.cos(angles), jnp.sin(angles))

def rotate(values, cosine_table, sine_table):
    half_width = values.shape[-1] // 2
    first_half = values[..., :half_width]
    second_half = values[..., half_width:]
    cosine_heads = cosine_table[..., None, :]
    sine_heads = sine_table[..., None, :]
    return jnp.concatenate([first_half * cosine_heads - second_half * sine_heads, second_half * cosine_heads + first_half * sine_heads], axis=-1)

def matrix_product(left_side, right_side):
    return jnp.dot(left_side, right_side, precision=highest)

def layer(inputs, params, doc_index, position):
    w_query, key_matrix, value_matrix, w_out, w_gate, w_up, w_down, gain_attn, gain_mlp, gain_query, gain_key = params
    token_length = inputs.shape[0]
    cosine_table, sine_table = rope_tables(position, HEAD_DIM)
    normalized_rows = lowered_rows(rms_scale(inputs, gain_attn))
    raw_query = lowered_backward(matrix_product(normalized_rows, w_query)).reshape(token_length, QUERY_HEADS, HEAD_DIM)
    unrotated_key = lowered_backward(matrix_product(normalized_rows, key_matrix)).reshape(token_length, KEY_VALUE_HEADS, HEAD_DIM)
    lowered_value = lowered_rows(lowered_backward(matrix_product(normalized_rows, value_matrix))).reshape(token_length, KEY_VALUE_HEADS, HEAD_DIM)
    rotated_query = lowered_rows(rotate(rms_scale(raw_query, gain_query), cosine_table, sine_table))
    key_rot = lowered_rows(rotate(rms_scale(unrotated_key, gain_key), cosine_table, sine_table))
    grouped_heads = rotated_query.reshape(token_length, KEY_VALUE_HEADS, QUERY_HEADS // KEY_VALUE_HEADS, HEAD_DIM)
    scores = lowered_backward(jnp.einsum('qhgd,khd->hgqk', grouped_heads, key_rot, precision=highest) * HEAD_DIM ** (-0.5))
    place_index = jnp.arange(token_length, dtype=jnp.int32)
    allowed = (doc_index[:, None] == doc_index[None, :]) & (place_index[:, None] >= place_index[None, :])
    scores = jnp.where(allowed[None, None], scores, masked_fill)
    probabilities = jax.nn.softmax(scores, axis=-1)
    attended = jnp.einsum('hgqk,khd->qhgd', lowered_rows(probabilities), lowered_value, precision=highest)
    attended = lowered_rows(lowered_backward(attended)).reshape(token_length, QUERY_HEADS * HEAD_DIM)
    residual = inputs + lowered_backward(matrix_product(attended, w_out))
    normed_mlp = lowered_rows(rms_scale(residual, gain_mlp))
    gate_rows = lowered_backward(matrix_product(normed_mlp, w_gate))
    up_rows = lowered_backward(matrix_product(normed_mlp, w_up))
    hidden = lowered_rows(jax.nn.silu(gate_rows) * up_rows)
    return residual + lowered_backward(matrix_product(hidden, w_down))

def reference(tokens, doc_starts, cotangent, w_query, key_matrix, value_matrix, w_out, w_gate, w_up, w_down, gain_attn, gain_mlp, gain_query, gain_key):
    params = tuple((weight_item.astype(jnp.float32) for weight_item in (w_query, key_matrix, value_matrix, w_out, w_gate, w_up, w_down, gain_attn, gain_mlp, gain_query, gain_key)))

    def one_sequence(grad_total, bundle):
        seq_tokens, seq_starts, seq_cotangent = bundle
        doc_index, position = doc_layout(seq_starts, SEQ_LEN)

        def forward(inputs, weights_all):
            return layer(inputs, weights_all, doc_index, position)
        output, backward = jax.vjp(forward, seq_tokens.astype(jnp.float32), params)
        grad_inputs, grad_params = backward(seq_cotangent.astype(jnp.float32))
        grad_total = tuple((total_item + grad_item for total_item, grad_item in zip(grad_total, grad_params)))
        return (grad_total, (output.astype(jnp.bfloat16), grad_inputs))
    zeros_all = tuple((jnp.zeros_like(weight_item) for weight_item in params))
    grad_total, (layer_out, grad_tokens) = lax.scan(one_sequence, zeros_all, (tokens, doc_starts, cotangent))
    return (layer_out, grad_tokens, grad_total[0], grad_total[1], grad_total[2], grad_total[3], grad_total[4], grad_total[5], grad_total[6], grad_total[7], grad_total[8], grad_total[9], grad_total[10])
```

```python
import jax
import jax.numpy as jnp
from jax import lax
from jax.experimental import pallas as pl
from jax.experimental.pallas import tpu as pltpu
from jax.sharding import PartitionSpec as P

MESH = pl.DeviceIdType.MESH
STREAMS = ((0, 1024), (1024, 1024), (2048, 896), (2944, 896))
ORDERS = (("y1", "y2", "z1", "z2"), ("y2", "y1", "z2", "z1"), ("z1", "z2", "y1", "y2"), ("z2", "z1", "y2", "y1"))
GAIN_ORDER = ("core", "y1", "y2", "z1", "z2", "x", "far")


class Place:
    def __init__(self):
        dp = lax.axis_index("dp")
        tensor = lax.axis_index("tensor")
        self.z, self.y, self.x = dp // 8, (dp // 2) % 4, dp % 2
        self.far, self.core = tensor // 2, tensor % 2

    def near(self, name):
        value = self.y if name[0] == "y" else self.z
        return value + 1 - 2 * (value % 2) if name[1] == "1" else 3 - value

    def device(self, name):
        z, y, x, far, core = self.z, self.y, self.x, self.far, self.core
        if name[0] == "y":
            y = self.near(name)
        elif name[0] == "z":
            z = self.near(name)
        elif name == "x":
            x = 1 - x
        elif name == "far":
            far = 1 - far
        else:
            core = 1 - core
        return ((z * 4 + y) * 2 + x, far * 2 + core)


def remote(src, dst, sems, index, device):
    copy = pltpu.make_async_remote_copy(
        src_ref=src,
        dst_ref=dst,
        send_sem=sems.at[0, index],
        recv_sem=sems.at[1, index],
        device_id=device,
        device_id_type=MESH,
    )
    copy.start()
    return copy


def sum_kernel(grads, gains, out, gains_out, *scratch):
    halves = scratch[:20]
    gain_parts, sems, gain_sems = scratch[20:]
    place = Place()
    barrier = pltpu.get_barrier_semaphore()
    for name in GAIN_ORDER:
        pl.semaphore_signal(barrier, inc=1, device_id=place.device(name), device_id_type=MESH)
    pl.semaphore_wait(barrier, len(GAIN_ORDER))

    def piece(stream, ref, axis, at):
        first, width = STREAMS[stream]
        columns = pl.ds(first, width)
        return ref.at[:, at, :, :, columns] if axis == "y" else ref.at[at, :, :, :, columns]

    def begin(stream, phase):
        order = ORDERS[stream]
        bufs = halves[stream * 5 : stream * 5 + 5]
        base = stream * 7
        if phase == 4:
            return [remote(bufs[3].at[1 - place.x], bufs[4], sems, base + 6, place.device("x"))]
        name = order[phase]
        partner = place.device(name)
        if phase in (1, 3):
            source = bufs[phase - 1].at[1]
            return [remote(source, bufs[phase], sems, base + (2 if phase == 1 else 5), partner)]
        there = place.near(name)
        other = place_other(order[phase + 1], there)
        copies = []
        for j, at in enumerate((there, other)):
            source = piece(stream, grads, name[0], at) if phase == 0 else bufs[1].at[at]
            copies.append(remote(source, bufs[phase].at[j], sems, base + (j if phase == 0 else 3 + j), partner))
        return copies

    def place_other(name, value):
        return value + 1 - 2 * (value % 2) if name[1] == "1" else 3 - value

    def finish(stream, phase, copies):
        order = ORDERS[stream]
        bufs = halves[stream * 5 : stream * 5 + 5]
        for copy in copies:
            copy.wait_recv()
        first, width = STREAMS[stream]
        if phase == 4:
            out[:, first : first + width] = bufs[4][...].astype(jnp.float32) + bufs[3][place.x].astype(jnp.float32)
        elif phase in (1, 3):
            bufs[phase][...] += bufs[phase - 1][0]
        else:
            name = order[phase]
            mine = place.y if name[0] == "y" else place.z
            for j, at in enumerate((mine, place_other(order[phase + 1], mine))):
                if phase == 0:
                    for k in range(4):
                        kept = grads[k, at, :, :, first : first + width] if name[0] == "y" else grads[at, k, :, :, first : first + width]
                        bufs[0][j, k] += kept
                else:
                    bufs[2][j] += bufs[1][at]

    started = []
    flying = [begin(stream, 0) for stream in range(4)]
    gain_parts[0] = gains[...]
    gain_copies = [remote(gain_parts.at[0], gain_parts.at[7], gain_sems, 0, place.device(GAIN_ORDER[0]))]
    for phase in range(5):
        for stream in range(4):
            finish(stream, phase, flying[stream])
            started += flying[stream]
            if phase < 4:
                flying[stream] = begin(stream, phase + 1)
        for step in ((0, 1), (2,), (3,), (4,), (5, 6))[phase]:
            gain_copies[step].wait_recv()
            total = gain_parts[step] + gain_parts[7 + step]
            if step < 6:
                gain_parts[step + 1] = total
                gain_copies.append(
                    remote(
                        gain_parts.at[step + 1],
                        gain_parts.at[8 + step],
                        gain_sems,
                        step + 1,
                        place.device(GAIN_ORDER[step + 1]),
                    )
                )
            else:
                gains_out[...] = total
    for copy in started + gain_copies:
        copy.wait_send()


def sum_gradients(grads, gains):
    columns = grads.shape[1]
    scratch = []
    for first, width in STREAMS:
        for lead in ((2, 4, 2), (4, 2), (2, 2), (2,), ()):
            scratch.append(pltpu.VMEM((*lead, 32, width), jnp.bfloat16))
    scratch.append(pltpu.VMEM((14, *gains.shape), jnp.float32))
    scratch.append(pltpu.SemaphoreType.DMA((2, 28)))
    scratch.append(pltpu.SemaphoreType.DMA((2, 7)))
    return pl.pallas_call(
        sum_kernel,
        out_shape=(
            jax.ShapeDtypeStruct((32, columns), jnp.float32),
            jax.ShapeDtypeStruct(gains.shape, jnp.float32),
        ),
        in_specs=[pl.BlockSpec(memory_space=pltpu.VMEM)] * 2,
        out_specs=(pl.BlockSpec(memory_space=pltpu.VMEM),) * 2,
        scratch_shapes=scratch,
        compiler_params=pltpu.CompilerParams(
            collective_id=0, has_side_effects=True, vmem_limit_bytes=48 * 2**20
        ),
        name="sum_gradients",
    )(grads.reshape(4, 4, 2, 32, columns), gains)

epsilon = 1e-06
rope_base = 1000000.0
masked_fill = -1e30


def rms_scale(values, scale_gain):
    return (
        values * lax.rsqrt(jnp.mean(values * values, axis=-1, keepdims=True) + epsilon) * scale_gain
    )


def doc_layout(starts, token_length):
    place_index = jnp.arange(token_length, dtype=jnp.int32)
    started = place_index[:, None] >= starts[..., None, :]
    doc_index = jnp.sum(started.astype(jnp.int32), axis=-1)
    doc_first = jnp.max(jnp.where(started, starts[..., None, :], 0), axis=-1)
    return (doc_index, place_index - doc_first)


def rope_tables(position, head_width):
    half_width = head_width // 2
    frequency = rope_base ** (-(jnp.arange(half_width, dtype=jnp.float32) * 2.0) / head_width)
    angles = position.astype(jnp.float32)[..., None] * frequency
    return (jnp.cos(angles), jnp.sin(angles))


def rotate(values, cosine_table, sine_table):
    half_width = values.shape[-1] // 2
    first_half = values[..., :half_width]
    second_half = values[..., half_width:]
    cosine_heads = cosine_table[..., None, :]
    sine_heads = sine_table[..., None, :]
    return jnp.concatenate(
        [
            first_half * cosine_heads - second_half * sine_heads,
            second_half * cosine_heads + first_half * sine_heads,
        ],
        axis=-1,
    )


def matrix_product(left_side, right_side):
    return jnp.dot(left_side, right_side, preferred_element_type=jnp.float32)


def outer_rows(left_side, right_side):
    return lax.dot_general(
        left_side, right_side, (((0,), (0,)), ((), ())), preferred_element_type=jnp.float32
    )


def times_transposed(left_side, right_side):
    return lax.dot_general(
        left_side, right_side, (((1,), (1,)), ((), ())), preferred_element_type=jnp.float32
    )


def allowed_mask(doc_seq):
    place_index = jnp.arange(doc_seq.shape[0], dtype=jnp.int32)
    return (doc_seq[:, None] == doc_seq[None, :]) & (place_index[:, None] >= place_index[None, :])


def score_block(query_seq, key_seq, doc_seq):
    token_length, heads_query, head_width = query_seq.shape
    heads_key = key_seq.shape[1]
    grouped_heads = query_seq.reshape(token_length, heads_key, heads_query // heads_key, head_width)
    scores = jnp.einsum(
        "qhgd,khd->hgqk", grouped_heads, key_seq, preferred_element_type=jnp.float32
    ) * head_width ** (-0.5)
    return (grouped_heads, jnp.where(allowed_mask(doc_seq)[None, None], scores, masked_fill))


def attend(bundle):
    query_seq, key_seq, value_seq, doc_seq = bundle
    token_length, heads_query, head_width = query_seq.shape
    grouped_heads, scores = score_block(query_seq, key_seq, doc_seq)
    row_top = jnp.max(scores, axis=-1, keepdims=True)
    weights = jnp.exp(scores - row_top)
    row_total = jnp.sum(weights, axis=-1, keepdims=True)
    probabilities = (weights / row_total).astype(jnp.bfloat16)
    attended = jnp.einsum(
        "hgqk,khd->qhgd", probabilities, value_seq, preferred_element_type=jnp.float32
    )
    return (attended.reshape(token_length, heads_query * head_width), row_top + jnp.log(row_total))


def attend_back(bundle):
    query_seq, key_seq, value_seq, doc_seq, log_total, grad_attended = bundle
    token_length, heads_query, head_width = query_seq.shape
    heads_key = key_seq.shape[1]
    grouped_heads, scores = score_block(query_seq, key_seq, doc_seq)
    probabilities = jnp.exp(scores - log_total)
    grad_grouped = grad_attended.reshape(
        token_length, heads_key, heads_query // heads_key, head_width
    )
    grad_probs = jnp.einsum(
        "qhgd,khd->hgqk", grad_grouped, value_seq, preferred_element_type=jnp.float32
    )
    grad_value = jnp.einsum(
        "hgqk,qhgd->khd",
        probabilities.astype(jnp.bfloat16),
        grad_grouped,
        preferred_element_type=jnp.float32,
    )
    row_inner = jnp.sum(grad_probs * probabilities, axis=-1, keepdims=True)
    grad_scores = (probabilities * (grad_probs - row_inner)).astype(jnp.bfloat16)
    score_scale = head_width ** (-0.5)
    grad_query = (
        jnp.einsum("hgqk,khd->qhgd", grad_scores, key_seq, preferred_element_type=jnp.float32)
        * score_scale
    )
    grad_key = (
        jnp.einsum("hgqk,qhgd->khd", grad_scores, grouped_heads, preferred_element_type=jnp.float32)
        * score_scale
    )
    return (grad_query.reshape(token_length, heads_query, head_width), grad_key, grad_value)


def shards(
    tokens,
    doc_starts,
    cotangent,
    w_query,
    key_matrix,
    value_matrix,
    w_out,
    w_gate,
    w_up,
    w_down,
    gain_attn,
    gain_mlp,
    gain_query,
    gain_key,
):
    seq_count, quarter, model_width = tokens.shape
    head_width = gain_query.shape[0]
    heads_query = w_query.shape[1] // head_width
    heads_key = key_matrix.shape[1] // head_width
    token_length = quarter * lax.axis_size("tensor")
    rows_all = seq_count * token_length
    doc_index, position = doc_layout(doc_starts, token_length)
    cosine_table, sine_table = rope_tables(position, head_width)

    def head_path(raw_values, scale_gain):
        return rotate(rms_scale(raw_values, scale_gain), cosine_table, sine_table)

    inputs = tokens.astype(jnp.float32)
    normed_attn = rms_scale(inputs, gain_attn).astype(jnp.bfloat16)
    gathered_attn = lax.all_gather(normed_attn, "tensor", axis=1, tiled=True).reshape(
        rows_all, model_width
    )
    raw_query = matrix_product(gathered_attn, w_query).reshape(
        seq_count, token_length, heads_query, head_width
    )
    unrotated_key = matrix_product(gathered_attn, key_matrix).reshape(
        seq_count, token_length, heads_key, head_width
    )
    value_seq = (
        matrix_product(gathered_attn, value_matrix)
        .astype(jnp.bfloat16)
        .reshape(seq_count, token_length, heads_key, head_width)
    )
    rotated_query = head_path(raw_query, gain_query).astype(jnp.bfloat16)
    key_rot = head_path(unrotated_key, gain_key).astype(jnp.bfloat16)
    attended, log_total = lax.map(attend, (rotated_query, key_rot, value_seq, doc_index))
    attended_low = attended.astype(jnp.bfloat16).reshape(rows_all, heads_query * head_width)
    attn_part = matrix_product(attended_low, w_out).reshape(seq_count, token_length, model_width)
    attn_share = lax.psum_scatter(
        attn_part.astype(jnp.bfloat16), "tensor", scatter_dimension=1, tiled=True
    ).astype(jnp.float32)
    residual = inputs + attn_share
    normed_mlp = rms_scale(residual, gain_mlp).astype(jnp.bfloat16)
    gathered_mlp = lax.all_gather(normed_mlp, "tensor", axis=1, tiled=True).reshape(
        rows_all, model_width
    )
    gate_rows = matrix_product(gathered_mlp, w_gate)
    up_rows = matrix_product(gathered_mlp, w_up)
    hidden = (jax.nn.silu(gate_rows) * up_rows).astype(jnp.bfloat16)
    mlp_part = matrix_product(hidden, w_down).reshape(seq_count, token_length, model_width)
    mlp_share = lax.psum_scatter(
        mlp_part.astype(jnp.bfloat16), "tensor", scatter_dimension=1, tiled=True
    ).astype(jnp.float32)
    layer_out = (residual + mlp_share).astype(jnp.bfloat16)
    grad_rows = lax.all_gather(cotangent, "tensor", axis=1, tiled=True).reshape(
        rows_all, model_width
    )
    grad_w_down = outer_rows(grad_rows, hidden)
    grad_hidden = times_transposed(grad_rows, w_down)
    sigmoid_rows = jax.nn.sigmoid(gate_rows)
    grad_gate = (
        grad_hidden * up_rows * sigmoid_rows * (1.0 + gate_rows * (1.0 - sigmoid_rows))
    ).astype(jnp.bfloat16)
    grad_up = (grad_hidden * jax.nn.silu(gate_rows)).astype(jnp.bfloat16)
    grad_w_gate = outer_rows(gathered_mlp, grad_gate)
    grad_w_up = outer_rows(gathered_mlp, grad_up)
    grad_normed_mlp = (
        times_transposed(grad_gate, w_gate) + times_transposed(grad_up, w_up)
    ).reshape(seq_count, token_length, model_width)
    grad_mlp_share = lax.psum_scatter(
        grad_normed_mlp.astype(jnp.bfloat16), "tensor", scatter_dimension=1, tiled=True
    ).astype(jnp.float32)
    mlp_norm_back = jax.vjp(rms_scale, residual, gain_mlp)[1]
    grad_resid_norm, grad_gain_mlp = mlp_norm_back(grad_mlp_share)
    grad_residual = cotangent.astype(jnp.float32) + grad_resid_norm
    grad_attn_rows = lax.all_gather(
        grad_residual.astype(jnp.bfloat16), "tensor", axis=1, tiled=True
    ).reshape(rows_all, model_width)
    grad_w_out = outer_rows(grad_attn_rows, attended_low)
    grad_attended = (
        times_transposed(grad_attn_rows, w_out)
        .astype(jnp.bfloat16)
        .reshape(seq_count, token_length, heads_query * head_width)
    )
    grad_query_rot, grad_key_rot, grad_value = lax.map(
        attend_back, (rotated_query, key_rot, value_seq, doc_index, log_total, grad_attended)
    )
    query_back = jax.vjp(head_path, raw_query, gain_query)[1]
    grad_raw_query, grad_gain_query = query_back(grad_query_rot)
    key_back = jax.vjp(head_path, unrotated_key, gain_key)[1]
    grad_raw_key, grad_gain_key = key_back(grad_key_rot)
    grad_query_low = grad_raw_query.astype(jnp.bfloat16).reshape(rows_all, heads_query * head_width)
    grad_key_low = grad_raw_key.astype(jnp.bfloat16).reshape(rows_all, heads_key * head_width)
    grad_value_low = grad_value.astype(jnp.bfloat16).reshape(rows_all, heads_key * head_width)
    grad_w_query = outer_rows(gathered_attn, grad_query_low)
    grad_w_key = outer_rows(gathered_attn, grad_key_low)
    grad_w_value = outer_rows(gathered_attn, grad_value_low)
    grad_normed_attn = (
        times_transposed(grad_query_low, w_query)
        + times_transposed(grad_key_low, key_matrix)
        + times_transposed(grad_value_low, value_matrix)
    ).reshape(seq_count, token_length, model_width)
    grad_attn_share = lax.psum_scatter(
        grad_normed_attn.astype(jnp.bfloat16), "tensor", scatter_dimension=1, tiled=True
    ).astype(jnp.float32)
    attn_norm_back = jax.vjp(rms_scale, inputs, gain_attn)[1]
    grad_inputs_norm, grad_gain_attn = attn_norm_back(grad_attn_share)
    grad_tokens = grad_residual + grad_inputs_norm
    all_grads = jnp.concatenate(
        [grad_w_query, grad_w_key, grad_w_value, grad_w_out, grad_w_gate, grad_w_up, grad_w_down], axis=1
    ).astype(jnp.bfloat16)
    all_gains = jnp.concatenate(
        [grad_gain_attn, grad_gain_mlp, grad_gain_query, grad_gain_key, jnp.zeros((6 * 128,), jnp.float32)]
    ).reshape(24, 128)
    summed, gain_sums = sum_gradients(all_grads, all_gains)
    gain_sums = gain_sums.reshape(-1)
    return (
        layer_out,
        grad_tokens,
        summed[:, :512],
        summed[:, 512:768],
        summed[:, 768:1024],
        summed[:, 1024:1536].T,
        summed[:, 1536:2304],
        summed[:, 2304:3072],
        summed[:, 3072:].T,
        gain_sums[:1024],
        gain_sums[1024:2048],
        gain_sums[2048:2176],
        gain_sums[2176:2304],
    )


def solution(mesh):
    in_specs = (
        P("dp", "tensor", None),
        P("dp", None),
        P("dp", "tensor", None),
        P(None, "tensor"),
        P(None, "tensor"),
        P(None, "tensor"),
        P("tensor", None),
        P(None, "tensor"),
        P(None, "tensor"),
        P("tensor", None),
        P(),
        P(),
        P(),
        P(),
    )
    out_specs = (
        P("dp", "tensor", None),
        P("dp", "tensor", None),
        P("dp", "tensor"),
        P("dp", "tensor"),
        P("dp", "tensor"),
        P("tensor", "dp"),
        P("dp", "tensor"),
        P("dp", "tensor"),
        P("tensor", "dp"),
        P(),
        P(),
        P(),
        P(),
    )
    return jax.shard_map(shards, mesh=mesh, in_specs=in_specs, out_specs=out_specs, check_vma=False)
```

```python
import math

import jax
import jax.numpy as jnp
import numpy as np
from jax import lax
from jax.experimental import pallas as pl
from jax.experimental.pallas import tpu as pltpu
from jax.sharding import PartitionSpec as P

MESH = pl.DeviceIdType.MESH
BF16 = jnp.bfloat16
F32 = jnp.float32
EPSILON = 1e-06
ROPE_BASE = 1000000.0
BLOCK = 256
HEAD = 128
QUERY_SCALE = math.log2(math.e) / math.sqrt(HEAD)
PARTNERS = ("core", "far", "y1", "y2", "z1", "z2", "x")
ORDERS = (("y1", "y2", "z1", "z2"), ("y2", "y1", "z2", "z1"), ("z1", "z2", "y1", "y2"), ("z2", "z1", "y2", "y1"))
MLP_WIDTHS = (640, 640, 512, 512)
ATTN_WIDTHS = (384, 384, 384, 384)
GAIN_ORDER = ("core", "y1", "y2", "z1", "z2", "x", "far")

SCRATCH = (
    ("w_qkv", (1024, 1024), BF16),
    ("t_qkv", (1024, 1024), BF16),
    ("w_down", (768, 1024), BF16),
    ("t_gu", (1536, 1024), BF16),
    ("mlp_mix", (4, 4, 64, 2304), BF16),
    ("attn_mix", (4, 4, 64, 1536), BF16),
    ("h1", (1024, 1024), BF16),
    ("h2", (1024, 1024), BF16),
    ("da", (1024, 1024), BF16),
    ("norm_qk", (768, 1024), BF16),
    ("root_qk", (8, 1024), F32),
    ("ob", (512, 1024), BF16),
    ("qs", (2, 4, 128, 512), BF16),
    ("ks_t", (256, 1024), BF16),
    ("ks", (2, 1024, 128), BF16),
    ("v_t", (2, 144, 1024), BF16),
    ("v", (2, 1024, 128), BF16),
    ("p", (20, 4, 64, 512), BF16),
    ("inv", (2, 4, 8, 512), F32),
    ("inner", (2, 4, 8, 512), F32),
    ("mask", (10, 256, 256), BF16),
    ("hidden", (768, 1024), BF16),
    ("dgu", (1536, 1024), BF16),
    ("cosine", (64, 1024), F32),
    ("sine", (64, 1024), F32),
    ("x_t", (1024, 256), BF16),
    ("resid", (1024, 256), F32),
    ("gain1", (1024, 128), F32),
    ("gain2", (1024, 128), F32),
    ("gain_q", (128, 128), F32),
    ("gain_k", (128, 128), F32),
    ("gain_sum", (1024, 128), F32),
    ("gain_q_sum", (128, 256), F32),
    ("gain_k_sum", (128, 256), F32),
    ("root1", (8, 256), F32),
    ("root2", (8, 256), F32),
    ("acc_o", (144, 512), F32),
    ("acc_q", (128, 512), F32),
    ("keep_far", (1024, 256), F32),
    ("keep_own", (1024, 256), F32),
    ("sib_out", (2, 1024, 256), BF16),
    ("sib_in", (2, 1024, 256), BF16),
    ("far_out", (1024, 256), BF16),
    ("far_in", (1024, 256), BF16),
    ("mlp_own", (1024, 256), F32),
    ("mlp_sib_out", (2, 1024, 256), BF16),
    ("mlp_sib_in", (2, 1024, 256), BF16),
    ("mlp_far_out", (1024, 256), BF16),
    ("mlp_far_in", (1024, 256), BF16),
    ("mlp_halves", (16, 4, 64, 640), BF16),
    ("sums", (32, 3840), F32),
    ("gain_parts", (14, 8, 1024), F32),
)
SEMAPHORES = 120


class Box:
    pass


class Place:
    def __init__(self):
        dp = lax.axis_index("dp")
        tensor = lax.axis_index("tensor")
        self.z, self.y, self.x = dp // 8, (dp // 2) % 4, dp % 2
        self.far, self.core = tensor // 2, tensor % 2
        self.me = tensor
        self.sib = self.far * 2 + 1 - self.core
        self.across = (1 - self.far) * 2 + self.core
        self.across_sib = (1 - self.far) * 2 + 1 - self.core

    def near(self, name):
        return step_of(name, self.y if name[0] == "y" else self.z)

    def device(self, name):
        z, y, x, far, core = self.z, self.y, self.x, self.far, self.core
        if name[0] == "y":
            y = self.near(name)
        elif name[0] == "z":
            z = self.near(name)
        elif name == "x":
            x = 1 - x
        elif name == "far":
            far = 1 - far
        else:
            core = 1 - core
        return ((z * 4 + y) * 2 + x, far * 2 + core)


def step_of(name, value):
    return value + 1 - 2 * (value % 2) if name[1] == "1" else 3 - value


def nn(left, right):
    return lax.dot_general(left, right, (((1,), (0,)), ((), ())), preferred_element_type=F32)


def nt(left, right):
    return lax.dot_general(left, right, (((1,), (1,)), ((), ())), preferred_element_type=F32)


def span(index, size=BLOCK):
    return pl.ds(pl.multiple_of(index * size, size), size)


def loop(count, body):
    def step(index, carry):
        body(index)
        return carry

    lax.fori_loop(0, count, step, 0)


def twice(values):
    return jnp.concatenate([values, values], axis=1)


def fold(values):
    return jnp.sum(values.reshape(values.shape[0] // 8, 8, values.shape[1]), axis=0)


class Links:
    def __init__(self, place, sems):
        self.place, self.sems, self.used, self.sent = place, sems, 0, []

    def send(self, src, dst, name):
        copy = pltpu.make_async_remote_copy(
            src_ref=src,
            dst_ref=dst,
            send_sem=self.sems.at[0, self.used],
            recv_sem=self.sems.at[1, self.used],
            device_id=self.place.device(name),
            device_id_type=MESH,
        )
        self.used += 1
        copy.start()
        return copy


class Gather:
    def __init__(self, links, at):
        self.links, self.at = links, at
        self.far, self.sib, self.passed = [], [], []

    def send(self, half):
        block = self.at(half, self.links.place.me)
        self.far.append(self.links.send(block, block, "far"))
        self.sib.append(self.links.send(block, block, "core"))

    def pass_on(self):
        for half, copy in enumerate(self.far):
            copy.wait_recv()
            block = self.at(half, self.links.place.across)
            self.passed.append(self.links.send(block, block, "core"))

    def near_ready(self):
        for copy in self.sib:
            copy.wait_recv()

    def far_ready(self):
        for copy in self.passed:
            copy.wait_recv()

    def drain(self):
        for copy in self.far + self.sib + self.passed:
            copy.wait_send()


class Reduce:
    def __init__(self, links, sib_out, sib_in, far_out, far_in):
        self.links = links
        self.sib_out, self.sib_in, self.far_out, self.far_in = sib_out, sib_in, far_out, far_in
        self.copies = [None, None]
        self.far = []

    def to_sibling(self, index):
        self.copies[index] = self.links.send(self.sib_out.at[index], self.sib_in.at[index], "core")

    def make_far(self, keep, half):
        if half == 0:
            self.copies[0].wait_recv()

        def body(i):
            rows = span(i + 4 * half, 128)
            self.far_out[rows, :] = (keep[rows, :] + self.sib_in[0, rows, :].astype(F32)).astype(BF16)

        loop(4, body)

    def send_far(self, half):
        rows = pl.ds(512 * half, 512)
        self.far.append(self.links.send(self.far_out.at[rows], self.far_in.at[rows], "far"))

    def arrive(self):
        self.copies[1].wait_recv()
        for copy in self.far:
            copy.wait_recv()

    def total(self, keep, rows):
        return keep[rows, :] + self.sib_in[1, rows, :].astype(F32) + self.far_in[rows, :].astype(F32)

    def drain(self):
        for copy in self.copies + self.far:
            copy.wait_send()


class DpSum:
    def __init__(self, links, source, widths, bufs, out, out_first):
        self.links, self.source, self.bufs, self.out, self.out_first = links, source, bufs, out, out_first
        self.widths = widths
        self.first = [sum(widths[:k]) for k in range(4)]
        self.phase = -1
        self.flying = [[], [], [], []]
        self.sent = []

    def held(self, stream, phase):
        w = self.widths[stream]
        at = 4 * stream
        if phase == 0:
            return self.bufs.at[pl.ds(at, 2), :, :, pl.ds(0, w)]
        if phase == 1:
            return self.bufs.at[at + 2, :, :, pl.ds(0, w)]
        if phase == 2:
            return self.bufs.at[at + 3, pl.ds(0, 2), :, pl.ds(0, w)]
        if phase == 3:
            return self.bufs.at[at + 3, 2, :, pl.ds(0, w)]
        return self.bufs.at[at + 3, 3, pl.ds(0, 32), pl.ds(0, w)]

    def begin(self, stream, phase):
        place, send = self.links.place, self.links.send
        order = ORDERS[stream]
        into = self.held(stream, phase)
        if phase == 4:
            theirs = self.held(stream, 3).at[span(1 - place.x, 32)]
            return [send(theirs, into, "x")]
        name = order[phase]
        if phase in (1, 3):
            return [send(self.held(stream, phase - 1).at[1], into, name)]
        there = place.near(name)
        copies = []
        for j, at in enumerate((there, step_of(order[phase + 1], there))):
            if phase == 2:
                source = self.held(stream, 1).at[at]
            else:
                columns = pl.ds(self.first[stream], self.widths[stream])
                source = self.source.at[:, at, :, columns] if name[0] == "y" else self.source.at[at, :, :, columns]
            copies.append(send(source, into.at[j], name))
        return copies

    def finish(self, stream, phase):
        place = self.links.place
        order, first, w = ORDERS[stream], self.first[stream], self.widths[stream]
        at = 4 * stream
        bufs = self.bufs
        for copy in self.flying[stream]:
            copy.wait_recv()
        if phase == 4:
            mine = bufs[at + 3, 2, span(place.x, 32), pl.ds(0, w)].astype(F32)
            columns = pl.ds(self.out_first + first, w)
            self.out[:, columns] = bufs[at + 3, 3, pl.ds(0, 32), pl.ds(0, w)].astype(F32) + mine
        elif phase == 3:
            bufs[at + 3, 2, :, pl.ds(0, w)] += bufs[at + 3, 0, :, pl.ds(0, w)]
        elif phase == 1:
            for k in range(4):
                bufs[at + 2, k, :, pl.ds(0, w)] += bufs[at, k, :, pl.ds(0, w)]
        else:
            name = order[phase]
            mine = place.y if name[0] == "y" else place.z
            for j, own in enumerate((mine, step_of(order[phase + 1], mine))):
                if phase == 2:
                    bufs[at + 3, j, :, pl.ds(0, w)] += bufs[at + 2, own, :, pl.ds(0, w)]
                    continue
                for k in range(4):
                    lead = (k, own) if name[0] == "y" else (own, k)
                    bufs[at + j, k, :, pl.ds(0, w)] += self.source[(*lead, slice(None), pl.ds(first, w))]

    def advance(self):
        for stream in range(4):
            if self.phase >= 0:
                self.finish(stream, self.phase)
                self.sent += self.flying[stream]
            if self.phase < 4:
                self.flying[stream] = self.begin(stream, self.phase + 1)
        self.phase += 1

    def drain(self):
        for copy in self.sent:
            copy.wait_send()


def head_forward(raw, gain, cosine, sine):
    root = lax.rsqrt(jnp.mean(raw * raw, axis=0, keepdims=True) + EPSILON)
    normed = raw * root
    scaled = normed * gain
    first, second = scaled[:64], scaled[64:]
    turned = jnp.concatenate([first * cosine - second * sine, second * cosine + first * sine], axis=0)
    return normed, root, turned


def head_backward(grad, normed, root, gain, cosine, sine):
    first, second = grad[:64], grad[64:]
    turned = jnp.concatenate([first * cosine + second * sine, second * cosine - first * sine], axis=0)
    scaled = turned * gain
    inner = jnp.mean(scaled * normed, axis=0, keepdims=True)
    return root * (scaled - normed * inner), turned * normed


def layer_kernel(
    x, starts, dy, wq, wk, wv, wo, wg, wu, wd, g1, g2, gq, gk, frequency,
    out, grad_x, out_q, out_k, out_v, out_o, out_g, out_u, out_d, out_g1, out_g2, out_gq, out_gk,
    *scratch,
):
    s = Box()
    for (name, _, _), ref in zip(SCRATCH, scratch):
        setattr(s, name, ref)
    link_sems, load_sems, ready = scratch[len(SCRATCH) :]
    place = Place()
    links = Links(place, link_sems)
    me, sib, across, across_sib = place.me, place.sib, place.across, place.across_sib

    barrier = pltpu.get_barrier_semaphore()
    for name in PARTNERS:
        pl.semaphore_signal(barrier, inc=1, device_id=place.device(name), device_id_type=MESH)
    pl.semaphore_wait(barrier, len(PARTNERS))

    loads = []

    def load(src, dst):
        copy = pltpu.make_async_copy(src, dst, load_sems.at[len(loads)])
        copy.start()
        loads.append(copy)

    load(wq, s.w_qkv.at[:, pl.ds(0, 512)])
    load(wk, s.w_qkv.at[:, pl.ds(512, 256)])
    load(wv, s.w_qkv.at[:, pl.ds(768, 256)])
    load(wo, s.h2.at[pl.ds(0, 512)])
    load(wg, s.mlp_mix.at[:, :, :, pl.ds(0, 768)])
    load(wu, s.mlp_mix.at[:, :, :, pl.ds(768, 768)])
    load(wd, s.w_down)

    def first_norm(i):
        rows = span(i, 64)
        xs = x[rows, :].astype(F32)
        root = lax.rsqrt(jnp.mean(xs * xs, axis=1, keepdims=True) + EPSILON)
        out[rows, :] = (xs * root * g1[...]).astype(BF16)

    loop(4, first_norm)
    gather_h1 = Gather(links, lambda half, b: s.h1.at[pl.ds(512 * half, 512), span(b)])
    for half in range(2):
        for j in range(2):
            s.h1[pl.ds(512 * half + 256 * j, 256), span(me)] = out[:, pl.ds(512 * half + 256 * j, 256)].T
        gather_h1.send(half)

    def dy_in(i):
        s.attn_mix[i, :, :, span(me)] = dy[:, span(i)].T.reshape(4, 64, BLOCK)

    loop(4, dy_in)
    for k in range(3):
        loads[k].wait()

    def turn_qkv(i):
        s.t_qkv[span(i), :] = s.w_qkv[:, span(i)].T

    loop(4, turn_qkv)

    place_row = lax.broadcasted_iota(jnp.int32, (8, 1024), 1)
    start_row = jnp.zeros((8, 1024), jnp.int32)
    for d in range(4):
        start_row = jnp.maximum(start_row, jnp.where(place_row >= starts[0, d], starts[0, d], 0))
    position = (place_row - start_row).astype(F32)
    for i in range(8):
        lanes = pl.ds(128 * i, 128)
        angle = frequency[...] * position[0:1, 128 * i : 128 * i + 128]
        s.cosine[:, lanes] = jnp.cos(angle)
        s.sine[:, lanes] = jnp.sin(angle)
    for qb in range(4):
        first = start_row[0:1, qb * 256 : qb * 256 + 256]
        query = lax.broadcasted_iota(jnp.int32, (256, 256), 1) + qb * 256
        for kb in range(qb + 1):
            key = lax.broadcasted_iota(jnp.int32, (256, 256), 0) + kb * 256
            allowed = (key <= query) & (key >= first)
            s.mask[qb * (qb + 1) // 2 + kb] = jnp.where(allowed, 1.0, 0.0).astype(BF16)

    s.gain1[...] = jnp.broadcast_to(g1[...], (128, 1024)).T
    s.gain2[...] = jnp.broadcast_to(g2[...], (128, 1024)).T
    s.gain_q[...] = jnp.broadcast_to(gq[...], (128, 128)).T
    s.gain_k[...] = jnp.broadcast_to(gk[...], (128, 128)).T
    s.gain_q_sum[...] = jnp.zeros((128, 256), F32)
    s.gain_k_sum[...] = jnp.zeros((128, 256), F32)
    for g in range(2):
        s.v_t[g, pl.ds(128, 16), :] = jnp.ones((16, 1024), BF16)

    def x_in(i, total):
        turned = x[:, span(i)].astype(F32).T
        s.x_t[span(i), :] = turned.astype(BF16)
        return total + fold(turned * turned)

    square = lax.fori_loop(0, 4, x_in, jnp.zeros((8, BLOCK), F32))
    root = lax.rsqrt(jnp.sum(square, axis=0, keepdims=True) / 1024.0 + EPSILON)
    s.root1[...] = jnp.broadcast_to(root, (8, BLOCK))

    loads[3].wait()

    def turn_out(i):
        s.attn_mix[i, :, :, pl.ds(1024, 512)] = s.h2[pl.ds(0, 512), span(i)].T.reshape(4, 64, 512)

    loop(4, turn_out)
    loads[4].wait()
    loads[5].wait()

    def turn_gu(i):
        for z in range(4):
            s.t_gu[span(i), pl.ds(256 * z, 256)] = s.mlp_mix[z, :, :, span(i)].reshape(256, 256).T

    loop(6, turn_gu)
    loads[6].wait()

    def turn_down(i):
        s.mlp_mix[i, :, :, pl.ds(1536, 768)] = s.w_down[:, span(i)].T.reshape(4, 64, 768)

    loop(4, turn_down)

    def project(b):
        columns = span(b)
        cosine, sine = s.cosine[:, columns], s.sine[:, columns]
        for g in range(2):
            raw = nn(s.t_qkv[pl.ds(256 * g, 256), :], s.h1[:, columns])
            gain = twice(s.gain_q[...] * QUERY_SCALE)
            for k in range(2):
                head = 2 * g + k
                normed, root, turned = head_forward(raw[128 * k : 128 * k + 128], gain, cosine, sine)
                s.norm_qk[pl.ds(128 * head, 128), columns] = normed.astype(BF16)
                s.root_qk[pl.ds(head, 1), columns] = root
                s.qs[g, b, :, pl.ds(256 * k, 256)] = turned.astype(BF16)
        raw = nn(s.t_qkv[pl.ds(512, 256), :], s.h1[:, columns])
        gain = twice(s.gain_k[...])
        for g in range(2):
            normed, root, turned = head_forward(raw[128 * g : 128 * g + 128], gain, cosine, sine)
            s.norm_qk[pl.ds(512 + 128 * g, 128), columns] = normed.astype(BF16)
            s.root_qk[pl.ds(4 + g, 1), columns] = root
            s.ks_t[pl.ds(128 * g, 128), columns] = turned.astype(BF16)
            s.ks[g, columns, :] = turned.astype(BF16).T
        raw = nn(s.t_qkv[pl.ds(768, 256), :], s.h1[:, columns]).astype(BF16)
        for g in range(2):
            s.v_t[g, pl.ds(0, 128), columns] = raw[128 * g : 128 * g + 128]
            s.v[g, columns, :] = raw[128 * g : 128 * g + 128].T

    gather_h1.near_ready()
    loop(2, lambda i: project(place.far * 2 + i))
    gather_h1.pass_on()
    gather_dy = Gather(links, lambda half, b: s.attn_mix.at[pl.ds(2 * half, 2), :, :, span(b)])
    gather_dy.send(0)
    gather_dy.send(1)
    gather_h1.far_ready()
    loop(2, lambda i: project((1 - place.far) * 2 + i))

    def attend(qb):
        def group(g):
            s.acc_o[...] = jnp.zeros((144, 512), F32)

            def keys(kb):
                at = qb * (qb + 1) // 2 + kb
                scores = nn(s.ks[g, span(kb), :], s.qs[g, qb])
                weights = jnp.exp2(scores).astype(BF16) * twice(s.mask[at])
                s.p[g * 10 + at] = weights.reshape(4, 64, 512)
                s.acc_o[...] += nn(s.v_t[g, :, span(kb)], weights)

            loop(qb + 1, keys)
            inverse = 1.0 / s.acc_o[pl.ds(128, 8), :]
            s.inv[g, qb] = inverse
            attended = (s.acc_o[pl.ds(0, 128), :] * inverse[0:1]).astype(BF16)
            rows = pl.multiple_of(g * 256, 256)
            s.ob[pl.ds(rows, 128), span(qb)] = attended[:, :256]
            s.ob[pl.ds(rows + 128, 128), span(qb)] = attended[:, 256:]

        loop(2, group)

    def out_product(b, store):
        def body(i):
            store(i, nn(s.attn_mix[i, :, :, pl.ds(1024, 512)].reshape(256, 512), s.ob[:, span(b)]))

        loop(4, body)

    def to(ref, index=None):
        def store(i, values):
            if index is None:
                ref[span(i), :] = values.astype(ref.dtype)
            else:
                ref[index, span(i), :] = values.astype(ref.dtype)

        return store

    sum_attn = Reduce(links, s.sib_out, s.sib_in, s.far_out, s.far_in)
    attend(across_sib)
    out_product(across_sib, to(s.sib_out, 0))
    sum_attn.to_sibling(0)
    attend(across)
    out_product(across, to(s.keep_far))
    for half in range(2):
        sum_attn.make_far(s.keep_far, half)
        sum_attn.send_far(half)
    attend(sib)
    out_product(sib, to(s.sib_out, 1))
    sum_attn.to_sibling(1)
    attend(me)
    out_product(me, to(s.keep_own))
    gather_dy.near_ready()
    gather_dy.pass_on()
    sum_attn.arrive()

    def second_norm(i, total):
        rows = span(i, 128)
        x1 = s.x_t[rows, :].astype(F32) + sum_attn.total(s.keep_own, rows)
        s.resid[rows, :] = x1
        return total + fold(x1 * x1)

    square = lax.fori_loop(0, 8, second_norm, jnp.zeros((8, BLOCK), F32))
    root2 = lax.rsqrt(jnp.sum(square, axis=0, keepdims=True) / 1024.0 + EPSILON)
    s.root2[...] = jnp.broadcast_to(root2, (8, BLOCK))
    gather_h2 = Gather(links, lambda half, b: s.h2.at[pl.ds(512 * half, 512), span(b)])
    for half in range(2):

        def scale_rows(i, half=half):
            rows = span(i + 4 * half, 128)
            s.h2[rows, span(me)] = (s.resid[rows, :] * s.root2[0:1] * twice(s.gain2[rows, :])).astype(BF16)

        loop(4, scale_rows)
        gather_h2.send(half)
    sum_attn.drain()
    gather_dy.far_ready()

    def dy_rows(i):
        return s.attn_mix[i, :, :, pl.ds(0, 1024)].reshape(256, 1024)

    def feed(b):
        columns = span(b)

        def body(j):
            normed = s.h2[:, columns]
            gate = nn(s.t_gu[span(j), :], normed)
            up = nn(s.t_gu[pl.ds(pl.multiple_of(768 + 256 * j, 256), 256), :], normed)
            grad = nn(s.w_down[span(j), :], s.attn_mix[:, :, :, columns].reshape(1024, 256))
            open_gate = jax.nn.sigmoid(gate)
            silu = gate * open_gate
            s.hidden[span(j), columns] = (silu * up).astype(BF16)
            s.dgu[span(j), columns] = (grad * up * open_gate * (1.0 + gate * (1.0 - open_gate))).astype(BF16)
            s.dgu[pl.ds(pl.multiple_of(768 + 256 * j, 256), 256), columns] = (grad * silu).astype(BF16)

        loop(3, body)

    def feed_back(b, store):
        def body(i):
            store(i, nn(s.mlp_mix[i, :, :, pl.ds(0, 1536)].reshape(256, 1536), s.dgu[:, span(b)]))

        loop(4, body)

    def mlp_product(b, store):
        def body(i):
            store(i, nn(s.mlp_mix[i, :, :, pl.ds(1536, 768)].reshape(256, 768), s.hidden[:, span(b)]))

        loop(4, body)

    sum_dh2 = Reduce(links, s.sib_out, s.sib_in, s.far_out, s.far_in)
    gather_h2.near_ready()
    feed(sib)
    feed_back(sib, to(s.sib_out, 1))
    sum_dh2.to_sibling(1)
    feed(me)
    feed_back(me, to(s.keep_own))
    gather_h2.pass_on()
    gather_h2.far_ready()
    feed(across_sib)
    feed_back(across_sib, to(s.sib_out, 0))
    sum_dh2.to_sibling(0)
    feed(across)
    feed_back(across, to(s.keep_far))
    for half in range(2):
        sum_dh2.make_far(s.keep_far, half)
        sum_dh2.send_far(half)

    sum_mlp = Reduce(links, s.mlp_sib_out, s.mlp_sib_in, s.mlp_far_out, s.mlp_far_in)
    mlp_product(across_sib, to(s.mlp_sib_out, 0))
    sum_mlp.to_sibling(0)
    mlp_product(sib, to(s.mlp_sib_out, 1))
    sum_mlp.to_sibling(1)
    mlp_product(across, to(s.keep_far))

    def mlp_mine(i, values):
        s.mlp_own[span(i), :] = s.resid[span(i), :] + values

    mlp_product(me, mlp_mine)
    for half in range(2):
        sum_mlp.make_far(s.keep_far, half)

    def down_grad(i):
        s.mlp_mix[i, :, :, pl.ds(1536, 768)] = nt(dy_rows(i), s.hidden[...]).astype(BF16).reshape(4, 64, 768)

    loop(4, down_grad)

    def gate_up_grad(i):
        for j in range(3):
            values = nt(s.h2[span(i), :], s.dgu[pl.ds(512 * j, 512), :]).astype(BF16)
            s.mlp_mix[i, :, :, pl.ds(512 * j, 512)] = values.reshape(4, 64, 512)

    loop(4, gate_up_grad)
    gather_h2.drain()
    again = pltpu.make_async_copy(wo, s.h2.at[pl.ds(0, 512)], load_sems.at[7])
    again.start()
    dp_mlp = DpSum(links, s.mlp_mix, MLP_WIDTHS, s.mlp_halves, s.sums, 1536)
    dp_mlp.advance()

    sum_dh2.arrive()

    def norm_back_sum(i, total):
        rows = span(i, 128)
        grad = sum_dh2.total(s.keep_own, rows)
        s.keep_own[rows, :] = grad
        product = grad * (s.resid[rows, :] * s.root2[0:1])
        s.gain_sum[rows, :] = product[:, :128] + product[:, 128:]
        return total + fold(product * twice(s.gain2[rows, :]))

    inner = lax.fori_loop(0, 8, norm_back_sum, jnp.zeros((8, BLOCK), F32))
    inner = jnp.sum(inner, axis=0, keepdims=True) / 1024.0
    gather_da = Gather(links, lambda half, b: s.da.at[pl.ds(512 * half, 512), span(b)])
    for half in range(2):

        def norm_back(i, half=half):
            rows = span(i + 4 * half, 128)
            scaled = s.keep_own[rows, :] * twice(s.gain2[rows, :])
            normed = s.resid[rows, :] * s.root2[0:1]
            own = s.attn_mix[2 * half + i // 2, pl.ds(2 * (i % 2), 2), :, span(me)].reshape(128, BLOCK).astype(F32)
            dx1 = own + s.root2[0:1] * (scaled - normed * inner)
            s.resid[rows, :] = dx1
            s.da[rows, span(me)] = dx1.astype(BF16)

        loop(4, norm_back)
        gather_da.send(half)
    sum_dh2.drain()
    s.gain_parts[0, 1:2, :] = jnp.sum(s.gain_sum[...].T, axis=0, keepdims=True)
    dp_mlp.advance()

    s.keep_own[...] = jnp.zeros((1024, 256), F32)
    s.keep_far[...] = jnp.zeros((1024, 256), F32)
    again.wait()

    def out_back(b):
        def body(g):
            grads = nn(s.h2[span(g), :], s.da[:, span(b)])
            both = jnp.concatenate([grads[:128], grads[128:]], axis=1) * s.inv[g, b][0:1]
            rows = pl.multiple_of(g * 256, 256)
            outs = jnp.concatenate([s.ob[pl.ds(rows, 128), span(b)], s.ob[pl.ds(rows + 128, 128), span(b)]], axis=1)
            s.inner[g, b] = jnp.broadcast_to(jnp.sum(both * outs.astype(F32), axis=0, keepdims=True), (8, 512))
            s.t_gu[span(g * 4 + b, 128), pl.ds(0, 512)] = both.astype(BF16)

        loop(2, body)

    gather_da.near_ready()
    loop(2, lambda i: out_back(place.far * 2 + i))
    gather_da.pass_on()
    for half in range(2):
        sum_mlp.send_far(half)
    gather_da.far_ready()
    loop(2, lambda i: out_back((1 - place.far) * 2 + i))

    def out_grad(i):
        s.attn_mix[i, :, :, pl.ds(1024, 512)] = nt(s.da[span(i), :], s.ob[...]).astype(BF16).reshape(4, 64, 512)

    loop(4, out_grad)
    dp_mlp.advance()

    def attend_back(qb):
        columns = span(qb)
        cosine, sine = s.cosine[:, columns], s.sine[:, columns]
        gain = twice(s.gain_q[...])
        for g in range(2):
            s.acc_q[...] = jnp.zeros((128, 512), F32)

            def keys(kb, g=g):
                at = g * 10 + qb * (qb + 1) // 2 + kb
                rows = span(kb)
                grads = s.t_gu[span(g * 4 + qb, 128), pl.ds(0, 512)]
                weights = s.p[at].reshape(256, 512)
                slope = nn(s.v[g, rows, :], grads) - s.inner[g, qb][0:1]
                ds = (weights.astype(F32) * slope).astype(BF16)
                s.keep_own[rows, pl.ds(128 * g, 128)] += nt(weights, grads)
                s.keep_far[rows, pl.ds(128 * g, 128)] += nt(ds, s.qs[g, qb])
                s.acc_q[...] += nn(s.ks_t[pl.ds(128 * g, 128), rows], ds)

            loop(qb + 1, keys)
            for k in range(2):
                head = 2 * g + k
                grad, gain_part = head_backward(
                    s.acc_q[:, pl.ds(256 * k, 256)] * (1.0 / math.sqrt(HEAD)),
                    s.norm_qk[pl.ds(128 * head, 128), columns].astype(F32),
                    s.root_qk[pl.ds(head, 1), columns],
                    gain,
                    cosine,
                    sine,
                )
                s.t_qkv[pl.ds(128 * head, 128), columns] = grad.astype(BF16)
                s.gain_q_sum[...] += gain_part

    loop(2, attend_back)
    dp_mlp.advance()
    loop(2, lambda i: attend_back(2 + i))
    dp_mlp.advance()

    for k, name in enumerate(PARTNERS[2:]):
        pl.semaphore_signal(ready.at[k], inc=1, device_id=place.device(name), device_id_type=MESH)

    def key_back(b):
        columns = span(b)
        cosine, sine = s.cosine[:, columns], s.sine[:, columns]
        gain = twice(s.gain_k[...])
        for g in range(2):
            grad, gain_part = head_backward(
                s.keep_far[columns, pl.ds(128 * g, 128)].T * math.log(2.0),
                s.norm_qk[pl.ds(512 + 128 * g, 128), columns].astype(F32),
                s.root_qk[pl.ds(4 + g, 1), columns],
                gain,
                cosine,
                sine,
            )
            s.t_qkv[pl.ds(512 + 128 * g, 128), columns] = grad.astype(BF16)
            s.gain_k_sum[...] += gain_part
            s.t_qkv[pl.ds(768 + 128 * g, 128), columns] = s.keep_own[columns, pl.ds(128 * g, 128)].T.astype(BF16)

    loop(4, key_back)

    def in_back(b, store):
        def body(i):
            store(i, nn(s.w_qkv[span(i), :], s.t_qkv[:, span(b)]))

        loop(4, body)

    sum_dh1 = Reduce(links, s.sib_out, s.sib_in, s.far_out, s.far_in)
    in_back(across_sib, to(s.sib_out, 0))
    sum_dh1.to_sibling(0)
    in_back(across, to(s.keep_far))
    for half in range(2):
        sum_dh1.make_far(s.keep_far, half)
        sum_dh1.send_far(half)
    gather_dy.drain()

    def qkv_grad(i):
        for j in range(2):
            values = nt(s.h1[span(i), :], s.t_qkv[pl.ds(512 * j, 512), :]).astype(BF16)
            s.attn_mix[i, :, :, pl.ds(512 * j, 512)] = values.reshape(4, 64, 512)

    loop(4, qkv_grad)
    for k in range(5):
        pl.semaphore_wait(ready.at[k], 1)
    dp_mlp.advance()
    dp_attn = DpSum(links, s.attn_mix, ATTN_WIDTHS, s.p, s.sums, 0)
    dp_attn.advance()
    in_back(sib, to(s.sib_out, 1))
    sum_dh1.to_sibling(1)
    in_back(me, to(s.keep_own))
    for row, part in ((0, s.gain_q_sum), (1, s.gain_k_sum)):
        both = part[:, pl.ds(0, 128)] + part[:, pl.ds(128, 128)]
        s.gain_parts[0, 2:3, pl.ds(128 * row, 128)] = jnp.sum(both.T, axis=0, keepdims=True)
    s.gain_parts[0, 2:3, pl.ds(256, 768)] = jnp.zeros((1, 768), F32)
    s.gain_parts[0, pl.ds(3, 5), :] = jnp.zeros((5, 1024), F32)

    sum_mlp.arrive()

    def layer_out(i):
        out[:, span(i)] = sum_mlp.total(s.mlp_own, span(i)).T.astype(BF16)

    loop(4, layer_out)
    dp_attn.advance()

    sum_dh1.arrive()

    def last_back_sum(i, total):
        rows = span(i, 128)
        grad = sum_dh1.total(s.keep_own, rows)
        s.keep_own[rows, :] = grad
        product = grad * (s.x_t[rows, :].astype(F32) * s.root1[0:1])
        s.gain_sum[rows, :] = product[:, :128] + product[:, 128:]
        return total + fold(product * twice(s.gain1[rows, :]))

    inner = lax.fori_loop(0, 8, last_back_sum, jnp.zeros((8, BLOCK), F32))
    inner = jnp.sum(inner, axis=0, keepdims=True) / 1024.0
    s.gain_parts[0, 0:1, :] = jnp.sum(s.gain_sum[...].T, axis=0, keepdims=True)
    gain_copies = [links.send(s.gain_parts.at[0], s.gain_parts.at[7], GAIN_ORDER[0])]

    def last_back(i):
        rows = span(i)
        scaled = s.keep_own[rows, :] * twice(s.gain1[rows, :])
        normed = s.x_t[rows, :].astype(F32) * s.root1[0:1]
        grad_x[:, rows] = (s.resid[rows, :] + s.root1[0:1] * (scaled - normed * inner)).T

    loop(4, last_back)

    for step in range(7):
        if step % 2 == 0 and dp_attn.phase < 5:
            dp_attn.advance()
        gain_copies[step].wait_recv()
        total = s.gain_parts[step] + s.gain_parts[7 + step]
        if step < 6:
            s.gain_parts[step + 1] = total
            following = links.send(s.gain_parts.at[step + 1], s.gain_parts.at[8 + step], GAIN_ORDER[step + 1])
            gain_copies.append(following)
        else:
            out_g1[...] = total[0:1]
            out_g2[...] = total[1:2]
            out_gq[...] = total[2:3, :128]
            out_gk[...] = total[2:3, 128:256]
    out_q[...] = s.sums[:, pl.ds(0, 512)]
    out_k[...] = s.sums[:, pl.ds(512, 256)]
    out_v[...] = s.sums[:, pl.ds(768, 256)]
    out_o[...] = s.sums[:, pl.ds(1024, 512)].T
    out_g[...] = s.sums[:, pl.ds(1536, 768)]
    out_u[...] = s.sums[:, pl.ds(2304, 768)]
    out_d[...] = s.sums[:, pl.ds(3072, 768)].T

    for copy in gain_copies:
        copy.wait_send()
    for exchange in (gather_h1, gather_da, sum_mlp, sum_dh1, dp_mlp, dp_attn):
        exchange.drain()


def shards(
    tokens,
    doc_starts,
    cotangent,
    w_query,
    key_matrix,
    value_matrix,
    w_out,
    w_gate,
    w_up,
    w_down,
    gain_attn,
    gain_mlp,
    gain_query,
    gain_key,
):
    frequency = ROPE_BASE ** (-(np.arange(64, dtype=np.float64) * 2.0) / HEAD)
    frequency = jnp.asarray(np.broadcast_to(frequency[:, None], (64, 128)).astype(np.float32))
    vmem = pl.BlockSpec(memory_space=pltpu.VMEM)
    hbm = pl.BlockSpec(memory_space=pl.ANY)
    smem = pl.BlockSpec(memory_space=pltpu.SMEM)

    def shaped(*shape, kind=F32):
        return jax.ShapeDtypeStruct(shape, kind)

    outs = pl.pallas_call(
        layer_kernel,
        out_shape=(
            shaped(256, 1024, kind=BF16),
            shaped(256, 1024),
            shaped(32, 512),
            shaped(32, 256),
            shaped(32, 256),
            shaped(512, 32),
            shaped(32, 768),
            shaped(32, 768),
            shaped(768, 32),
            shaped(1, 1024),
            shaped(1, 1024),
            shaped(1, 128),
            shaped(1, 128),
        ),
        in_specs=[vmem, smem, vmem] + [hbm] * 7 + [vmem] * 5,
        out_specs=(vmem,) * 13,
        scratch_shapes=[pltpu.VMEM(shape, kind) for _, shape, kind in SCRATCH]
        + [
            pltpu.SemaphoreType.DMA((2, SEMAPHORES)),
            pltpu.SemaphoreType.DMA((8,)),
            pltpu.SemaphoreType.REGULAR((5,)),
        ],
        compiler_params=pltpu.CompilerParams(
            collective_id=0, has_side_effects=True, vmem_limit_bytes=64 * 2**20 - 2**16
        ),
        cost_estimate=pl.CostEstimate(flops=32 * 10**9, bytes_accessed=2**24, transcendentals=2**22),
        name="layer",
    )(
        tokens.reshape(256, 1024),
        doc_starts,
        cotangent.reshape(256, 1024),
        w_query,
        key_matrix,
        value_matrix,
        w_out,
        w_gate.reshape(4, 4, 64, 768),
        w_up.reshape(4, 4, 64, 768),
        w_down,
        gain_attn.reshape(1, 1024),
        gain_mlp.reshape(1, 1024),
        gain_query.reshape(1, 128),
        gain_key.reshape(1, 128),
        frequency,
    )
    return (
        outs[0].reshape(1, 256, 1024),
        outs[1].reshape(1, 256, 1024),
        *outs[2:9],
        *(gain.reshape(-1) for gain in outs[9:]),
    )


def solution(mesh):
    in_specs = (
        P("dp", "tensor", None),
        P("dp", None),
        P("dp", "tensor", None),
        P(None, "tensor"),
        P(None, "tensor"),
        P(None, "tensor"),
        P("tensor", None),
        P(None, "tensor"),
        P(None, "tensor"),
        P("tensor", None),
        P(),
        P(),
        P(),
        P(),
    )
    out_specs = (
        P("dp", "tensor", None),
        P("dp", "tensor", None),
        P("dp", "tensor"),
        P("dp", "tensor"),
        P("dp", "tensor"),
        P("tensor", "dp"),
        P("dp", "tensor"),
        P("dp", "tensor"),
        P("tensor", "dp"),
        P(),
        P(),
        P(),
        P(),
    )
    return jax.shard_map(shards, mesh=mesh, in_specs=in_specs, out_specs=out_specs, check_vma=False)
```

```python
import math

import jax
import jax.numpy as jnp
import numpy as np
from jax import lax
from jax.experimental import pallas as pl
from jax.experimental.pallas import tpu as pltpu
from jax.sharding import PartitionSpec as P

MESH = pl.DeviceIdType.MESH
BF16 = jnp.bfloat16
F32 = jnp.float32
EPSILON = 1e-06
ROPE_BASE = 1000000.0
BLOCK = 256
HEAD = 128
QUERY_SCALE = math.log2(math.e) / math.sqrt(HEAD)
PARTNERS = ("core", "far", "y1", "y2", "z1", "z2", "x")
ORDERS = (("y1", "y2", "z1", "z2"), ("y2", "y1", "z2", "z1"), ("z1", "z2", "y1", "y2"), ("z2", "z1", "y2", "y1"))
MLP_STREAMS = ((640, 0, 0), (640, 4, 0), (512, 8, 0), (512, 12, 0))
HIGH_STREAMS = ((256, 10, 0), (256, 10, 256), (256, 14, 0), (256, 14, 256))
LOW_STREAMS = ((128, 0, 0), (128, 0, 128), (128, 0, 256), (128, 0, 384))
GAIN_ORDER = ("core", "y1", "y2", "z1", "z2", "x", "far")

SCRATCH = (
    ("w_qkv", (1024, 1024), BF16),
    ("t_qkv", (1024, 1024), BF16),
    ("w_down", (768, 1024), BF16),
    ("t_gu", (1536, 1024), BF16),
    ("mlp_mix", (4, 4, 64, 2304), BF16),
    ("attn_mix", (4, 4, 64, 1536), BF16),
    ("h1", (1024, 1024), BF16),
    ("h2", (1024, 1024), BF16),
    ("da", (1024, 1024), BF16),
    ("norm_qk", (768, 1024), BF16),
    ("root_qk", (8, 1024), F32),
    ("ob", (512, 1024), BF16),
    ("qs", (2, 4, 128, 512), BF16),
    ("ks_t", (256, 1024), BF16),
    ("ks", (2, 1024, 128), BF16),
    ("v_t", (2, 144, 1024), BF16),
    ("v", (2, 1024, 128), BF16),
    ("p", (20, 4, 64, 512), BF16),
    ("inv", (2, 4, 8, 512), F32),
    ("inner", (2, 4, 8, 512), F32),
    ("mask", (10, 256, 256), BF16),
    ("hidden", (768, 1024), BF16),
    ("dgu", (1536, 1024), BF16),
    ("cosine", (64, 1024), F32),
    ("sine", (64, 1024), F32),
    ("x_t", (1024, 256), BF16),
    ("resid", (1024, 256), F32),
    ("gain1", (1024, 128), F32),
    ("gain2", (1024, 128), F32),
    ("gain_q", (128, 128), F32),
    ("gain_k", (128, 128), F32),
    ("gain_sum", (1024, 128), F32),
    ("gain_q_sum", (128, 256), F32),
    ("gain_k_sum", (128, 256), F32),
    ("root1", (8, 256), F32),
    ("root2", (8, 256), F32),
    ("acc_o", (3, 2, 144, 512), F32),
    ("acc_q", (128, 512), F32),
    ("keep_far", (1024, 256), F32),
    ("keep_own", (1024, 256), F32),
    ("sib_out", (2, 1024, 256), BF16),
    ("sib_in", (2, 1024, 256), BF16),
    ("far_out", (1024, 256), BF16),
    ("far_in", (1024, 256), BF16),
    ("mlp_own", (1024, 256), F32),
    ("mlp_sib_out", (2, 1024, 256), BF16),
    ("mlp_sib_in", (2, 1024, 256), BF16),
    ("mlp_far_out", (1024, 256), BF16),
    ("mlp_far_in", (1024, 256), BF16),
    ("mlp_halves", (16, 4, 64, 640), BF16),
    ("sums", (32, 3840), F32),
    ("result", (256, 1024), F32),
    ("stage", (256, 1024), BF16),
    ("gain_parts", (14, 8, 1024), F32),
)
SEMAPHORES = 140


class Box:
    pass


class Place:
    def __init__(self):
        dp = lax.axis_index("dp")
        tensor = lax.axis_index("tensor")
        self.z, self.y, self.x = dp // 8, (dp // 2) % 4, dp % 2
        self.far, self.core = tensor // 2, tensor % 2
        self.me = tensor
        self.sib = self.far * 2 + 1 - self.core
        self.across = (1 - self.far) * 2 + self.core
        self.across_sib = (1 - self.far) * 2 + 1 - self.core

    def near(self, name):
        return step_of(name, self.y if name[0] == "y" else self.z)

    def device(self, name):
        z, y, x, far, core = self.z, self.y, self.x, self.far, self.core
        if name[0] == "y":
            y = self.near(name)
        elif name[0] == "z":
            z = self.near(name)
        elif name == "x":
            x = 1 - x
        elif name == "far":
            far = 1 - far
        else:
            core = 1 - core
        return ((z * 4 + y) * 2 + x, far * 2 + core)


def step_of(name, value):
    return value + 1 - 2 * (value % 2) if name[1] == "1" else 3 - value


def nn(left, right):
    return lax.dot_general(left, right, (((1,), (0,)), ((), ())), preferred_element_type=F32)


def nt(left, right):
    return lax.dot_general(left, right, (((1,), (1,)), ((), ())), preferred_element_type=F32)


def span(index, size=BLOCK):
    return pl.ds(pl.multiple_of(index * size, size), size)


def loop(count, body):
    def step(index, carry):
        body(index)
        return carry

    lax.fori_loop(0, count, step, 0)


def twice(values):
    return jnp.concatenate([values, values], axis=1)


def fold(values):
    return jnp.sum(values.reshape(values.shape[0] // 8, 8, values.shape[1]), axis=0)


class Links:
    def __init__(self, place, sems):
        self.place, self.sems, self.used, self.sent = place, sems, 0, []

    def send(self, src, dst, name):
        copy = pltpu.make_async_remote_copy(
            src_ref=src,
            dst_ref=dst,
            send_sem=self.sems.at[0, self.used],
            recv_sem=self.sems.at[1, self.used],
            device_id=self.place.device(name),
            device_id_type=MESH,
        )
        self.used += 1
        copy.start()
        return copy


class Gather:
    def __init__(self, links, at):
        self.links, self.at = links, at
        self.far, self.sib, self.passed = [], [], []

    def send(self, half):
        block = self.at(half, self.links.place.me)
        self.far.append(self.links.send(block, block, "far"))
        self.sib.append(self.links.send(block, block, "core"))

    def pass_on(self):
        for half, copy in enumerate(self.far):
            copy.wait_recv()
            block = self.at(half, self.links.place.across)
            self.passed.append(self.links.send(block, block, "core"))

    def near_ready(self):
        for copy in self.sib:
            copy.wait_recv()

    def far_ready(self):
        for copy in self.passed:
            copy.wait_recv()

    def drain(self):
        for copy in self.far + self.sib + self.passed:
            copy.wait_send()


class Reduce:
    def __init__(self, links, sib_out, sib_in, far_out, far_in):
        self.links = links
        self.sib_out, self.sib_in, self.far_out, self.far_in = sib_out, sib_in, far_out, far_in
        self.copies = [None, None]
        self.far = []

    def to_sibling(self, index):
        self.copies[index] = self.links.send(self.sib_out.at[index], self.sib_in.at[index], "core")

    def make_far(self, keep, half):
        if half == 0:
            self.copies[0].wait_recv()

        def body(i):
            rows = span(i + 4 * half, 128)
            self.far_out[rows, :] = (keep[rows, :] + self.sib_in[0, rows, :].astype(F32)).astype(BF16)

        loop(4, body)

    def send_far(self, half):
        rows = pl.ds(512 * half, 512)
        self.far.append(self.links.send(self.far_out.at[rows], self.far_in.at[rows], "far"))

    def arrive(self):
        self.copies[1].wait_recv()
        for copy in self.far:
            copy.wait_recv()

    def total(self, keep, rows):
        return keep[rows, :] + self.sib_in[1, rows, :].astype(F32) + self.far_in[rows, :].astype(F32)

    def drain(self):
        for copy in self.copies + self.far:
            copy.wait_send()


class DpSum:
    def __init__(self, links, source, source_first, streams, bufs, out, out_first):
        self.links, self.source, self.bufs, self.out = links, source, bufs, out
        self.streams = streams
        before = [sum(w for w, _, _ in streams[:k]) for k in range(4)]
        self.source_first = [source_first + first for first in before]
        self.out_first = [out_first + first for first in before]
        self.phase = -1
        self.flying = [[], [], [], []]
        self.sent = []

    def spot(self, stream, slot, *rest):
        w, at, column = self.streams[stream]
        lead = pl.ds(at + slot.start, slot.size) if isinstance(slot, pl.Slice) else at + slot
        return (lead, *rest, pl.ds(column, w))

    def held(self, stream, phase):
        every = slice(None)
        if phase == 0:
            spot = self.spot(stream, pl.ds(0, 2), every, every)
        elif phase == 1:
            spot = self.spot(stream, 2, every, every)
        elif phase == 2:
            spot = self.spot(stream, 3, pl.ds(0, 2), every)
        elif phase == 3:
            spot = self.spot(stream, 3, 2, every)
        else:
            spot = self.spot(stream, 3, 3, pl.ds(0, 32))
        return self.bufs.at[spot]

    def begin(self, stream, phase):
        place, send = self.links.place, self.links.send
        order = ORDERS[stream]
        into = self.held(stream, phase)
        if phase == 4:
            theirs = self.bufs.at[self.spot(stream, 3, 2, span(1 - place.x, 32))]
            return [send(theirs, into, "x")]
        name = order[phase]
        if phase in (1, 3):
            return [send(self.held(stream, phase - 1).at[1], into, name)]
        there = place.near(name)
        copies = []
        for j, at in enumerate((there, step_of(order[phase + 1], there))):
            if phase == 2:
                source = self.held(stream, 1).at[at]
            else:
                columns = pl.ds(self.source_first[stream], self.streams[stream][0])
                source = self.source.at[:, at, :, columns] if name[0] == "y" else self.source.at[at, :, :, columns]
            copies.append(send(source, into.at[j], name))
        return copies

    def finish(self, stream, phase):
        place, spot, bufs = self.links.place, self.spot, self.bufs
        order, w = ORDERS[stream], self.streams[stream][0]
        every = slice(None)
        for copy in self.flying[stream]:
            copy.wait_recv()
        if phase == 4:
            mine = bufs[spot(stream, 3, 2, span(place.x, 32))].astype(F32)
            columns = pl.ds(self.out_first[stream], w)
            self.out[:, columns] = bufs[spot(stream, 3, 3, pl.ds(0, 32))].astype(F32) + mine
        elif phase == 3:
            bufs[spot(stream, 3, 2, every)] += bufs[spot(stream, 3, 0, every)]
        elif phase == 1:
            for k in range(4):
                bufs[spot(stream, 2, k, every)] += bufs[spot(stream, 0, k, every)]
        else:
            name = order[phase]
            mine = place.y if name[0] == "y" else place.z
            for j, own in enumerate((mine, step_of(order[phase + 1], mine))):
                if phase == 2:
                    bufs[spot(stream, 3, j, every)] += bufs[spot(stream, 2, own, every)]
                    continue
                for k in range(4):
                    lead = (k, own) if name[0] == "y" else (own, k)
                    kept = self.source[(*lead, every, pl.ds(self.source_first[stream], w))]
                    bufs[spot(stream, j, k, every)] += kept

    def advance(self):
        if self.phase == 5:
            return
        for stream in range(4):
            if self.phase >= 0:
                self.finish(stream, self.phase)
                self.sent += self.flying[stream]
            if self.phase < 4:
                self.flying[stream] = self.begin(stream, self.phase + 1)
        self.phase += 1

    def complete(self):
        while self.phase < 5:
            self.advance()

    def drain(self):
        for copy in self.sent:
            copy.wait_send()


class GainSum:
    def __init__(self, links, parts):
        self.links, self.parts, self.copies, self.step = links, parts, [], 0
        self.begin()

    def begin(self):
        step = self.step
        self.copies.append(self.links.send(self.parts.at[step], self.parts.at[7 + step], GAIN_ORDER[step]))

    def advance(self):
        if self.step == 7:
            return
        step = self.step
        self.copies[step].wait_recv()
        total = self.parts[step] + self.parts[7 + step]
        self.step += 1
        if self.step < 7:
            self.parts[self.step] = total
            self.begin()
        else:
            self.total = total

    def complete(self):
        while self.step < 7:
            self.advance()

    def drain(self):
        for copy in self.copies:
            copy.wait_send()


def head_forward(raw, gain, cosine, sine):
    root = lax.rsqrt(jnp.mean(raw * raw, axis=0, keepdims=True) + EPSILON)
    normed = raw * root
    scaled = normed * gain
    first, second = scaled[:64], scaled[64:]
    turned = jnp.concatenate([first * cosine - second * sine, second * cosine + first * sine], axis=0)
    return normed, root, turned


def head_backward(grad, normed, root, gain, cosine, sine):
    first, second = grad[:64], grad[64:]
    turned = jnp.concatenate([first * cosine + second * sine, second * cosine - first * sine], axis=0)
    scaled = turned * gain
    inner = jnp.mean(scaled * normed, axis=0, keepdims=True)
    return root * (scaled - normed * inner), turned * normed


def layer_kernel(
    x, starts, dy, wq, wk, wv, wo, wg, wu, wd, g1, g2, gq, gk, frequency,
    out, grad_x, out_sums, out_g1, out_g2, out_gq, out_gk,
    *scratch,
):
    s = Box()
    for (name, _, _), ref in zip(SCRATCH, scratch):
        setattr(s, name, ref)
    link_sems, load_sems, ready = scratch[len(SCRATCH) :]
    place = Place()
    links = Links(place, link_sems)
    me, sib, across, across_sib = place.me, place.sib, place.across, place.across_sib

    barrier = pltpu.get_barrier_semaphore()
    for name in PARTNERS:
        pl.semaphore_signal(barrier, inc=1, device_id=place.device(name), device_id_type=MESH)

    loads = []

    def load(src, dst):
        copy = pltpu.make_async_copy(src, dst, load_sems.at[len(loads)])
        copy.start()
        loads.append(copy)

    for g in range(2):
        load(wq.at[:, pl.ds(256 * g, 256)], s.w_qkv.at[:, pl.ds(512 * g, 256)])
        load(wk.at[:, pl.ds(128 * g, 128)], s.w_qkv.at[:, pl.ds(512 * g + 256, 128)])
        load(wv.at[:, pl.ds(128 * g, 128)], s.w_qkv.at[:, pl.ds(512 * g + 384, 128)])
    load(wo, s.h2.at[pl.ds(0, 512)])
    load(wg, s.mlp_mix.at[:, :, :, pl.ds(0, 768)])
    load(wu, s.mlp_mix.at[:, :, :, pl.ds(768, 768)])
    load(wd, s.w_down)
    load(dy, s.da.at[pl.ds(0, 256)])

    def first_norm(i):
        rows = span(i, 64)
        xs = x[rows, :].astype(F32)
        root = lax.rsqrt(jnp.mean(xs * xs, axis=1, keepdims=True) + EPSILON)
        s.stage[rows, :] = (xs * root * g1[...]).astype(BF16)

    loop(4, first_norm)
    gather_h1 = Gather(links, lambda half, b: s.h1.at[pl.ds(512 * half, 512), span(b)])
    for half in range(2):
        for j in range(2):
            s.h1[pl.ds(512 * half + 256 * j, 256), span(me)] = s.stage[:, pl.ds(512 * half + 256 * j, 256)].T
        if half == 0:
            pl.semaphore_wait(barrier, len(PARTNERS))
        gather_h1.send(half)

    def dy_in(i):
        s.attn_mix[i, :, :, span(me)] = s.da[pl.ds(0, 256), span(i)].T.reshape(4, 64, BLOCK)

    loads[10].wait()
    loop(4, dy_in)
    for k in range(6):
        loads[k].wait()

    def turn_qkv(i):
        s.t_qkv[span(i), :] = s.w_qkv[:, span(i)].T

    loop(4, turn_qkv)

    place_row = lax.broadcasted_iota(jnp.int32, (8, 1024), 1)
    start_row = jnp.zeros((8, 1024), jnp.int32)
    for d in range(4):
        start_row = jnp.maximum(start_row, jnp.where(place_row >= starts[0, d], starts[0, d], 0))
    position = (place_row - start_row).astype(F32)
    for i in range(8):
        lanes = pl.ds(128 * i, 128)
        angle = frequency[...] * position[0:1, 128 * i : 128 * i + 128]
        s.cosine[:, lanes] = jnp.cos(angle)
        s.sine[:, lanes] = jnp.sin(angle)
    for qb in range(4):
        first = start_row[0:1, qb * 256 : qb * 256 + 256]
        query = lax.broadcasted_iota(jnp.int32, (256, 256), 1) + qb * 256
        for kb in range(qb + 1):
            key = lax.broadcasted_iota(jnp.int32, (256, 256), 0) + kb * 256
            allowed = (key <= query) & (key >= first)
            s.mask[qb * (qb + 1) // 2 + kb] = jnp.where(allowed, 1.0, 0.0).astype(BF16)

    s.gain1[...] = jnp.broadcast_to(g1[...], (128, 1024)).T
    s.gain2[...] = jnp.broadcast_to(g2[...], (128, 1024)).T
    s.gain_q[...] = jnp.broadcast_to(gq[...], (128, 128)).T
    s.gain_k[...] = jnp.broadcast_to(gk[...], (128, 128)).T
    s.gain_q_sum[...] = jnp.zeros((128, 256), F32)
    s.gain_k_sum[...] = jnp.zeros((128, 256), F32)
    for g in range(2):
        s.v_t[g, pl.ds(128, 16), :] = jnp.ones((16, 1024), BF16)

    def x_in(i, total):
        turned = x[:, span(i)].astype(F32).T
        s.x_t[span(i), :] = turned.astype(BF16)
        return total + fold(turned * turned)

    square = lax.fori_loop(0, 4, x_in, jnp.zeros((8, BLOCK), F32))
    root = lax.rsqrt(jnp.sum(square, axis=0, keepdims=True) / 1024.0 + EPSILON)
    s.root1[...] = jnp.broadcast_to(root, (8, BLOCK))

    loads[6].wait()

    def turn_out(i):
        s.attn_mix[i, :, :, pl.ds(1024, 512)] = s.h2[pl.ds(0, 512), span(i)].T.reshape(4, 64, 512)

    loop(4, turn_out)
    loads[7].wait()
    loads[8].wait()

    def turn_gu(i):
        for z in range(4):
            s.t_gu[span(i), pl.ds(256 * z, 256)] = s.mlp_mix[z, :, :, span(i)].reshape(256, 256).T

    loop(6, turn_gu)
    loads[9].wait()

    def turn_down(i):
        s.mlp_mix[i, :, :, pl.ds(1536, 768)] = s.w_down[:, span(i)].T.reshape(4, 64, 768)

    loop(4, turn_down)

    def project(b):
        columns = span(b)
        cosine, sine = s.cosine[:, columns], s.sine[:, columns]
        query_gain = twice(s.gain_q[...] * QUERY_SCALE)
        key_gain = twice(s.gain_k[...])
        for g in range(2):
            raw = nn(s.t_qkv[pl.ds(512 * g, 256), :], s.h1[:, columns])
            for k in range(2):
                head = 3 * g + k
                normed, root, turned = head_forward(raw[128 * k : 128 * k + 128], query_gain, cosine, sine)
                s.norm_qk[pl.ds(128 * head, 128), columns] = normed.astype(BF16)
                s.root_qk[pl.ds(head, 1), columns] = root
                s.qs[g, b, :, pl.ds(256 * k, 256)] = turned.astype(BF16)
            raw = nn(s.t_qkv[pl.ds(512 * g + 256, 256), :], s.h1[:, columns])
            normed, root, turned = head_forward(raw[:128], key_gain, cosine, sine)
            s.norm_qk[pl.ds(384 * g + 256, 128), columns] = normed.astype(BF16)
            s.root_qk[pl.ds(3 * g + 2, 1), columns] = root
            s.ks_t[pl.ds(128 * g, 128), columns] = turned.astype(BF16)
            s.ks[g, columns, :] = turned.astype(BF16).T
            values = raw[128:].astype(BF16)
            s.v_t[g, pl.ds(0, 128), columns] = values
            s.v[g, columns, :] = values.T

    def attend_to(qb, slot, first, last):
        def group(g):
            def keys(kb):
                at = qb * (qb + 1) // 2 + kb
                scores = nn(s.ks[g, span(kb), :], s.qs[g, qb])
                weights = jnp.exp2(scores).astype(BF16) * twice(s.mask[at])
                s.p[g * 10 + at] = weights.reshape(4, 64, 512)
                s.acc_o[slot, g] += nn(s.v_t[g, :, span(kb)], weights)

            lax.fori_loop(first, last, lambda kb, carry: (keys(kb), carry)[1], 0)

        loop(2, group)

    def attend_end(qb, slot):
        def group(g):
            inverse = 1.0 / s.acc_o[slot, g, pl.ds(128, 8), :]
            s.inv[g, qb] = inverse
            attended = (s.acc_o[slot, g, pl.ds(0, 128), :] * inverse[0:1]).astype(BF16)
            rows = pl.multiple_of(g * 256, 256)
            s.ob[pl.ds(rows, 128), span(qb)] = attended[:, :256]
            s.ob[pl.ds(rows + 128, 128), span(qb)] = attended[:, 256:]

        loop(2, group)

    s.acc_o[pl.ds(0, 2)] = jnp.zeros((2, 2, 144, 512), F32)
    gather_h1.near_ready()
    loop(2, lambda i: project(place.far * 2 + i))
    loop(2, lambda i: attend_to(place.far * 2 + i, i, place.far * 2, place.far * 2 + i + 1))
    gather_h1.pass_on()
    gather_dy = Gather(links, lambda half, b: s.attn_mix.at[pl.ds(2 * half, 2), :, :, span(b)])
    gather_dy.send(0)
    gather_dy.send(1)
    gather_h1.far_ready()
    loop(2, lambda i: project((1 - place.far) * 2 + i))

    def out_product(b, store, first=0, last=4):
        def body(i):
            store(i, nn(s.attn_mix[i, :, :, pl.ds(1024, 512)].reshape(256, 512), s.ob[:, span(b)]))

        lax.fori_loop(first, last, lambda i, carry: (body(i), carry)[1], 0)

    def to(ref, index=None):
        def store(i, values):
            if index is None:
                ref[span(i), :] = values.astype(ref.dtype)
            else:
                ref[index, span(i), :] = values.astype(ref.dtype)

        return store

    sum_attn = Reduce(links, s.sib_out, s.sib_in, s.far_out, s.far_in)

    def attend_far(qb):
        s.acc_o[2] = jnp.zeros((2, 144, 512), F32)
        attend_to(qb, 2, 0, qb + 1)
        attend_end(qb, 2)

    attend_far(across_sib)
    out_product(across_sib, to(s.sib_out, 0))
    sum_attn.to_sibling(0)
    attend_far(across)
    for half in range(2):
        out_product(across, to(s.keep_far), 2 * half, 2 * half + 2)
        sum_attn.make_far(s.keep_far, half)
        sum_attn.send_far(half)

    def attend_own(i):
        attend_to(place.far * 2 + i, i, 0, place.far * 2)
        attend_end(place.far * 2 + i, i)

    loop(2, attend_own)
    out_product(sib, to(s.sib_out, 1))
    sum_attn.to_sibling(1)
    out_product(me, to(s.keep_own))
    gather_dy.near_ready()
    gather_dy.pass_on()
    sum_attn.arrive()

    def second_norm(i, total):
        rows = span(i, 128)
        x1 = s.x_t[rows, :].astype(F32) + sum_attn.total(s.keep_own, rows)
        s.resid[rows, :] = x1
        return total + fold(x1 * x1)

    square = lax.fori_loop(0, 8, second_norm, jnp.zeros((8, BLOCK), F32))
    root2 = lax.rsqrt(jnp.sum(square, axis=0, keepdims=True) / 1024.0 + EPSILON)
    s.root2[...] = jnp.broadcast_to(root2, (8, BLOCK))
    gather_h2 = Gather(links, lambda half, b: s.h2.at[pl.ds(512 * half, 512), span(b)])
    for half in range(2):

        def scale_rows(i, half=half):
            rows = span(i + 4 * half, 128)
            s.h2[rows, span(me)] = (s.resid[rows, :] * s.root2[0:1] * twice(s.gain2[rows, :])).astype(BF16)

        loop(4, scale_rows)
        gather_h2.send(half)
    sum_attn.drain()
    gather_dy.far_ready()

    def dy_rows(i):
        return s.attn_mix[i, :, :, pl.ds(0, 1024)].reshape(256, 1024)

    def feed(b):
        columns = span(b)

        def body(j):
            normed = s.h2[:, columns]
            gate = nn(s.t_gu[span(j), :], normed)
            up = nn(s.t_gu[pl.ds(pl.multiple_of(768 + 256 * j, 256), 256), :], normed)
            grad = nn(s.w_down[span(j), :], s.attn_mix[:, :, :, columns].reshape(1024, 256))
            open_gate = jax.nn.sigmoid(gate)
            silu = gate * open_gate
            s.hidden[span(j), columns] = (silu * up).astype(BF16)
            s.dgu[span(j), columns] = (grad * up * open_gate * (1.0 + gate * (1.0 - open_gate))).astype(BF16)
            s.dgu[pl.ds(pl.multiple_of(768 + 256 * j, 256), 256), columns] = (grad * silu).astype(BF16)

        loop(3, body)

    def feed_back(b, store, first=0, last=4):
        def body(i):
            store(i, nn(s.mlp_mix[i, :, :, pl.ds(0, 1536)].reshape(256, 1536), s.dgu[:, span(b)]))

        lax.fori_loop(first, last, lambda i, carry: (body(i), carry)[1], 0)

    def mlp_product(b, store):
        def body(i):
            store(i, nn(s.mlp_mix[i, :, :, pl.ds(1536, 768)].reshape(256, 768), s.hidden[:, span(b)]))

        loop(4, body)

    sum_dh2 = Reduce(links, s.sib_out, s.sib_in, s.far_out, s.far_in)
    gather_h2.near_ready()
    feed(sib)
    feed_back(sib, to(s.sib_out, 1))
    sum_dh2.to_sibling(1)
    feed(me)
    feed_back(me, to(s.keep_own))
    gather_h2.pass_on()
    gather_h2.far_ready()
    feed(across_sib)
    feed_back(across_sib, to(s.sib_out, 0))
    sum_dh2.to_sibling(0)
    feed(across)
    for half in range(2):
        feed_back(across, to(s.keep_far), 2 * half, 2 * half + 2)
        sum_dh2.make_far(s.keep_far, half)
        sum_dh2.send_far(half)

    sum_mlp = Reduce(links, s.mlp_sib_out, s.mlp_sib_in, s.mlp_far_out, s.mlp_far_in)
    mlp_product(across_sib, to(s.mlp_sib_out, 0))
    sum_mlp.to_sibling(0)
    mlp_product(sib, to(s.mlp_sib_out, 1))
    sum_mlp.to_sibling(1)
    mlp_product(across, to(s.keep_far))

    def mlp_mine(i, values):
        s.mlp_own[span(i), :] = s.resid[span(i), :] + values

    mlp_product(me, mlp_mine)
    for half in range(2):
        sum_mlp.make_far(s.keep_far, half)

    def down_grad(i):
        s.mlp_mix[i, :, :, pl.ds(1536, 768)] = nt(dy_rows(i), s.hidden[...]).astype(BF16).reshape(4, 64, 768)

    loop(4, down_grad)

    def gate_up_grad(i):
        for j in range(3):
            values = nt(s.h2[span(i), :], s.dgu[pl.ds(512 * j, 512), :]).astype(BF16)
            s.mlp_mix[i, :, :, pl.ds(512 * j, 512)] = values.reshape(4, 64, 512)

    loop(4, gate_up_grad)
    gather_h2.drain()
    load(wo, s.h2.at[pl.ds(0, 512)])
    dp_mlp = DpSum(links, s.mlp_mix, 0, MLP_STREAMS, s.mlp_halves, s.sums, 1536)
    dp_mlp.advance()

    sum_dh2.arrive()

    def norm_back_sum(i, total):
        rows = span(i, 128)
        grad = sum_dh2.total(s.keep_own, rows)
        s.keep_own[rows, :] = grad
        product = grad * (s.resid[rows, :] * s.root2[0:1])
        s.gain_sum[rows, :] = product[:, :128] + product[:, 128:]
        return total + fold(product * twice(s.gain2[rows, :]))

    inner = lax.fori_loop(0, 8, norm_back_sum, jnp.zeros((8, BLOCK), F32))
    inner = jnp.sum(inner, axis=0, keepdims=True) / 1024.0
    gather_da = Gather(links, lambda half, b: s.da.at[pl.ds(512 * half, 512), span(b)])
    for half in range(2):

        def norm_back(i, half=half):
            rows = span(i + 4 * half, 128)
            scaled = s.keep_own[rows, :] * twice(s.gain2[rows, :])
            normed = s.resid[rows, :] * s.root2[0:1]
            own = s.attn_mix[2 * half + i // 2, pl.ds(2 * (i % 2), 2), :, span(me)].reshape(128, BLOCK).astype(F32)
            dx1 = own + s.root2[0:1] * (scaled - normed * inner)
            s.resid[rows, :] = dx1
            s.da[rows, span(me)] = dx1.astype(BF16)

        loop(4, norm_back)
        gather_da.send(half)
    sum_dh2.drain()
    s.gain_parts[0, 1:2, :] = jnp.sum(s.gain_sum[...].T, axis=0, keepdims=True)
    s.gain_sum[...] = jnp.zeros((1024, 128), F32)

    s.keep_own[...] = jnp.zeros((1024, 256), F32)
    s.keep_far[...] = jnp.zeros((1024, 256), F32)
    loads[11].wait()

    def out_back(b):
        def body(g):
            grads = nn(s.h2[span(g), :], s.da[:, span(b)])
            both = jnp.concatenate([grads[:128], grads[128:]], axis=1) * s.inv[g, b][0:1]
            rows = pl.multiple_of(g * 256, 256)
            outs = jnp.concatenate([s.ob[pl.ds(rows, 128), span(b)], s.ob[pl.ds(rows + 128, 128), span(b)]], axis=1)
            s.inner[g, b] = jnp.broadcast_to(jnp.sum(both * outs.astype(F32), axis=0, keepdims=True), (8, 512))
            s.t_gu[span(g * 4 + b, 128), pl.ds(0, 512)] = both.astype(BF16)

        loop(2, body)

    def attend_back(qb, g):
        columns = span(qb)
        cosine, sine = s.cosine[:, columns], s.sine[:, columns]
        gain = twice(s.gain_q[...])
        s.acc_q[...] = jnp.zeros((128, 512), F32)

        def keys(kb):
            at = g * 10 + qb * (qb + 1) // 2 + kb
            rows = span(kb)
            grads = s.t_gu[span(g * 4 + qb, 128), pl.ds(0, 512)]
            weights = s.p[at].reshape(256, 512)
            slope = nn(s.v[g, rows, :], grads) - s.inner[g, qb][0:1]
            ds = (weights.astype(F32) * slope).astype(BF16)
            s.keep_own[rows, pl.ds(128 * g, 128)] += nt(weights, grads)
            s.keep_far[rows, pl.ds(128 * g, 128)] += nt(ds, s.qs[g, qb])
            s.acc_q[...] += nn(s.ks_t[pl.ds(128 * g, 128), rows], ds)

        loop(qb + 1, keys)
        for k in range(2):
            head = 3 * g + k
            grad, gain_part = head_backward(
                s.acc_q[:, pl.ds(256 * k, 256)] * (1.0 / math.sqrt(HEAD)),
                s.norm_qk[pl.ds(128 * head, 128), columns].astype(F32),
                s.root_qk[pl.ds(head, 1), columns],
                gain,
                cosine,
                sine,
            )
            s.t_qkv[pl.ds(512 * g + 128 * k, 128), columns] = grad.astype(BF16)
            s.gain_q_sum[...] += gain_part

    def key_back(g):
        gain = twice(s.gain_k[...])

        def body(b):
            columns = span(b)
            grad, gain_part = head_backward(
                s.keep_far[columns, pl.ds(128 * g, 128)].T * math.log(2.0),
                s.norm_qk[pl.ds(384 * g + 256, 128), columns].astype(F32),
                s.root_qk[pl.ds(3 * g + 2, 1), columns],
                gain,
                s.cosine[:, columns],
                s.sine[:, columns],
            )
            s.t_qkv[pl.ds(512 * g + 256, 128), columns] = grad.astype(BF16)
            s.gain_k_sum[...] += gain_part
            s.t_qkv[pl.ds(512 * g + 384, 128), columns] = s.keep_own[columns, pl.ds(128 * g, 128)].T.astype(BF16)

        loop(4, body)

    def tell_ready(g):
        for k, name in enumerate(PARTNERS[2:]):
            pl.semaphore_signal(ready.at[g, k], inc=1, device_id=place.device(name), device_id_type=MESH)

    def wait_ready(g):
        for k in range(5):
            pl.semaphore_wait(ready.at[g, k], 1)

    def qkv_grad(g):
        def body(i):
            values = nt(s.h1[span(i), :], s.t_qkv[pl.ds(512 * g, 512), :]).astype(BF16)
            s.attn_mix[i, :, :, pl.ds(512 * g, 512)] = values.reshape(4, 64, 512)

        loop(4, body)

    def out_grad(i):
        s.attn_mix[i, :, :, pl.ds(1024, 512)] = nt(s.da[span(i), :], s.ob[...]).astype(BF16).reshape(4, 64, 512)

    gather_da.near_ready()
    loop(2, lambda i: out_back(place.far * 2 + i))
    for g in range(2):
        loop(2, lambda i, g=g: attend_back(place.far * 2 + i, g))
    gather_da.pass_on()
    for half in range(2):
        sum_mlp.send_far(half)
    dp_mlp.advance()
    gather_da.far_ready()
    loop(2, lambda i: out_back((1 - place.far) * 2 + i))
    gather_dy.drain()

    loop(2, lambda i: attend_back((1 - place.far) * 2 + i, 1))
    dp_mlp.advance()
    key_back(1)
    tell_ready(1)
    loop(4, out_grad)
    qkv_grad(1)
    wait_ready(1)
    dp_high = DpSum(links, s.attn_mix, 512, HIGH_STREAMS, s.p, s.sums, 512)
    dp_high.advance()
    loop(2, lambda i: attend_back((1 - place.far) * 2 + i, 0))
    dp_mlp.advance()
    key_back(0)
    tell_ready(0)

    def in_back(b, store, first=0, last=4):
        columns = span(b)

        def body(i):
            values = nn(s.w_qkv[span(i), :], s.t_qkv[:, columns])
            product = values * s.h1[span(i), columns].astype(F32)
            s.gain_sum[span(i), :] += product[:, :128] + product[:, 128:]
            store(i, values)

        lax.fori_loop(first, last, lambda i, carry: (body(i), carry)[1], 0)

    sum_dh1 = Reduce(links, s.sib_out, s.sib_in, s.far_out, s.far_in)
    in_back(across_sib, to(s.sib_out, 0))
    sum_dh1.to_sibling(0)
    for half in range(2):
        in_back(across, to(s.keep_far), 2 * half, 2 * half + 2)
        sum_dh1.make_far(s.keep_far, half)
        sum_dh1.send_far(half)
    qkv_grad(0)
    wait_ready(0)
    dp_low = DpSum(links, s.attn_mix, 0, LOW_STREAMS, s.p, s.sums, 0)
    dp_low.advance()
    dp_high.advance()
    in_back(sib, to(s.sib_out, 1))
    sum_dh1.to_sibling(1)
    in_back(me, to(s.keep_own))
    s.gain_parts[0, 0:1, :] = jnp.sum((s.gain_sum[...] / s.gain1[...]).T, axis=0, keepdims=True)
    for row, part in ((0, s.gain_q_sum), (1, s.gain_k_sum)):
        both = part[:, pl.ds(0, 128)] + part[:, pl.ds(128, 128)]
        s.gain_parts[0, 2:3, pl.ds(128 * row, 128)] = jnp.sum(both.T, axis=0, keepdims=True)
    s.gain_parts[0, 2:3, pl.ds(256, 768)] = jnp.zeros((1, 768), F32)
    s.gain_parts[0, pl.ds(3, 5), :] = jnp.zeros((5, 1024), F32)
    gains = GainSum(links, s.gain_parts)
    dp_low.advance()
    dp_high.advance()
    dp_mlp.advance()
    gains.advance()

    sum_mlp.arrive()

    def layer_out(i):
        s.stage[:, span(i)] = sum_mlp.total(s.mlp_own, span(i)).T.astype(BF16)

    loop(4, layer_out)
    load(s.stage, out)
    dp_low.advance()
    dp_high.advance()
    dp_mlp.advance()
    gains.advance()

    sum_dh1.arrive()

    def last_back_sum(i, total):
        rows = span(i, 128)
        grad = sum_dh1.total(s.keep_own, rows)
        s.keep_own[rows, :] = grad
        product = grad * (s.x_t[rows, :].astype(F32) * s.root1[0:1])
        return total + fold(product * twice(s.gain1[rows, :]))

    inner = lax.fori_loop(0, 8, last_back_sum, jnp.zeros((8, BLOCK), F32))
    inner = jnp.sum(inner, axis=0, keepdims=True) / 1024.0

    def last_back(i):
        rows = span(i)
        scaled = s.keep_own[rows, :] * twice(s.gain1[rows, :])
        normed = s.x_t[rows, :].astype(F32) * s.root1[0:1]
        s.result[:, rows] = (s.resid[rows, :] + s.root1[0:1] * (scaled - normed * inner)).T

    loop(4, last_back)
    load(s.result, grad_x)
    dp_mlp.complete()
    while dp_low.phase < 5 or dp_high.phase < 5 or gains.step < 7:
        dp_low.advance()
        dp_high.advance()
        gains.advance()
    load(s.sums, out_sums)
    out_g1[...] = gains.total[0:1]
    out_g2[...] = gains.total[1:2]
    out_gq[...] = gains.total[2:3, :128]
    out_gk[...] = gains.total[2:3, 128:256]

    for copy in loads[12:]:
        copy.wait()
    for exchange in (gather_h1, gather_da, sum_mlp, sum_dh1, dp_mlp, dp_high, dp_low, gains):
        exchange.drain()


def deliver_kernel(*refs):
    given, outs, held, (sems_in, sems_out) = refs[:7], refs[7:20], refs[20:27], refs[27:]
    copies = [pltpu.make_async_copy(a, b, sems_in.at[k]) for k, (a, b) in enumerate(zip(given, held))]
    for copy in copies:
        copy.start()
    sums = held[2]
    parts = [(held[0], outs[0]), (held[1], outs[1])]
    for g in range(2):
        for out, first, width in ((outs[2], 0, 256), (outs[3], 256, 128), (outs[4], 384, 128)):
            parts.append((sums.at[:, pl.ds(512 * g + first, width)], out.at[:, pl.ds(width * g, width)]))
    for out, first, width in ((outs[5], 1024, 512), (outs[6], 1536, 768), (outs[7], 2304, 768), (outs[8], 3072, 768)):
        parts.append((sums.at[:, pl.ds(first, width)], out))
    parts += list(zip(held[3:], outs[9:]))
    arrived = [False] * 7
    started = []
    for k, (src, dst) in enumerate(parts):
        need = k if k < 2 else 2 if k < 12 else k - 9
        if not arrived[need]:
            copies[need].wait()
            arrived[need] = True
        started.append(pltpu.make_async_copy(src, dst, sems_out.at[k]))
        started[k].start()
    for copy in started:
        copy.wait()


def shards(
    tokens,
    doc_starts,
    cotangent,
    w_query,
    key_matrix,
    value_matrix,
    w_out,
    w_gate,
    w_up,
    w_down,
    gain_attn,
    gain_mlp,
    gain_query,
    gain_key,
):
    frequency = ROPE_BASE ** (-(np.arange(64, dtype=np.float64) * 2.0) / HEAD)
    frequency = jnp.asarray(np.broadcast_to(frequency[:, None], (64, 128)).astype(np.float32))
    vmem = pl.BlockSpec(memory_space=pltpu.VMEM)
    hbm = pl.BlockSpec(memory_space=pl.ANY)
    smem = pl.BlockSpec(memory_space=pltpu.SMEM)

    def shaped(*shape, kind=F32):
        return jax.ShapeDtypeStruct(shape, kind)

    gains = (shaped(1, 1024), shaped(1, 1024), shaped(1, 128), shaped(1, 128))
    given = (shaped(256, 1024, kind=BF16), shaped(256, 1024), shaped(32, 3840), *gains)
    widths = (512, 256, 256, 512, 768, 768, 768)
    outs = pl.pallas_call(
        layer_kernel,
        out_shape=given,
        in_specs=[vmem, smem] + [hbm] * 8 + [vmem] * 5,
        out_specs=(hbm,) * 3 + (vmem,) * 4,
        scratch_shapes=[pltpu.VMEM(shape, kind) for _, shape, kind in SCRATCH]
        + [
            pltpu.SemaphoreType.DMA((2, SEMAPHORES)),
            pltpu.SemaphoreType.DMA((16,)),
            pltpu.SemaphoreType.REGULAR((2, 5)),
        ],
        compiler_params=pltpu.CompilerParams(
            collective_id=0, has_side_effects=True, vmem_limit_bytes=64 * 2**20 - 2**16
        ),
        cost_estimate=pl.CostEstimate(flops=32 * 10**9, bytes_accessed=2**24, transcendentals=2**22),
        name="layer",
    )(
        tokens.reshape(256, 1024),
        doc_starts,
        cotangent.reshape(256, 1024),
        w_query,
        key_matrix,
        value_matrix,
        w_out,
        w_gate.reshape(4, 4, 64, 768),
        w_up.reshape(4, 4, 64, 768),
        w_down,
        gain_attn.reshape(1, 1024),
        gain_mlp.reshape(1, 1024),
        gain_query.reshape(1, 128),
        gain_key.reshape(1, 128),
        frequency,
    )
    outs = pl.pallas_call(
        deliver_kernel,
        out_shape=given[:2] + tuple(shaped(32, width) for width in widths) + gains,
        in_specs=[hbm] * 7,
        out_specs=(hbm,) * 13,
        scratch_shapes=[pltpu.VMEM(one.shape, one.dtype) for one in given]
        + [pltpu.SemaphoreType.DMA((7,)), pltpu.SemaphoreType.DMA((16,))],
        name="deliver",
    )(*outs)
    return (
        outs[0].reshape(1, 256, 1024),
        outs[1].reshape(1, 256, 1024),
        *outs[2:5],
        outs[5].T,
        *outs[6:8],
        outs[8].T,
        *(gain.reshape(-1) for gain in outs[9:]),
    )


def solution(mesh):
    in_specs = (
        P("dp", "tensor", None),
        P("dp", None),
        P("dp", "tensor", None),
        P(None, "tensor"),
        P(None, "tensor"),
        P(None, "tensor"),
        P("tensor", None),
        P(None, "tensor"),
        P(None, "tensor"),
        P("tensor", None),
        P(),
        P(),
        P(),
        P(),
    )
    out_specs = (
        P("dp", "tensor", None),
        P("dp", "tensor", None),
        P("dp", "tensor"),
        P("dp", "tensor"),
        P("dp", "tensor"),
        P("tensor", "dp"),
        P("dp", "tensor"),
        P("dp", "tensor"),
        P("tensor", "dp"),
        P(),
        P(),
        P(),
        P(),
    )
    return jax.shard_map(shards, mesh=mesh, in_specs=in_specs, out_specs=out_specs, check_vma=False)
```

```python
import math

import jax
import jax.numpy as jnp
import numpy as np
from jax import lax
from jax.experimental import pallas as pl
from jax.experimental.pallas import tpu as pltpu
from jax.sharding import PartitionSpec as P

MESH = pl.DeviceIdType.MESH
BF16 = jnp.bfloat16
F32 = jnp.float32
EPSILON = 1e-06
ROPE_BASE = 1000000.0
BLOCK = 256
HALF = 128
HEAD = 128
QUERY_SCALE = math.log2(math.e) / math.sqrt(HEAD)
PARTNERS = ("core", "far", "y1", "y2", "z1", "z2", "x")
DIAGONALS = (("y", 2), ("z", 2), ("tensor", "far_core"))
ORDERS = (("y1", "y2", "z1", "z2"), ("y2", "y1", "z2", "z1"), ("z1", "z2", "y1", "y2"), ("z2", "z1", "y2", "y1"))
MLP_STREAMS = (
    ("mlp_mix", 0, 640, 0, 0, 0, 1536),
    ("mlp_mix", 640, 640, 4, 0, 1, 2176),
    ("mlp_mix", 1280, 256, 8, 0, 2, 2816),
    ("t_gu", 0, 256, 8, 256, 2, 3072),
    ("t_gu", 256, 512, 12, 0, 3, 3328),
)
ATTN_STREAMS = tuple(("attn_mix", 384 * k, 384, 4 * k, 0, k, 384 * k) for k in range(4))
GAIN_ORDER = ("y", "z", "tensor", "x")

SCRATCH = (
    ("w_qkv", (1024, 1024), BF16),
    ("t_qkv", (1024, 1024), BF16),
    ("w_down", (768, 1024), BF16),
    ("t_gu", (6, 4, 64, 1024), BF16),
    ("mlp_mix", (4, 4, 64, 2304), BF16),
    ("attn_mix", (4, 4, 64, 1536), BF16),
    ("h1", (1024, 1024), BF16),
    ("h2", (1024, 1024), BF16),
    ("da", (1024, 1024), BF16),
    ("norm_qk", (768, 1024), BF16),
    ("root_qk", (8, 1024), F32),
    ("ob", (512, 1024), BF16),
    ("qs", (2, 4, 128, 512), BF16),
    ("ks_t", (256, 1024), BF16),
    ("ks", (2, 1024, 128), BF16),
    ("v_t", (2, 144, 1024), BF16),
    ("v", (2, 1024, 128), BF16),
    ("p", (20, 4, 64, 512), BF16),
    ("inv", (2, 4, 8, 512), F32),
    ("inner", (2, 4, 8, 512), F32),
    ("hidden", (768, 1024), BF16),
    ("dgu", (1536, 1024), BF16),
    ("cosine", (64, 1024), F32),
    ("sine", (64, 1024), F32),
    ("x_t", (1024, 256), BF16),
    ("resid", (1024, 256), F32),
    ("gain1", (1024, 128), F32),
    ("gain2", (1024, 128), F32),
    ("gain_q", (128, 128), F32),
    ("gain_k", (128, 128), F32),
    ("gain_sum", (1024, 128), F32),
    ("gain_q_sum", (128, 128), F32),
    ("gain_k_sum", (128, 256), F32),
    ("root1", (8, 256), F32),
    ("root2", (8, 256), F32),
    ("keep_far", (1024, 256), F32),
    ("keep_own", (1024, 256), F32),
    ("sib_out", (2, 2, 1024, 128), BF16),
    ("sib_in", (2, 2, 1024, 128), BF16),
    ("far_out", (2, 1024, 128), BF16),
    ("far_in", (2, 1024, 128), BF16),
    ("mlp_own", (1024, 256), F32),
    ("mlp_sib_out", (2, 2, 1024, 128), BF16),
    ("mlp_sib_in", (2, 2, 1024, 128), BF16),
    ("mlp_far_out", (2, 1024, 128), BF16),
    ("mlp_far_in", (2, 1024, 128), BF16),
    ("mlp_halves", (16, 4, 64, 640), BF16),
    ("sums", (32, 3840), F32),
    ("stage", (256, 1024), BF16),
    ("x_in", (256, 1024), BF16),
    ("g1_in", (1, 1024), F32),
    ("g2_in", (1, 1024), F32),
    ("gq_in", (1, 128), F32),
    ("gk_in", (1, 128), F32),
    ("frequency", (64, 128), F32),
    ("gain_own", (24, 128), F32),
    ("gain_parts", (4, 4, 24, 128), F32),
)
SEMAPHORES = 160


class Box:
    pass


class Place:
    def __init__(self):
        dp = lax.axis_index("dp")
        tensor = lax.axis_index("tensor")
        self.z, self.y, self.x = dp // 8, (dp // 2) % 4, dp % 2
        self.far, self.core = tensor // 2, tensor % 2
        self.me = tensor
        self.sib = self.far * 2 + 1 - self.core
        self.across = (1 - self.far) * 2 + self.core
        self.across_sib = (1 - self.far) * 2 + 1 - self.core

    def near(self, name):
        return step_of(name, self.y if name[0] == "y" else self.z)

    def along(self, name):
        return {"y": self.y, "z": self.z, "x": self.x, "tensor": self.me}[name]

    def device(self, name):
        z, y, x, far, core = self.z, self.y, self.x, self.far, self.core
        if isinstance(name, tuple):
            axis, steps = name
            if axis == "tensor":
                if steps == "far_core":
                    far, core = 1 - far, 1 - core
                else:
                    turned = (self.me + steps) % 4
                    far, core = turned // 2, turned % 2
            elif axis == "y":
                y = (y + steps) % 4
            elif axis == "z":
                z = (z + steps) % 4
            else:
                x = 1 - x
        elif name[0] == "y":
            y = self.near(name)
        elif name[0] == "z":
            z = self.near(name)
        elif name == "x":
            x = 1 - x
        elif name == "far":
            far = 1 - far
        else:
            core = 1 - core
        return ((z * 4 + y) * 2 + x, far * 2 + core)


def step_of(name, value):
    return value + 1 - 2 * (value % 2) if name[1] == "1" else 3 - value


def nn(left, right):
    return lax.dot_general(left, right, (((1,), (0,)), ((), ())), preferred_element_type=F32)


def nt(left, right):
    return lax.dot_general(left, right, (((1,), (1,)), ((), ())), preferred_element_type=F32)


def span(index, size=BLOCK):
    return pl.ds(pl.multiple_of(index * size, size), size)


def loop(count, body):
    def step(index, carry):
        body(index)
        return carry

    lax.fori_loop(0, count, step, 0)


def twice(values):
    return jnp.concatenate([values, values], axis=1)


def fold(values):
    return jnp.sum(values.reshape(values.shape[0] // 8, 8, values.shape[1]), axis=0)


def sub(block, part):
    return pl.ds(pl.multiple_of(block * BLOCK + part * HALF, HALF), HALF)


def lanes(part, size=128):
    return pl.ds(part * size, size)


class Links:
    def __init__(self, place, sems):
        self.place, self.sems, self.used, self.sent = place, sems, 0, []

    def send(self, src, dst, name):
        copy = pltpu.make_async_remote_copy(
            src_ref=src,
            dst_ref=dst,
            send_sem=self.sems.at[0, self.used],
            recv_sem=self.sems.at[1, self.used],
            device_id=self.place.device(name),
            device_id_type=MESH,
        )
        self.used += 1
        copy.start()
        return copy


class Gather:
    def __init__(self, links, at):
        self.links, self.at = links, at
        self.far, self.sib, self.passed = [], [], []

    def send_far(self, part):
        half = self.at(self.links.place.me, part)
        self.far.append(self.links.send(half, half, "far"))

    def send_near(self, part):
        half = self.at(self.links.place.me, part)
        self.sib.append(self.links.send(half, half, "core"))

    def send(self, part):
        self.send_far(part)
        self.send_near(part)

    def pass_on(self, part):
        self.far[part].wait_recv()
        half = self.at(self.links.place.across, part)
        self.passed.append(self.links.send(half, half, "core"))

    def near_ready(self, part):
        self.sib[part].wait_recv()

    def far_ready(self, part):
        self.passed[part].wait_recv()

    def drain(self):
        for copy in self.far + self.sib + self.passed:
            copy.wait_send()


class Reduce:
    def __init__(self, links, sib_out, sib_in, far_out, far_in):
        self.links = links
        self.sib_out, self.sib_in, self.far_out, self.far_in = sib_out, sib_in, far_out, far_in
        self.copies = {}

    def to_sibling(self, index, part):
        copy = self.links.send(self.sib_out.at[index, part], self.sib_in.at[index, part], "core")
        self.copies[index, part] = copy

    def make_far(self, keep, part):
        self.copies[0, part].wait_recv()

        def body(i):
            rows = span(i, 512)
            summed = keep[rows, lanes(part)] + self.sib_in[0, part, rows, :].astype(F32)
            self.far_out[part, rows, :] = summed.astype(BF16)

        loop(2, body)

    def send_far(self, part):
        self.copies[2, part] = self.links.send(self.far_out.at[part], self.far_in.at[part], "far")

    def arrive(self, part):
        self.copies[1, part].wait_recv()
        self.copies[2, part].wait_recv()

    def total(self, keep, part, rows):
        near = keep[rows, lanes(part)] + self.sib_in[1, part, rows, :].astype(F32)
        return near + self.far_in[part, rows, :].astype(F32)

    def drain(self):
        for copy in self.copies.values():
            copy.wait_send()


class DpSum:
    def __init__(self, links, box, streams, bufs):
        self.links, self.bufs, self.out = links, bufs, box.sums
        self.streams = [(getattr(box, name), *rest) for name, *rest in streams]
        self.phase = -1
        self.flying = [[] for _ in streams]
        self.sent = []

    def spot(self, stream, slot, *rest):
        _, _, w, at, column, _, _ = self.streams[stream]
        lead = pl.ds(at + slot.start, slot.size) if isinstance(slot, pl.Slice) else at + slot
        return (lead, *rest, pl.ds(column, w))

    def held(self, stream, phase):
        every = slice(None)
        if phase == 0:
            spot = self.spot(stream, pl.ds(0, 2), every, every)
        elif phase == 1:
            spot = self.spot(stream, 2, every, every)
        elif phase == 2:
            spot = self.spot(stream, 3, pl.ds(0, 2), every)
        elif phase == 3:
            spot = self.spot(stream, 3, 2, every)
        else:
            spot = self.spot(stream, 3, 3, pl.ds(0, 32))
        return self.bufs.at[spot]

    def begin(self, stream, phase):
        place, send = self.links.place, self.links.send
        source_ref, first, w, _, _, order, _ = self.streams[stream]
        order = ORDERS[order]
        into = self.held(stream, phase)
        if phase == 4:
            theirs = self.bufs.at[self.spot(stream, 3, 2, span(1 - place.x, 32))]
            return [send(theirs, into, "x")]
        name = order[phase]
        if phase in (1, 3):
            return [send(self.held(stream, phase - 1).at[1], into, name)]
        there = place.near(name)
        copies = []
        for j, at in enumerate((there, step_of(order[phase + 1], there))):
            if phase == 2:
                source = self.held(stream, 1).at[at]
            else:
                lead = (pl.ds(0, 4), at) if name[0] == "y" else (at, slice(None))
                source = source_ref.at[(*lead, slice(None), pl.ds(first, w))]
            copies.append(send(source, into.at[j], name))
        return copies

    def finish(self, stream, phase):
        place, spot, bufs = self.links.place, self.spot, self.bufs
        source_ref, first, w, _, _, order, out_first = self.streams[stream]
        order = ORDERS[order]
        every = slice(None)
        for copy in self.flying[stream]:
            copy.wait_recv()
        if phase == 4:
            mine = bufs[spot(stream, 3, 2, span(place.x, 32))].astype(F32)
            columns = pl.ds(out_first, w)
            self.out[:, columns] = bufs[spot(stream, 3, 3, pl.ds(0, 32))].astype(F32) + mine
        elif phase == 3:
            bufs[spot(stream, 3, 2, every)] += bufs[spot(stream, 3, 0, every)]
        elif phase == 1:
            for k in range(4):
                bufs[spot(stream, 2, k, every)] += bufs[spot(stream, 0, k, every)]
        else:
            name = order[phase]
            mine = place.y if name[0] == "y" else place.z
            for j, own in enumerate((mine, step_of(order[phase + 1], mine))):
                if phase == 2:
                    bufs[spot(stream, 3, j, every)] += bufs[spot(stream, 2, own, every)]
                    continue
                for k in range(4):
                    lead = (k, own) if name[0] == "y" else (own, k)
                    kept = source_ref[(*lead, every, pl.ds(first, w))]
                    bufs[spot(stream, j, k, every)] += kept

    def advance(self):
        if self.phase == 5:
            return
        for stream in range(len(self.streams)):
            if self.phase >= 0:
                self.finish(stream, self.phase)
                self.sent += self.flying[stream]
            if self.phase < 4:
                self.flying[stream] = self.begin(stream, self.phase + 1)
        self.phase += 1

    def complete(self):
        while self.phase < 5:
            self.advance()

    def drain(self):
        for copy in self.sent:
            copy.wait_send()


class GainSum:
    def __init__(self, links, own, parts):
        self.links, self.parts, self.copies, self.step = links, parts, [], 0
        self.begin(own[...])

    def begin(self, values):
        place, name = self.links.place, GAIN_ORDER[self.step]
        mine = place.along(name)
        half = self.parts.at[self.step, mine]
        self.parts[self.step, mine] = values
        count = 2 if name == "x" else 4
        self.copies.append([self.links.send(half, half, (name, k)) for k in range(1, count)])

    def advance(self):
        if self.step == 4:
            return
        for copy in self.copies[self.step]:
            copy.wait_recv()
        parts = [self.parts[self.step, k] for k in range(len(self.copies[self.step]) + 1)]
        total = parts[0] + parts[1]
        if len(parts) == 4:
            total = total + (parts[2] + parts[3])
        self.step += 1
        if self.step < 4:
            self.begin(total)
        else:
            self.total = total

    def drain(self):
        for copies in self.copies:
            for copy in copies:
                copy.wait_send()


def head_forward(raw, gain, cosine, sine):
    root = lax.rsqrt(jnp.mean(raw * raw, axis=0, keepdims=True) + EPSILON)
    normed = raw * root
    scaled = normed * gain
    first, second = scaled[:64], scaled[64:]
    turned = jnp.concatenate([first * cosine - second * sine, second * cosine + first * sine], axis=0)
    return normed, root, turned


def head_backward(grad, normed, root, gain, cosine, sine):
    first, second = grad[:64], grad[64:]
    turned = jnp.concatenate([first * cosine + second * sine, second * cosine - first * sine], axis=0)
    scaled = turned * gain
    inner = jnp.mean(scaled * normed, axis=0, keepdims=True)
    return root * (scaled - normed * inner), turned * normed


def layer_kernel(
    x, starts, dy, wq, wk, wv, wo, wg, wu, wd, g1, g2, gq, gk, frequency,
    out, grad_x, out_sums, out_gains,
    *scratch,
):
    s = Box()
    for (name, _, _), ref in zip(SCRATCH, scratch):
        setattr(s, name, ref)
    link_sems, load_sems, ready = scratch[len(SCRATCH) :]
    place = Place()
    links = Links(place, link_sems)
    me, sib, across, across_sib = place.me, place.sib, place.across, place.across_sib

    barrier = pltpu.get_barrier_semaphore()
    for name in PARTNERS + DIAGONALS:
        pl.semaphore_signal(barrier, inc=1, device_id=place.device(name), device_id_type=MESH)

    loads = []

    def load(src, dst):
        copy = pltpu.make_async_copy(src, dst, load_sems.at[len(loads)])
        copy.start()
        loads.append(copy)

    load(x, s.x_in)
    load(g1, s.g1_in)
    for g in range(2):
        load(wq.at[:, pl.ds(256 * g, 256)], s.w_qkv.at[:, pl.ds(512 * g, 256)])
        load(wk.at[:, pl.ds(128 * g, 128)], s.w_qkv.at[:, pl.ds(512 * g + 256, 128)])
        load(wv.at[:, pl.ds(128 * g, 128)], s.w_qkv.at[:, pl.ds(512 * g + 384, 128)])
    load(wo, s.h2.at[pl.ds(0, 512)])
    load(wg, s.mlp_mix.at[:, :, :, pl.ds(0, 768)])
    load(wu, s.mlp_mix.at[:, :, :, pl.ds(768, 768)])
    load(wd, s.w_down)
    load(dy, s.da.at[pl.ds(0, 256)])
    load(g2, s.g2_in)
    load(gq, s.gq_in)
    load(gk, s.gk_in)
    load(frequency, s.frequency)

    near_pair, far_pair = (sib, me), (across_sib, across)

    def pair(ref, rows, blocks, part):
        return jnp.concatenate([ref[rows, sub(b, part)] for b in blocks], axis=1)

    def unpair(ref, rows, blocks, part, values):
        for n, b in enumerate(blocks):
            ref[rows, sub(b, part)] = values[:, HALF * n : HALF * n + HALF]

    every = pl.ds(0, 1024)

    loads[0].wait()
    loads[1].wait()
    gather_h1 = Gather(links, lambda b, part: s.h1.at[:, sub(b, part)])
    for part in range(2):

        def first_norm(i, part=part):
            rows = span(2 * part + i, 64)
            xs = s.x_in[rows, :].astype(F32)
            root = lax.rsqrt(jnp.mean(xs * xs, axis=1, keepdims=True) + EPSILON)
            s.stage[rows, :] = (xs * root * s.g1_in[...]).astype(BF16)

        loop(2, first_norm)
        for j in range(4):
            s.h1[pl.ds(256 * j, 256), sub(me, part)] = s.stage[lanes(part), pl.ds(256 * j, 256)].T
        if part == 0:
            pl.semaphore_wait(barrier, len(PARTNERS) + len(DIAGONALS))
        gather_h1.send(part)

    for k in range(2, 8):
        loads[k].wait()

    def turn_qkv(i):
        s.t_qkv[span(i), :] = s.w_qkv[:, span(i)].T

    loop(4, turn_qkv)

    for k in range(13, 17):
        loads[k].wait()
    place_row = lax.broadcasted_iota(jnp.int32, (8, 1024), 1)
    start_row = jnp.zeros((8, 1024), jnp.int32)
    for d in range(4):
        start_row = jnp.maximum(start_row, jnp.where(place_row >= starts[0, d], starts[0, d], 0))
    position = (place_row - start_row).astype(F32)
    for i in range(8):
        columns = pl.ds(128 * i, 128)
        angle = s.frequency[...] * position[0:1, 128 * i : 128 * i + 128]
        s.cosine[:, columns] = jnp.cos(angle)
        s.sine[:, columns] = jnp.sin(angle)
    for qb in range(4):
        first = start_row[0:1, qb * 256 : qb * 256 + 256]
        query = lax.broadcasted_iota(jnp.int32, (256, 256), 1) + qb * 256
        for kb in range(qb + 1):
            key = lax.broadcasted_iota(jnp.int32, (256, 256), 0) + kb * 256
            allowed = (key <= query) & (key >= first)
            s.dgu[pl.ds(256 * kb, 256), pl.ds(256 * qb, 256)] = jnp.where(allowed, 1.0, 0.0).astype(BF16)

    s.gain1[...] = jnp.broadcast_to(s.g1_in[...], (128, 1024)).T
    s.gain2[...] = jnp.broadcast_to(s.g2_in[...], (128, 1024)).T
    s.gain_q[...] = jnp.broadcast_to(s.gq_in[...], (128, 128)).T
    s.gain_k[...] = jnp.broadcast_to(s.gk_in[...], (128, 128)).T
    s.gain_q_sum[...] = jnp.zeros((128, 128), F32)
    s.gain_sum[...] = jnp.zeros((1024, 128), F32)
    s.gain_k_sum[...] = jnp.zeros((128, 256), F32)
    for g in range(2):
        s.v_t[g, pl.ds(128, 16), :] = jnp.ones((16, 1024), BF16)

    def x_in(i, total):
        turned = s.x_in[:, span(i)].astype(F32).T
        s.x_t[span(i), :] = turned.astype(BF16)
        return total + fold(turned * turned)

    square = lax.fori_loop(0, 4, x_in, jnp.zeros((8, BLOCK), F32))
    root = lax.rsqrt(jnp.sum(square, axis=0, keepdims=True) / 1024.0 + EPSILON)
    s.root1[...] = jnp.broadcast_to(root, (8, BLOCK))

    loads[8].wait()

    def turn_out(i):
        s.attn_mix[i, :, :, pl.ds(1024, 512)] = s.h2[pl.ds(0, 512), span(i)].T.reshape(4, 64, 512)

    loop(4, turn_out)
    loads[9].wait()
    loads[10].wait()

    def turn_gu(i):
        for z in range(4):
            turned = s.mlp_mix[z, :, :, span(i)].reshape(256, 256).T
            s.t_gu[i, :, :, pl.ds(256 * z, 256)] = turned.reshape(4, 64, 256)

    loop(6, turn_gu)
    loads[11].wait()

    def turn_down(i):
        s.mlp_mix[i, :, :, pl.ds(1536, 768)] = s.w_down[:, span(i)].T.reshape(4, 64, 768)

    loop(4, turn_down)

    def dy_in(i):
        s.attn_mix[i, :, :, span(me)] = s.da[pl.ds(0, 256), span(i)].T.reshape(4, 64, BLOCK)

    loads[12].wait()
    loop(4, dy_in)

    def project(blocks, part):
        cosine, sine = pair(s.cosine, pl.ds(0, 64), blocks, part), pair(s.sine, pl.ds(0, 64), blocks, part)
        query_gain = twice(s.gain_q[...] * QUERY_SCALE)
        key_gain = twice(s.gain_k[...])
        every_raw = nn(s.t_qkv[...], pair(s.h1, every, blocks, part))
        for g in range(2):
            raw = every_raw[512 * g : 512 * g + 512]
            for k in range(2):
                head = 3 * g + k
                normed, root, turned = head_forward(raw[128 * k : 128 * k + 128], query_gain, cosine, sine)
                unpair(s.norm_qk, pl.ds(128 * head, 128), blocks, part, normed.astype(BF16))
                unpair(s.root_qk, pl.ds(head, 1), blocks, part, root)
                turned = turned.astype(BF16)
                for n, b in enumerate(blocks):
                    s.qs[g, b, :, pl.ds(256 * part + 128 * k, 128)] = turned[:, HALF * n : HALF * n + HALF]
            normed, root, turned = head_forward(raw[256:384], key_gain, cosine, sine)
            turned, values = turned.astype(BF16), raw[384:].astype(BF16)
            unpair(s.norm_qk, pl.ds(384 * g + 256, 128), blocks, part, normed.astype(BF16))
            unpair(s.root_qk, pl.ds(3 * g + 2, 1), blocks, part, root)
            unpair(s.ks_t, pl.ds(128 * g, 128), blocks, part, turned)
            for n, b in enumerate(blocks):
                s.v_t[g, pl.ds(0, 128), sub(b, part)] = values[:, HALF * n : HALF * n + HALF]
                s.ks[g, sub(b, part), :] = turned[:, HALF * n : HALF * n + HALF].T
                s.v[g, sub(b, part), :] = values[:, HALF * n : HALF * n + HALF].T

    def both_roles(own, body):
        for far in range(2):
            blocks = (2 * far, 2 * far + 1) if own else (2 - 2 * far, 3 - 2 * far)
            pl.when(place.far == far)(lambda blocks=blocks: body(blocks))

    def p_slots(g, qb):
        return pl.ds(g * 10 + qb * (qb + 1) // 2, qb + 1)

    def attend(blocks, parts):
        first, wide = 256 * parts[0], 256 * len(parts)
        cut = pl.ds(first, wide)
        chains = [(qb, g, 256 * (qb + 1)) for qb in blocks for g in range(2)]
        scores = [nn(s.ks[g, pl.ds(0, keys), :], s.qs[g, qb, :, cut]) for qb, g, keys in chains]
        weights = []
        for (qb, g, keys), score in zip(chains, scores):
            halves = [twice(s.dgu[pl.ds(0, keys), pl.ds(256 * qb + HALF * part, HALF)]) for part in parts]
            mask = halves[0] if len(parts) == 1 else jnp.concatenate(halves, axis=1)
            weights.append(jnp.exp2(score).astype(BF16) * mask)
        products = [nn(s.v_t[g, :, pl.ds(0, keys)], weight) for (qb, g, keys), weight in zip(chains, weights)]
        for (qb, g, keys), weight, product in zip(chains, weights, products):
            s.p[p_slots(g, qb), :, :, cut] = weight.reshape(qb + 1, 4, 64, wide)
            inverse = 1.0 / product[128:136]
            s.inv[g, qb, :, cut] = inverse
            attended = (product[:128] * inverse[0:1]).astype(BF16)
            for n, part in enumerate(parts):
                for k in range(2):
                    columns = slice(256 * n + 128 * k, 256 * n + 128 * k + 128)
                    s.ob[pl.ds(256 * g + 128 * k, 128), pl.ds(256 * qb + HALF * part, HALF)] = attended[:, columns]

    def out_product(blocks, part, store):
        attended = pair(s.ob, pl.ds(0, 512), blocks, part)
        store(nn(s.attn_mix[:, :, :, pl.ds(1024, 512)].reshape(1024, 512), attended))

    def split(sib_out, index, part, keep):
        def store(values):
            sib_out[index, part] = values[:, :HALF].astype(BF16)
            keep[:, lanes(part)] = values[:, HALF:]

        return store

    for part in range(2):
        gather_h1.near_ready(part)
        project(near_pair, part)
    gather_h1.pass_on(0)
    gather_h1.far_ready(0)
    project(far_pair, 0)
    gather_h1.pass_on(1)
    gather_dy = Gather(links, lambda b, part: s.attn_mix.at[:, :, :, sub(b, part)])
    for part in range(2):
        gather_dy.send_near(part)
    gather_dy.send_far(0)
    gather_h1.far_ready(1)
    project(far_pair, 1)

    sum_attn = Reduce(links, s.sib_out, s.sib_in, s.far_out, s.far_in)
    for part in range(2):
        both_roles(False, lambda blocks, part=part: attend(blocks, (part,)))
        out_product(far_pair, part, split(s.sib_out, 0, part, s.keep_far))
        sum_attn.to_sibling(0, part)
        if part == 1:
            sum_attn.make_far(s.keep_far, 0)
            sum_attn.send_far(0)
    both_roles(True, lambda blocks: attend(blocks, (0, 1)))
    sum_attn.make_far(s.keep_far, 1)
    sum_attn.send_far(1)
    for part in range(2):
        out_product(near_pair, part, split(s.sib_out, 1, part, s.keep_own))
        sum_attn.to_sibling(1, part)
    for part in range(2):
        gather_dy.near_ready(part)
    gather_dy.pass_on(0)

    gather_h2 = Gather(links, lambda b, part: s.h2.at[:, sub(b, part)])

    def second_norm(part):
        sum_attn.arrive(part)

        def square(i, total):
            x1 = s.x_t[span(i), lanes(part)].astype(F32) + sum_attn.total(s.keep_own, part, span(i))
            s.resid[span(i), lanes(part)] = x1
            return total + fold(x1 * x1)

        total = lax.fori_loop(0, 4, square, jnp.zeros((8, HALF), F32))
        root = lax.rsqrt(jnp.sum(total, axis=0, keepdims=True) / 1024.0 + EPSILON)
        s.root2[:, lanes(part)] = jnp.broadcast_to(root, (8, HALF))

        def scale(i):
            normed = s.resid[span(i), lanes(part)] * s.root2[0:1, lanes(part)]
            s.h2[span(i), sub(me, part)] = (normed * s.gain2[span(i), :]).astype(BF16)

        loop(4, scale)
        gather_h2.send(part)

    second_norm(0)
    second_norm(1)
    gather_dy.send_far(1)
    sum_attn.drain()
    gather_dy.far_ready(0)

    def feed(blocks, part):
        def body(j):
            gate = nn(s.t_gu[j].reshape(256, 1024), pair(s.h2, every, blocks, part))
            up = nn(s.t_gu[3 + j].reshape(256, 1024), pair(s.h2, every, blocks, part))
            grads = [s.attn_mix[:, :, :, sub(b, part)].reshape(1024, HALF) for b in blocks]
            grad = nn(s.w_down[span(j), :], jnp.concatenate(grads, axis=1))
            open_gate = jax.nn.sigmoid(gate)
            silu = gate * open_gate
            unpair(s.hidden, span(j), blocks, part, (silu * up).astype(BF16))
            dgate = (grad * up * open_gate * (1.0 + gate * (1.0 - open_gate))).astype(BF16)
            unpair(s.dgu, span(j), blocks, part, dgate)
            unpair(s.dgu, span(3 + j), blocks, part, (grad * silu).astype(BF16))

        for j in range(3):
            body(j)

    def feed_back(blocks, part, store):
        grads = pair(s.dgu, pl.ds(0, 1536), blocks, part)
        store(nn(s.mlp_mix[:, :, :, pl.ds(0, 1536)].reshape(1024, 1536), grads))

    def mlp_product(blocks, part, store):
        hidden = pair(s.hidden, pl.ds(0, 768), blocks, part)
        store(nn(s.mlp_mix[:, :, :, pl.ds(1536, 768)].reshape(1024, 768), hidden))

    sum_dh2 = Reduce(links, s.sib_out, s.sib_in, s.far_out, s.far_in)
    for part in range(2):
        gather_h2.near_ready(part)
        feed(near_pair, part)
        feed_back(near_pair, part, split(s.sib_out, 1, part, s.keep_own))
        sum_dh2.to_sibling(1, part)
    gather_h2.pass_on(0)
    gather_h2.far_ready(0)
    feed(far_pair, 0)
    feed_back(far_pair, 0, split(s.sib_out, 0, 0, s.keep_far))
    sum_dh2.to_sibling(0, 0)
    gather_h2.pass_on(1)
    sum_dh2.make_far(s.keep_far, 0)
    sum_dh2.send_far(0)
    gather_dy.pass_on(1)
    gather_h2.far_ready(1)
    gather_dy.far_ready(1)
    feed(far_pair, 1)
    feed_back(far_pair, 1, split(s.sib_out, 0, 1, s.keep_far))
    sum_dh2.to_sibling(0, 1)

    def gate_up_grad(j):
        values = nt(s.h2[...], s.dgu[pl.ds(512 * j, 512), :]).astype(BF16)
        s.mlp_mix[:, :, :, pl.ds(512 * j, 512)] = values.reshape(4, 4, 64, 512)

    def down_grad(j):
        values = nt(s.attn_mix[:, :, :, pl.ds(0, 1024)].reshape(1024, 1024), s.hidden[pl.ds(384 * j, 384), :])
        s.t_gu[pl.ds(0, 4), :, :, pl.ds(384 * j, 384)] = values.astype(BF16).reshape(4, 4, 64, 384)

    gather_da = Gather(links, lambda b, part: s.da.at[:, sub(b, part)])

    def norm_back(part):
        sum_dh2.arrive(part)

        def inner_sum(i, total):
            grad = sum_dh2.total(s.keep_own, part, span(i))
            s.keep_own[span(i), lanes(part)] = grad
            product = grad * (s.resid[span(i), lanes(part)] * s.root2[0:1, lanes(part)])
            s.gain_sum[span(i), :] += product
            return total + fold(product * s.gain2[span(i), :])

        inner = lax.fori_loop(0, 4, inner_sum, jnp.zeros((8, HALF), F32))
        inner = jnp.sum(inner, axis=0, keepdims=True) / 1024.0

        def body(i):
            root = s.root2[0:1, lanes(part)]
            scaled = s.keep_own[span(i), lanes(part)] * s.gain2[span(i), :]
            normed = s.resid[span(i), lanes(part)] * root
            own = s.attn_mix[i, :, :, sub(me, part)].reshape(256, HALF).astype(F32)
            s.da[span(i), sub(me, part)] = (own + root * (scaled - normed * inner)).astype(BF16)
            s.mlp_own[span(i), lanes(part)] = s.resid[span(i), lanes(part)]
            s.resid[span(i), lanes(part)] = own + root * (scaled - normed * inner)

        loop(4, body)
        gather_da.send(part)

    gate_up_grad(0)
    sum_dh2.make_far(s.keep_far, 1)
    sum_dh2.send_far(1)
    gate_up_grad(1)
    norm_back(0)
    gate_up_grad(2)
    gather_h2.drain()
    load(wo, s.h2.at[pl.ds(0, 512)])
    down_grad(0)
    down_grad(1)
    dp_mlp = DpSum(links, s, MLP_STREAMS, s.mlp_halves)
    dp_mlp.advance()
    norm_back(1)
    sum_dh2.drain()

    def put_gain(first, row):
        for k in range(row.shape[1] // 128):
            s.gain_own[first + k : first + k + 1, :] = row[:, 128 * k : 128 * k + 128]

    put_gain(8, jnp.sum(s.gain_sum[...].T, axis=0, keepdims=True))
    s.gain_sum[...] = jnp.zeros((1024, 128), F32)

    sum_mlp = Reduce(links, s.mlp_sib_out, s.mlp_sib_in, s.mlp_far_out, s.mlp_far_in)

    def mlp_mine(part):
        def store(values):
            s.mlp_sib_out[1, part] = values[:, :HALF].astype(BF16)
            s.mlp_own[:, lanes(part)] += values[:, HALF:]

        return store

    for part in range(2):
        mlp_product(far_pair, part, split(s.mlp_sib_out, 0, part, s.keep_far))
        sum_mlp.to_sibling(0, part)
    for part in range(2):
        mlp_product(near_pair, part, mlp_mine(part))
        sum_mlp.to_sibling(1, part)
    for part in range(2):
        sum_mlp.make_far(s.keep_far, part)

    s.keep_own[...] = jnp.zeros((1024, 256), F32)
    s.keep_far[...] = jnp.zeros((1024, 256), F32)
    loads[17].wait()

    def dob(g, b, part):
        index = g * 4 + b
        return (4 + index // 4, pl.ds(2 * ((index // 2) % 2), 2), slice(None), pl.ds(pl.multiple_of((index % 2) * 512 + part * 256, 256), 256))

    def out_back(blocks, part):
        two = lanes(part, 256)
        every_grad = nn(s.h2[pl.ds(0, 512), :], pair(s.da, every, blocks, part))
        for g in range(2):
            grads = every_grad[256 * g : 256 * g + 256]
            for n, b in enumerate(blocks):
                columns = slice(HALF * n, HALF * n + HALF)
                both = jnp.concatenate([grads[:128, columns], grads[128:, columns]], axis=1) * s.inv[g, b, 0:1, two]
                outs = [s.ob[pl.ds(256 * g + 128 * k, 128), sub(b, part)] for k in range(2)]
                inner = jnp.sum(both * jnp.concatenate(outs, axis=1).astype(F32), axis=0, keepdims=True)
                s.inner[g, b, :, two] = jnp.broadcast_to(inner, (8, 256))
                s.t_gu[dob(g, b, part)] = both.astype(BF16).reshape(2, 64, 256)

    def attend_back(blocks, parts, groups):
        first, wide = 256 * parts[0], 256 * len(parts)
        cut = pl.ds(first, wide)
        chains = [(qb, g, 256 * (qb + 1)) for qb in blocks for g in groups]
        grads, weights, slopes, changes, key_parts, query_parts, value_parts = [], [], [], [], [], [], []
        for qb, g, keys in chains:
            index = g * 4 + qb
            at = (4 + index // 4, pl.ds(2 * ((index // 2) % 2), 2), slice(None), pl.ds((index % 2) * 512 + first, wide))
            grads.append(s.t_gu[at].reshape(128, wide))
            weights.append(s.p[p_slots(g, qb), :, :, cut].reshape(keys, wide))
        for (qb, g, keys), grad in zip(chains, grads):
            slopes.append(nn(s.v[g, pl.ds(0, keys), :], grad))
        for weight, grad in zip(weights, grads):
            value_parts.append(nt(weight, grad))
        for (qb, g, keys), weight, slope in zip(chains, weights, slopes):
            changes.append((weight.astype(F32) * (slope - s.inner[g, qb, 0:1, cut])).astype(BF16))
        for (qb, g, keys), change in zip(chains, changes):
            key_parts.append(nt(change, s.qs[g, qb, :, cut]))
            query_parts.append(nn(s.ks_t[pl.ds(128 * g, 128), pl.ds(0, keys)], change))
        for (qb, g, keys), value_part, key_part, query_part in zip(chains, value_parts, key_parts, query_parts):
            s.keep_own[pl.ds(0, keys), lanes(g)] += value_part
            s.keep_far[pl.ds(0, keys), lanes(g)] += key_part
            for n, part in enumerate(parts):
                columns = pl.ds(256 * qb + HALF * part, HALF)
                for k in range(2):
                    head = 3 * g + k
                    grad, gain_part = head_backward(
                        query_part[:, 256 * n + 128 * k : 256 * n + 128 * k + 128] * (1.0 / math.sqrt(HEAD)),
                        s.norm_qk[pl.ds(128 * head, 128), columns].astype(F32),
                        s.root_qk[pl.ds(head, 1), columns],
                        s.gain_q[...],
                        s.cosine[:, columns],
                        s.sine[:, columns],
                    )
                    s.t_qkv[pl.ds(512 * g + 128 * k, 128), columns] = grad.astype(BF16)
                    s.gain_q_sum[...] += gain_part

    def key_back(g):
        gain = twice(s.gain_k[...])

        def body(b):
            columns = span(b)
            grad, gain_part = head_backward(
                s.keep_far[columns, lanes(g)].T * math.log(2.0),
                s.norm_qk[pl.ds(384 * g + 256, 128), columns].astype(F32),
                s.root_qk[pl.ds(3 * g + 2, 1), columns],
                gain,
                s.cosine[:, columns],
                s.sine[:, columns],
            )
            s.t_qkv[pl.ds(512 * g + 256, 128), columns] = grad.astype(BF16)
            s.gain_k_sum[...] += gain_part
            s.t_qkv[pl.ds(512 * g + 384, 128), columns] = s.keep_own[columns, lanes(g)].T.astype(BF16)

        loop(4, body)

    def tell_ready():
        for k, name in enumerate(PARTNERS[2:]):
            pl.semaphore_signal(ready.at[k], inc=1, device_id=place.device(name), device_id_type=MESH)

    def wait_ready():
        for k in range(5):
            pl.semaphore_wait(ready.at[k], 1)

    def qkv_grad(g):
        values = nt(s.h1[...], s.t_qkv[pl.ds(512 * g, 512), :]).astype(BF16)
        s.attn_mix[:, :, :, pl.ds(512 * g, 512)] = values.reshape(4, 4, 64, 512)

    def out_grad():
        values = nt(s.da[...], s.ob[...]).astype(BF16)
        s.attn_mix[:, :, :, pl.ds(1024, 512)] = values.reshape(4, 4, 64, 512)

    for part in range(2):
        gather_da.near_ready(part)
        out_back(near_pair, part)
    gather_da.pass_on(0)
    both_roles(True, lambda blocks: attend_back(blocks, (0, 1), (0, 1)))
    gather_da.far_ready(0)
    out_back(far_pair, 0)
    gather_da.pass_on(1)
    sum_mlp.send_far(0)
    both_roles(False, lambda blocks: attend_back(blocks, (0,), (0, 1)))
    gather_da.far_ready(1)
    out_back(far_pair, 1)
    gather_dy.drain()
    both_roles(False, lambda blocks: attend_back(blocks, (1,), (0, 1)))
    tell_ready()
    dp_mlp.advance()
    for g in range(2):
        key_back(g)
    out_grad()
    for g in range(2):
        qkv_grad(g)
    wait_ready()
    dp_attn = DpSum(links, s, ATTN_STREAMS, s.p)
    dp_attn.advance()

    def in_back(blocks, part, store):
        values = nn(s.w_qkv[...], pair(s.t_qkv, every, blocks, part))
        product = values * pair(s.h1, every, blocks, part).astype(F32)
        s.gain_sum[...] += product[:, :HALF] + product[:, HALF:]
        store(values)

    sum_dh1 = Reduce(links, s.sib_out, s.sib_in, s.far_out, s.far_in)
    for part in range(2):
        in_back(far_pair, part, split(s.sib_out, 0, part, s.keep_far))
        sum_dh1.to_sibling(0, part)
    for part in range(2):
        sum_dh1.make_far(s.keep_far, part)
        sum_dh1.send_far(part)
    sum_mlp.send_far(1)
    for part in range(2):
        in_back(near_pair, part, split(s.sib_out, 1, part, s.keep_own))
        sum_dh1.to_sibling(1, part)
    put_gain(0, jnp.sum((s.gain_sum[...] / s.gain1[...]).T, axis=0, keepdims=True))
    both = s.gain_k_sum[:, lanes(0)] + s.gain_k_sum[:, lanes(1)]
    put_gain(16, jnp.sum(s.gain_q_sum[...].T, axis=0, keepdims=True))
    put_gain(17, jnp.sum(both.T, axis=0, keepdims=True))
    s.gain_own[pl.ds(18, 6), :] = jnp.zeros((6, 128), F32)
    gains = GainSum(links, s.gain_own, s.gain_parts)
    dp_mlp.advance()
    gains.advance()
    dp_mlp.advance()
    dp_attn.advance()
    gains.advance()
    dp_mlp.advance()

    for part in range(2):
        sum_dh1.arrive(part)

        def inner_sum(i, total, part=part):
            grad = sum_dh1.total(s.keep_own, part, span(i))
            s.keep_own[span(i), lanes(part)] = grad
            normed = s.x_t[span(i), lanes(part)].astype(F32) * s.root1[0:1, lanes(part)]
            return total + fold(grad * normed * s.gain1[span(i), :])

        inner = lax.fori_loop(0, 4, inner_sum, jnp.zeros((8, HALF), F32))
        inner = jnp.sum(inner, axis=0, keepdims=True) / 1024.0

        def last_back(i, part=part, inner=inner):
            root = s.root1[0:1, lanes(part)]
            scaled = s.keep_own[span(i), lanes(part)] * s.gain1[span(i), :]
            normed = s.x_t[span(i), lanes(part)].astype(F32) * root
            s.resid[span(i), lanes(part)] += root * (scaled - normed * inner)

        loop(4, last_back)
        if part == 0:
            dp_attn.advance()
            gains.advance()
    load(s.resid, grad_x)

    for part in range(2):
        sum_mlp.arrive(part)

        def layer_out(i, part=part):
            s.stage[lanes(part), span(i)] = sum_mlp.total(s.mlp_own, part, span(i)).T.astype(BF16)

        loop(4, layer_out)
    load(s.stage, out)
    while dp_attn.phase < 5 or dp_mlp.phase < 5 or gains.step < 4:
        dp_attn.advance()
        gains.advance()
        dp_mlp.advance()
    load(s.sums, out_sums)
    s.gain_own[...] = gains.total
    load(s.gain_own, out_gains)

    for copy in loads[18:]:
        copy.wait()
    for exchange in (gather_h1, gather_da, sum_mlp, sum_dh1, dp_mlp, dp_attn, gains):
        exchange.drain()


def deliver_kernel(*refs):
    given, outs, held = refs[:4], refs[4:17], refs[17:21]
    turned, gain_rows, sems_in, sems_out = refs[21:]
    arrivals = [pltpu.make_async_copy(a, b, sems_in.at[k]) for k, (a, b) in enumerate(zip(given, held))]
    for copy in arrivals:
        copy.start()
    started = []

    def send(src, dst):
        copy = pltpu.make_async_copy(src, dst, sems_out.at[len(started)])
        copy.start()
        started.append(copy)

    arrivals[3].wait()
    gain_rows[0] = held[3][16:17]
    gain_rows[1] = held[3][17:18]
    send(held[3].at[pl.ds(0, 8)], outs[9])
    send(held[3].at[pl.ds(8, 8)], outs[10])
    send(gain_rows.at[0], outs[11])
    send(gain_rows.at[1], outs[12])
    arrivals[2].wait()
    sums = held[2]
    for g in range(2):
        for out, first, width in ((outs[2], 0, 256), (outs[3], 256, 128), (outs[4], 384, 128)):
            send(sums.at[:, pl.ds(512 * g + first, width)], out.at[:, pl.ds(width * g, width)])
    for out, first, width in ((outs[5], 1024, 512), (outs[6], 1536, 768), (outs[7], 2304, 768), (outs[8], 3072, 768)):
        send(sums.at[:, pl.ds(first, width)], out)
    arrivals[0].wait()
    send(held[0], outs[0])
    arrivals[1].wait()
    for i in range(4):
        turned[:, pl.ds(256 * i, 256)] = held[1][pl.ds(256 * i, 256), :].T
    send(turned, outs[1])
    for copy in started:
        copy.wait()


def shards(
    tokens,
    doc_starts,
    cotangent,
    w_query,
    key_matrix,
    value_matrix,
    w_out,
    w_gate,
    w_up,
    w_down,
    gain_attn,
    gain_mlp,
    gain_query,
    gain_key,
):
    frequency = ROPE_BASE ** (-(np.arange(64, dtype=np.float64) * 2.0) / HEAD)
    frequency = jnp.asarray(np.broadcast_to(frequency[:, None], (64, 128)).astype(np.float32))
    hbm = pl.BlockSpec(memory_space=pl.ANY)
    smem = pl.BlockSpec(memory_space=pltpu.SMEM)

    def shaped(*shape, kind=F32):
        return jax.ShapeDtypeStruct(shape, kind)

    gains = (shaped(8, 128), shaped(8, 128), shaped(1, 128), shaped(1, 128))
    given = (shaped(256, 1024, kind=BF16), shaped(1024, 256), shaped(32, 3840), shaped(24, 128))
    widths = (512, 256, 256, 512, 768, 768, 768)
    outs = pl.pallas_call(
        layer_kernel,
        out_shape=given,
        in_specs=[hbm, smem] + [hbm] * 13,
        out_specs=(hbm,) * 4,
        scratch_shapes=[pltpu.VMEM(shape, kind) for _, shape, kind in SCRATCH]
        + [
            pltpu.SemaphoreType.DMA((2, SEMAPHORES)),
            pltpu.SemaphoreType.DMA((24,)),
            pltpu.SemaphoreType.REGULAR((5,)),
        ],
        compiler_params=pltpu.CompilerParams(
            collective_id=0, has_side_effects=True, vmem_limit_bytes=64 * 2**20 - 2**16
        ),
        cost_estimate=pl.CostEstimate(flops=32 * 10**9, bytes_accessed=2**24, transcendentals=2**22),
        name="layer",
    )(
        tokens.reshape(256, 1024),
        doc_starts,
        cotangent.reshape(256, 1024),
        w_query,
        key_matrix,
        value_matrix,
        w_out,
        w_gate.reshape(4, 4, 64, 768),
        w_up.reshape(4, 4, 64, 768),
        w_down,
        gain_attn.reshape(1, 1024),
        gain_mlp.reshape(1, 1024),
        gain_query.reshape(1, 128),
        gain_key.reshape(1, 128),
        frequency,
    )
    outs = pl.pallas_call(
        deliver_kernel,
        out_shape=(given[0], shaped(256, 1024)) + tuple(shaped(32, width) for width in widths) + gains,
        in_specs=[hbm] * 4,
        out_specs=(hbm,) * 13,
        scratch_shapes=[pltpu.VMEM(one.shape, one.dtype) for one in given]
        + [
            pltpu.VMEM((256, 1024), F32),
            pltpu.VMEM((2, 1, 128), F32),
            pltpu.SemaphoreType.DMA((4,)),
            pltpu.SemaphoreType.DMA((16,)),
        ],
        name="deliver",
    )(*outs)
    return (
        outs[0].reshape(1, 256, 1024),
        outs[1].reshape(1, 256, 1024),
        *outs[2:5],
        outs[5].T,
        *outs[6:8],
        outs[8].T,
        *(gain.reshape(-1) for gain in outs[9:]),
    )


def solution(mesh):
    in_specs = (
        P("dp", "tensor", None),
        P("dp", None),
        P("dp", "tensor", None),
        P(None, "tensor"),
        P(None, "tensor"),
        P(None, "tensor"),
        P("tensor", None),
        P(None, "tensor"),
        P(None, "tensor"),
        P("tensor", None),
        P(),
        P(),
        P(),
        P(),
    )
    out_specs = (
        P("dp", "tensor", None),
        P("dp", "tensor", None),
        P("dp", "tensor"),
        P("dp", "tensor"),
        P("dp", "tensor"),
        P("tensor", "dp"),
        P("dp", "tensor"),
        P("dp", "tensor"),
        P("tensor", "dp"),
        P(),
        P(),
        P(),
        P(),
    )
    return jax.shard_map(shards, mesh=mesh, in_specs=in_specs, out_specs=out_specs, check_vma=False)
```

```python
import math

import jax
import jax.numpy as jnp
import numpy as np
from jax import lax
from jax.experimental import pallas as pl
from jax.experimental.pallas import tpu as pltpu
from jax.sharding import PartitionSpec as P

MESH = pl.DeviceIdType.MESH
BF16 = jnp.bfloat16
F32 = jnp.float32
EPSILON = 1e-06
ROPE_BASE = 1000000.0
BLOCK = 256
HALF = 128
HEAD = 128
QUERY_SCALE = math.log2(math.e) / math.sqrt(HEAD)
PARTNERS = ("core", "far", "y1", "y2", "z1", "z2", "x")
DIAGONALS = (("y", 2), ("z", 2), ("tensor", "far_core"))
ORDERS = (("y1", "y2", "z1", "z2"), ("y2", "y1", "z2", "z1"), ("z1", "z2", "y1", "y2"), ("z2", "z1", "y2", "y1"))
MLP_STREAMS = (
    ("mlp_mix", 0, 640, 0, 0, 0, 1536),
    ("mlp_mix", 640, 640, 4, 0, 1, 2176),
    ("mlp_mix", 1280, 256, 8, 0, 2, 2816),
    ("t_gu", 0, 256, 8, 256, 2, 3072),
    ("t_gu", 256, 512, 12, 0, 3, 3328),
)
ATTN_STREAMS = tuple(("attn_mix", 384 * k, 384, 4 * k, 0, k, 384 * k) for k in range(4))
GAIN_ORDER = ("y", "z", "tensor", "x")

SCRATCH = (
    ("w_qkv", (1024, 1024), BF16),
    ("t_qkv", (1024, 1024), BF16),
    ("w_down", (768, 1024), BF16),
    ("t_gu", (6, 4, 64, 1024), BF16),
    ("mlp_mix", (4, 4, 64, 2304), BF16),
    ("attn_mix", (4, 4, 64, 1536), BF16),
    ("h1", (1024, 1024), BF16),
    ("h2", (1024, 1024), BF16),
    ("da", (1024, 1024), BF16),
    ("norm_qk", (768, 1024), BF16),
    ("root_qk", (8, 1024), F32),
    ("ob", (512, 1024), BF16),
    ("qs", (2, 4, 128, 512), BF16),
    ("ks_t", (256, 1024), BF16),
    ("ks", (2, 1024, 128), BF16),
    ("v_t", (2, 144, 1024), BF16),
    ("v", (2, 1024, 128), BF16),
    ("p", (20, 4, 64, 512), BF16),
    ("inv", (2, 4, 8, 512), F32),
    ("inner", (2, 4, 8, 512), F32),
    ("hidden", (768, 1024), BF16),
    ("dgu", (1536, 1024), BF16),
    ("cosine", (64, 1024), F32),
    ("sine", (64, 1024), F32),
    ("x_t", (1024, 256), BF16),
    ("resid", (1024, 256), F32),
    ("gain1", (1024, 128), F32),
    ("gain2", (1024, 128), F32),
    ("gain_q", (128, 128), F32),
    ("gain_k", (128, 128), F32),
    ("gain_sum", (1024, 128), F32),
    ("gain_q_sum", (128, 128), F32),
    ("gain_k_sum", (128, 256), F32),
    ("root1", (8, 256), F32),
    ("root2", (8, 256), F32),
    ("keep_far", (1024, 256), F32),
    ("keep_own", (1024, 256), F32),
    ("sib_out", (2, 2, 1024, 128), BF16),
    ("sib_in", (2, 2, 1024, 128), BF16),
    ("far_out", (2, 1024, 128), BF16),
    ("far_in", (2, 1024, 128), BF16),
    ("mlp_own", (1024, 256), F32),
    ("mlp_sib_out", (2, 2, 1024, 128), BF16),
    ("mlp_sib_in", (2, 2, 1024, 128), BF16),
    ("mlp_far_out", (2, 1024, 128), BF16),
    ("mlp_far_in", (2, 1024, 128), BF16),
    ("mlp_halves", (16, 4, 64, 640), BF16),
    ("sums", (32, 3840), F32),
    ("stage", (256, 1024), BF16),
    ("x_in", (256, 1024), BF16),
    ("g1_in", (1, 1024), F32),
    ("g2_in", (1, 1024), F32),
    ("gq_in", (1, 128), F32),
    ("gk_in", (1, 128), F32),
    ("frequency", (64, 128), F32),
    ("gain_own", (24, 128), F32),
    ("gain_parts", (4, 4, 24, 128), F32),
)
SEMAPHORES = 160


class Box:
    pass


class Place:
    def __init__(self):
        dp = lax.axis_index("dp")
        tensor = lax.axis_index("tensor")
        self.z, self.y, self.x = dp // 8, (dp // 2) % 4, dp % 2
        self.far, self.core = tensor // 2, tensor % 2
        self.me = tensor
        self.sib = self.far * 2 + 1 - self.core
        self.across = (1 - self.far) * 2 + self.core
        self.across_sib = (1 - self.far) * 2 + 1 - self.core

    def near(self, name):
        return step_of(name, self.y if name[0] == "y" else self.z)

    def along(self, name):
        return {"y": self.y, "z": self.z, "x": self.x, "tensor": self.me}[name]

    def device(self, name):
        z, y, x, far, core = self.z, self.y, self.x, self.far, self.core
        if isinstance(name, tuple):
            axis, steps = name
            if axis == "tensor":
                if steps == "far_core":
                    far, core = 1 - far, 1 - core
                else:
                    turned = (self.me + steps) % 4
                    far, core = turned // 2, turned % 2
            elif axis == "y":
                y = (y + steps) % 4
            elif axis == "z":
                z = (z + steps) % 4
            else:
                x = 1 - x
        elif name[0] == "y":
            y = self.near(name)
        elif name[0] == "z":
            z = self.near(name)
        elif name == "x":
            x = 1 - x
        elif name == "far":
            far = 1 - far
        else:
            core = 1 - core
        return ((z * 4 + y) * 2 + x, far * 2 + core)


def step_of(name, value):
    return value + 1 - 2 * (value % 2) if name[1] == "1" else 3 - value


def nn(left, right):
    return lax.dot_general(left, right, (((1,), (0,)), ((), ())), preferred_element_type=F32)


def nt(left, right):
    return lax.dot_general(left, right, (((1,), (1,)), ((), ())), preferred_element_type=F32)


def span(index, size=BLOCK):
    return pl.ds(pl.multiple_of(index * size, size), size)


def loop(count, body):
    def step(index, carry):
        body(index)
        return carry

    lax.fori_loop(0, count, step, 0)


def twice(values):
    return jnp.concatenate([values, values], axis=1)


def fold(values):
    return jnp.sum(values.reshape(values.shape[0] // 8, 8, values.shape[1]), axis=0)


def sub(block, part):
    return pl.ds(pl.multiple_of(block * BLOCK + part * HALF, HALF), HALF)


def lanes(part, size=128):
    return pl.ds(part * size, size)


class Links:
    def __init__(self, place, sems):
        self.place, self.sems, self.used, self.sent = place, sems, 0, []

    def send(self, src, dst, name):
        copy = pltpu.make_async_remote_copy(
            src_ref=src,
            dst_ref=dst,
            send_sem=self.sems.at[0, self.used],
            recv_sem=self.sems.at[1, self.used],
            device_id=self.place.device(name),
            device_id_type=MESH,
        )
        self.used += 1
        copy.start()
        return copy


class Gather:
    def __init__(self, links, at):
        self.links, self.at = links, at
        self.far, self.sib, self.passed = [], [], []

    def send_far(self, part):
        half = self.at(self.links.place.me, part)
        self.far.append(self.links.send(half, half, "far"))

    def send_near(self, part):
        half = self.at(self.links.place.me, part)
        self.sib.append(self.links.send(half, half, "core"))

    def send(self, part):
        self.send_far(part)
        self.send_near(part)

    def pass_on(self, part):
        self.far[part].wait_recv()
        half = self.at(self.links.place.across, part)
        self.passed.append(self.links.send(half, half, "core"))

    def near_ready(self, part):
        self.sib[part].wait_recv()

    def far_ready(self, part):
        self.passed[part].wait_recv()

    def drain(self):
        for copy in self.far + self.sib + self.passed:
            copy.wait_send()


class Reduce:
    def __init__(self, links, sib_out, sib_in, far_out, far_in):
        self.links = links
        self.sib_out, self.sib_in, self.far_out, self.far_in = sib_out, sib_in, far_out, far_in
        self.copies = {}

    def to_sibling(self, index, part):
        copy = self.links.send(self.sib_out.at[index, part], self.sib_in.at[index, part], "core")
        self.copies[index, part] = copy

    def make_far(self, keep, part):
        self.copies[0, part].wait_recv()

        def body(i):
            rows = span(i, 512)
            summed = keep[rows, lanes(part)] + self.sib_in[0, part, rows, :].astype(F32)
            self.far_out[part, rows, :] = summed.astype(BF16)

        loop(2, body)

    def send_far(self, part):
        self.copies[2, part] = self.links.send(self.far_out.at[part], self.far_in.at[part], "far")

    def arrive(self, part):
        self.copies[1, part].wait_recv()
        self.copies[2, part].wait_recv()

    def total(self, keep, part, rows):
        near = keep[rows, lanes(part)] + self.sib_in[1, part, rows, :].astype(F32)
        return near + self.far_in[part, rows, :].astype(F32)

    def release(self, index, part):
        self.copies.pop((index, part)).wait_send()

    def drain(self):
        for copy in self.copies.values():
            copy.wait_send()


class DpSum:
    def __init__(self, links, box, streams, bufs):
        self.links, self.bufs, self.out = links, bufs, box.sums
        self.streams = [(getattr(box, name), *rest) for name, *rest in streams]
        self.phase = -1
        self.flying = [[] for _ in streams]
        self.sent = []

    def spot(self, stream, slot, *rest):
        _, _, w, at, column, _, _ = self.streams[stream]
        lead = pl.ds(at + slot.start, slot.size) if isinstance(slot, pl.Slice) else at + slot
        return (lead, *rest, pl.ds(column, w))

    def held(self, stream, phase):
        every = slice(None)
        if phase == 0:
            spot = self.spot(stream, pl.ds(0, 2), every, every)
        elif phase == 1:
            spot = self.spot(stream, 2, every, every)
        elif phase == 2:
            spot = self.spot(stream, 3, pl.ds(0, 2), every)
        elif phase == 3:
            spot = self.spot(stream, 3, 2, every)
        else:
            spot = self.spot(stream, 3, 3, pl.ds(0, 32))
        return self.bufs.at[spot]

    def begin(self, stream, phase):
        place, send = self.links.place, self.links.send
        source_ref, first, w, _, _, order, _ = self.streams[stream]
        order = ORDERS[order]
        into = self.held(stream, phase)
        if phase == 4:
            theirs = self.bufs.at[self.spot(stream, 3, 2, span(1 - place.x, 32))]
            return [send(theirs, into, "x")]
        name = order[phase]
        if phase in (1, 3):
            return [send(self.held(stream, phase - 1).at[1], into, name)]
        there = place.near(name)
        copies = []
        for j, at in enumerate((there, step_of(order[phase + 1], there))):
            if phase == 2:
                source = self.held(stream, 1).at[at]
            else:
                lead = (pl.ds(0, 4), at) if name[0] == "y" else (at, slice(None))
                source = source_ref.at[(*lead, slice(None), pl.ds(first, w))]
            copies.append(send(source, into.at[j], name))
        return copies

    def finish(self, stream, phase):
        place, spot, bufs = self.links.place, self.spot, self.bufs
        source_ref, first, w, _, _, order, out_first = self.streams[stream]
        order = ORDERS[order]
        every = slice(None)
        for copy in self.flying[stream]:
            copy.wait_recv()
        if phase == 4:
            mine = bufs[spot(stream, 3, 2, span(place.x, 32))].astype(F32)
            columns = pl.ds(out_first, w)
            self.out[:, columns] = bufs[spot(stream, 3, 3, pl.ds(0, 32))].astype(F32) + mine
        elif phase == 3:
            bufs[spot(stream, 3, 2, every)] += bufs[spot(stream, 3, 0, every)]
        elif phase == 1:
            for k in range(4):
                bufs[spot(stream, 2, k, every)] += bufs[spot(stream, 0, k, every)]
        else:
            name = order[phase]
            mine = place.y if name[0] == "y" else place.z
            for j, own in enumerate((mine, step_of(order[phase + 1], mine))):
                if phase == 2:
                    bufs[spot(stream, 3, j, every)] += bufs[spot(stream, 2, own, every)]
                    continue
                for k in range(4):
                    lead = (k, own) if name[0] == "y" else (own, k)
                    kept = source_ref[(*lead, every, pl.ds(first, w))]
                    bufs[spot(stream, j, k, every)] += kept

    def start(self, *streams):
        for stream in streams:
            self.flying[stream] = self.begin(stream, 0)
        self.phase = 0

    def advance(self):
        if self.phase == 5:
            return
        for stream in range(len(self.streams)):
            self.finish(stream, self.phase)
            self.sent += self.flying[stream]
            if self.phase < 4:
                self.flying[stream] = self.begin(stream, self.phase + 1)
        self.phase += 1

    def complete(self):
        while self.phase < 5:
            self.advance()

    def drain(self):
        for copy in self.sent:
            copy.wait_send()


class GainSum:
    def __init__(self, links, own, parts):
        self.links, self.parts, self.copies, self.step = links, parts, [], 0
        self.begin(own[...])

    def begin(self, values):
        place, name = self.links.place, GAIN_ORDER[self.step]
        mine = place.along(name)
        half = self.parts.at[self.step, mine]
        self.parts[self.step, mine] = values
        count = 2 if name == "x" else 4
        self.copies.append([self.links.send(half, half, (name, k)) for k in range(1, count)])

    def advance(self):
        if self.step == 4:
            return
        for copy in self.copies[self.step]:
            copy.wait_recv()
        parts = [self.parts[self.step, k] for k in range(len(self.copies[self.step]) + 1)]
        total = parts[0] + parts[1]
        if len(parts) == 4:
            total = total + (parts[2] + parts[3])
        self.step += 1
        if self.step < 4:
            self.begin(total)
        else:
            self.total = total

    def drain(self):
        for copies in self.copies:
            for copy in copies:
                copy.wait_send()


def head_forward(raw, gain, cosine, sine):
    root = lax.rsqrt(jnp.mean(raw * raw, axis=0, keepdims=True) + EPSILON)
    normed = raw * root
    scaled = normed * gain
    first, second = scaled[:64], scaled[64:]
    turned = jnp.concatenate([first * cosine - second * sine, second * cosine + first * sine], axis=0)
    return normed, root, turned


def head_backward(grad, normed, root, gain, cosine, sine):
    first, second = grad[:64], grad[64:]
    turned = jnp.concatenate([first * cosine + second * sine, second * cosine - first * sine], axis=0)
    scaled = turned * gain
    inner = jnp.mean(scaled * normed, axis=0, keepdims=True)
    return root * (scaled - normed * inner), turned * normed


def layer_kernel(
    x, starts, dy, wq, wk, wv, wo, wg, wu, wd, g1, g2, gq, gk, frequency,
    out, grad_x, out_sums, out_gains,
    *scratch,
):
    s = Box()
    for (name, _, _), ref in zip(SCRATCH, scratch):
        setattr(s, name, ref)
    link_sems, load_sems, ready = scratch[len(SCRATCH) :]
    place = Place()
    links = Links(place, link_sems)
    me, sib, across, across_sib = place.me, place.sib, place.across, place.across_sib

    barrier = pltpu.get_barrier_semaphore()
    for name in PARTNERS + DIAGONALS:
        pl.semaphore_signal(barrier, inc=1, device_id=place.device(name), device_id_type=MESH)

    loads = []

    def load(src, dst):
        copy = pltpu.make_async_copy(src, dst, load_sems.at[len(loads)])
        copy.start()
        loads.append(copy)

    load(x, s.x_in)
    load(g1, s.g1_in)
    for g in range(2):
        load(wq.at[:, pl.ds(256 * g, 256)], s.w_qkv.at[:, pl.ds(512 * g, 256)])
        load(wk.at[:, pl.ds(128 * g, 128)], s.w_qkv.at[:, pl.ds(512 * g + 256, 128)])
        load(wv.at[:, pl.ds(128 * g, 128)], s.w_qkv.at[:, pl.ds(512 * g + 384, 128)])
    load(wo, s.h2.at[pl.ds(0, 512)])
    load(wg, s.mlp_mix.at[:, :, :, pl.ds(0, 768)])
    load(wu, s.mlp_mix.at[:, :, :, pl.ds(768, 768)])
    load(wd, s.w_down)
    load(dy, s.da.at[pl.ds(0, 256)])
    load(g2, s.g2_in)
    load(gq, s.gq_in)
    load(gk, s.gk_in)
    load(frequency, s.frequency)

    near_pair, far_pair = (sib, me), (across_sib, across)

    def pair(ref, rows, blocks, part):
        return jnp.concatenate([ref[rows, sub(b, part)] for b in blocks], axis=1)

    def unpair(ref, rows, blocks, part, values):
        for n, b in enumerate(blocks):
            ref[rows, sub(b, part)] = values[:, HALF * n : HALF * n + HALF]

    every = pl.ds(0, 1024)

    loads[0].wait()
    loads[1].wait()
    gather_h1 = Gather(links, lambda b, part: s.h1.at[:, sub(b, part)])
    for part in range(2):

        def first_norm(i, part=part):
            rows = span(2 * part + i, 64)
            xs = s.x_in[rows, :].astype(F32)
            root = lax.rsqrt(jnp.mean(xs * xs, axis=1, keepdims=True) + EPSILON)
            s.stage[rows, :] = (xs * root * s.g1_in[...]).astype(BF16)

        loop(2, first_norm)
        for j in range(4):
            s.h1[pl.ds(256 * j, 256), sub(me, part)] = s.stage[lanes(part), pl.ds(256 * j, 256)].T
        if part == 0:
            pl.semaphore_wait(barrier, len(PARTNERS) + len(DIAGONALS))
        gather_h1.send(part)

    for k in range(2, 8):
        loads[k].wait()

    def turn_qkv(i):
        s.t_qkv[span(i), :] = s.w_qkv[:, span(i)].T

    loop(4, turn_qkv)

    for k in range(13, 17):
        loads[k].wait()
    place_row = lax.broadcasted_iota(jnp.int32, (8, 1024), 1)
    start_row = jnp.zeros((8, 1024), jnp.int32)
    for d in range(4):
        start_row = jnp.maximum(start_row, jnp.where(place_row >= starts[0, d], starts[0, d], 0))
    position = (place_row - start_row).astype(F32)
    for i in range(8):
        columns = pl.ds(128 * i, 128)
        angle = s.frequency[...] * position[0:1, 128 * i : 128 * i + 128]
        s.cosine[:, columns] = jnp.cos(angle)
        s.sine[:, columns] = jnp.sin(angle)
    for qb in range(4):
        first = start_row[0:1, qb * 256 : qb * 256 + 256]
        query = lax.broadcasted_iota(jnp.int32, (256, 256), 1) + qb * 256
        for kb in range(qb + 1):
            key = lax.broadcasted_iota(jnp.int32, (256, 256), 0) + kb * 256
            allowed = (key <= query) & (key >= first)
            s.dgu[pl.ds(256 * kb, 256), pl.ds(256 * qb, 256)] = jnp.where(allowed, 1.0, 0.0).astype(BF16)

    s.gain1[...] = jnp.broadcast_to(s.g1_in[...], (128, 1024)).T
    s.gain2[...] = jnp.broadcast_to(s.g2_in[...], (128, 1024)).T
    s.gain_q[...] = jnp.broadcast_to(s.gq_in[...], (128, 128)).T
    s.gain_k[...] = jnp.broadcast_to(s.gk_in[...], (128, 128)).T
    s.gain_q_sum[...] = jnp.zeros((128, 128), F32)
    s.gain_sum[...] = jnp.zeros((1024, 128), F32)
    s.gain_k_sum[...] = jnp.zeros((128, 256), F32)
    for g in range(2):
        s.v_t[g, pl.ds(128, 16), :] = jnp.ones((16, 1024), BF16)

    def x_in(i, total):
        turned = s.x_in[:, span(i)].astype(F32).T
        s.x_t[span(i), :] = turned.astype(BF16)
        return total + fold(turned * turned)

    square = lax.fori_loop(0, 4, x_in, jnp.zeros((8, BLOCK), F32))
    root = lax.rsqrt(jnp.sum(square, axis=0, keepdims=True) / 1024.0 + EPSILON)
    s.root1[...] = jnp.broadcast_to(root, (8, BLOCK))

    loads[8].wait()

    def turn_out(i):
        s.attn_mix[i, :, :, pl.ds(1024, 512)] = s.h2[pl.ds(0, 512), span(i)].T.reshape(4, 64, 512)

    loop(4, turn_out)
    loads[9].wait()
    loads[10].wait()

    def turn_gu(i):
        for z in range(4):
            turned = s.mlp_mix[z, :, :, span(i)].reshape(256, 256).T
            s.t_gu[i, :, :, pl.ds(256 * z, 256)] = turned.reshape(4, 64, 256)

    loop(6, turn_gu)
    loads[11].wait()

    def turn_down(i):
        s.mlp_mix[i, :, :, pl.ds(1536, 768)] = s.w_down[:, span(i)].T.reshape(4, 64, 768)

    loop(4, turn_down)

    def dy_in(i):
        s.attn_mix[i, :, :, span(me)] = s.da[pl.ds(0, 256), span(i)].T.reshape(4, 64, BLOCK)

    loads[12].wait()
    loop(4, dy_in)

    def project(blocks, part):
        cosine, sine = pair(s.cosine, pl.ds(0, 64), blocks, part), pair(s.sine, pl.ds(0, 64), blocks, part)
        query_gain = twice(s.gain_q[...] * QUERY_SCALE)
        key_gain = twice(s.gain_k[...])
        every_raw = nn(s.t_qkv[...], pair(s.h1, every, blocks, part))
        for g in range(2):
            raw = every_raw[512 * g : 512 * g + 512]
            for k in range(2):
                head = 3 * g + k
                normed, root, turned = head_forward(raw[128 * k : 128 * k + 128], query_gain, cosine, sine)
                unpair(s.norm_qk, pl.ds(128 * head, 128), blocks, part, normed.astype(BF16))
                unpair(s.root_qk, pl.ds(head, 1), blocks, part, root)
                turned = turned.astype(BF16)
                for n, b in enumerate(blocks):
                    s.qs[g, b, :, pl.ds(256 * part + 128 * k, 128)] = turned[:, HALF * n : HALF * n + HALF]
            normed, root, turned = head_forward(raw[256:384], key_gain, cosine, sine)
            turned, values = turned.astype(BF16), raw[384:].astype(BF16)
            unpair(s.norm_qk, pl.ds(384 * g + 256, 128), blocks, part, normed.astype(BF16))
            unpair(s.root_qk, pl.ds(3 * g + 2, 1), blocks, part, root)
            unpair(s.ks_t, pl.ds(128 * g, 128), blocks, part, turned)
            for n, b in enumerate(blocks):
                s.v_t[g, pl.ds(0, 128), sub(b, part)] = values[:, HALF * n : HALF * n + HALF]
                s.ks[g, sub(b, part), :] = turned[:, HALF * n : HALF * n + HALF].T
                s.v[g, sub(b, part), :] = values[:, HALF * n : HALF * n + HALF].T

    def both_roles(own, body):
        for far in range(2):
            blocks = (2 * far, 2 * far + 1) if own else (2 - 2 * far, 3 - 2 * far)
            pl.when(place.far == far)(lambda blocks=blocks: body(blocks))

    def p_slots(g, qb):
        return pl.ds(g * 10 + qb * (qb + 1) // 2, qb + 1)

    def attend(blocks, parts):
        first, wide = 256 * parts[0], 256 * len(parts)
        cut = pl.ds(first, wide)
        chains = [(qb, g, 256 * (qb + 1)) for qb in blocks for g in range(2)]
        scores = [nn(s.ks[g, pl.ds(0, keys), :], s.qs[g, qb, :, cut]) for qb, g, keys in chains]
        weights = []
        for (qb, g, keys), score in zip(chains, scores):
            halves = [twice(s.dgu[pl.ds(0, keys), pl.ds(256 * qb + HALF * part, HALF)]) for part in parts]
            mask = halves[0] if len(parts) == 1 else jnp.concatenate(halves, axis=1)
            weights.append(jnp.exp2(score).astype(BF16) * mask)
        products = [nn(s.v_t[g, :, pl.ds(0, keys)], weight) for (qb, g, keys), weight in zip(chains, weights)]
        for (qb, g, keys), weight, product in zip(chains, weights, products):
            s.p[p_slots(g, qb), :, :, cut] = weight.reshape(qb + 1, 4, 64, wide)
            inverse = 1.0 / product[128:136]
            s.inv[g, qb, :, cut] = inverse
            attended = (product[:128] * inverse[0:1]).astype(BF16)
            for n, part in enumerate(parts):
                for k in range(2):
                    columns = slice(256 * n + 128 * k, 256 * n + 128 * k + 128)
                    s.ob[pl.ds(256 * g + 128 * k, 128), pl.ds(256 * qb + HALF * part, HALF)] = attended[:, columns]

    def out_product(blocks, part, store):
        attended = pair(s.ob, pl.ds(0, 512), blocks, part)
        store(nn(s.attn_mix[:, :, :, pl.ds(1024, 512)].reshape(1024, 512), attended))

    def split(sib_out, index, part, keep):
        def store(values):
            sib_out[index, part] = values[:, :HALF].astype(BF16)
            keep[:, lanes(part)] = values[:, HALF:]

        return store

    for part in range(2):
        gather_h1.near_ready(part)
        project(near_pair, part)
    gather_h1.pass_on(0)
    gather_h1.far_ready(0)
    project(far_pair, 0)
    gather_h1.pass_on(1)
    gather_dy = Gather(links, lambda b, part: s.attn_mix.at[:, :, :, sub(b, part)])
    for part in range(2):
        gather_dy.send_near(part)
    gather_dy.send_far(0)
    gather_h1.far_ready(1)
    project(far_pair, 1)

    sum_attn = Reduce(links, s.sib_out, s.sib_in, s.far_out, s.far_in)
    for part in range(2):
        both_roles(False, lambda blocks, part=part: attend(blocks, (part,)))
        if part == 1:
            sum_attn.make_far(s.keep_far, 0)
            sum_attn.send_far(0)
        out_product(far_pair, part, split(s.sib_out, 0, part, s.keep_far))
        sum_attn.to_sibling(0, part)
    both_roles(True, lambda blocks: attend(blocks, (0, 1)))
    sum_attn.make_far(s.keep_far, 1)
    sum_attn.send_far(1)
    for part in range(2):
        out_product(near_pair, part, split(s.sib_out, 1, part, s.keep_own))
        sum_attn.to_sibling(1, part)
    for part in range(2):
        gather_dy.near_ready(part)
    gather_dy.pass_on(0)

    gather_h2 = Gather(links, lambda b, part: s.h2.at[:, sub(b, part)])

    def second_norm(part):
        sum_attn.arrive(part)

        def square(i, total):
            x1 = s.x_t[span(i), lanes(part)].astype(F32) + sum_attn.total(s.keep_own, part, span(i))
            s.resid[span(i), lanes(part)] = x1
            return total + fold(x1 * x1)

        total = lax.fori_loop(0, 4, square, jnp.zeros((8, HALF), F32))
        root = lax.rsqrt(jnp.sum(total, axis=0, keepdims=True) / 1024.0 + EPSILON)
        s.root2[:, lanes(part)] = jnp.broadcast_to(root, (8, HALF))

        def scale(i):
            normed = s.resid[span(i), lanes(part)] * s.root2[0:1, lanes(part)]
            s.h2[span(i), sub(me, part)] = (normed * s.gain2[span(i), :]).astype(BF16)

        loop(4, scale)
        gather_h2.send(part)

    def feed(blocks, part):
        def body(j):
            gate = nn(s.t_gu[j].reshape(256, 1024), pair(s.h2, every, blocks, part))
            up = nn(s.t_gu[3 + j].reshape(256, 1024), pair(s.h2, every, blocks, part))
            grads = [s.attn_mix[:, :, :, sub(b, part)].reshape(1024, HALF) for b in blocks]
            grad = nn(s.w_down[span(j), :], jnp.concatenate(grads, axis=1))
            open_gate = jax.nn.sigmoid(gate)
            silu = gate * open_gate
            unpair(s.hidden, span(j), blocks, part, (silu * up).astype(BF16))
            dgate = (grad * up * open_gate * (1.0 + gate * (1.0 - open_gate))).astype(BF16)
            unpair(s.dgu, span(j), blocks, part, dgate)
            unpair(s.dgu, span(3 + j), blocks, part, (grad * silu).astype(BF16))

        for j in range(3):
            body(j)

    def feed_back(blocks, part, store):
        grads = pair(s.dgu, pl.ds(0, 1536), blocks, part)
        store(nn(s.mlp_mix[:, :, :, pl.ds(0, 1536)].reshape(1024, 1536), grads))

    def mlp_product(blocks, part, store):
        hidden = pair(s.hidden, pl.ds(0, 768), blocks, part)
        store(nn(s.mlp_mix[:, :, :, pl.ds(1536, 768)].reshape(1024, 768), hidden))

    sum_dh2 = Reduce(links, s.sib_out, s.sib_in, s.far_out, s.far_in)

    def feed_near(part):
        gather_h2.near_ready(part)
        feed(near_pair, part)
        feed_back(near_pair, part, split(s.sib_out, 1, part, s.keep_own))
        sum_dh2.to_sibling(1, part)

    second_norm(0)
    sum_attn.release(1, 0)
    feed_near(0)
    second_norm(1)
    sum_attn.drain()
    gather_h2.pass_on(0)
    feed_near(1)
    gather_dy.send_far(1)
    gather_dy.far_ready(0)
    gather_h2.far_ready(0)
    feed(far_pair, 0)
    feed_back(far_pair, 0, split(s.sib_out, 0, 0, s.keep_far))
    sum_dh2.to_sibling(0, 0)
    sum_dh2.make_far(s.keep_far, 0)
    sum_dh2.send_far(0)
    gather_h2.pass_on(1)
    gather_dy.pass_on(1)
    gather_h2.far_ready(1)
    gather_dy.far_ready(1)
    feed(far_pair, 1)
    feed_back(far_pair, 1, split(s.sib_out, 0, 1, s.keep_far))
    sum_dh2.to_sibling(0, 1)

    dp_mlp = DpSum(links, s, MLP_STREAMS, s.mlp_halves)

    def feed_grad(stream):
        name, first, w, _, _, _, _ = MLP_STREAMS[stream]
        if name == "mlp_mix":
            values = nt(s.h2[...], s.dgu[pl.ds(first, w), :])
        else:
            values = nt(s.attn_mix[:, :, :, pl.ds(0, 1024)].reshape(1024, 1024), s.hidden[pl.ds(first, w), :])
        into = getattr(s, name)
        into[pl.ds(0, 4), :, :, pl.ds(first, w)] = values.astype(BF16).reshape(4, 4, 64, w)
        dp_mlp.start(stream)

    gather_da = Gather(links, lambda b, part: s.da.at[:, sub(b, part)])

    def norm_back(part):
        sum_dh2.arrive(part)

        def inner_sum(i, total):
            grad = sum_dh2.total(s.keep_own, part, span(i))
            s.keep_own[span(i), lanes(part)] = grad
            product = grad * (s.resid[span(i), lanes(part)] * s.root2[0:1, lanes(part)])
            s.gain_sum[span(i), :] += product
            return total + fold(product * s.gain2[span(i), :])

        inner = lax.fori_loop(0, 4, inner_sum, jnp.zeros((8, HALF), F32))
        inner = jnp.sum(inner, axis=0, keepdims=True) / 1024.0

        def body(i):
            root = s.root2[0:1, lanes(part)]
            scaled = s.keep_own[span(i), lanes(part)] * s.gain2[span(i), :]
            normed = s.resid[span(i), lanes(part)] * root
            own = s.attn_mix[i, :, :, sub(me, part)].reshape(256, HALF).astype(F32)
            s.da[span(i), sub(me, part)] = (own + root * (scaled - normed * inner)).astype(BF16)
            s.mlp_own[span(i), lanes(part)] = s.resid[span(i), lanes(part)]
            s.resid[span(i), lanes(part)] = own + root * (scaled - normed * inner)

        loop(4, body)
        gather_da.send(part)

    feed_grad(0)
    sum_dh2.make_far(s.keep_far, 1)
    sum_dh2.send_far(1)
    feed_grad(1)
    norm_back(0)
    feed_grad(4)
    feed_grad(2)
    feed_grad(3)
    gather_h2.drain()
    load(wo, s.h2.at[pl.ds(0, 512)])
    norm_back(1)
    sum_dh2.drain()

    def put_gain(first, row):
        for k in range(row.shape[1] // 128):
            s.gain_own[first + k : first + k + 1, :] = row[:, 128 * k : 128 * k + 128]

    put_gain(8, jnp.sum(s.gain_sum[...].T, axis=0, keepdims=True))
    s.gain_sum[...] = jnp.zeros((1024, 128), F32)

    sum_mlp = Reduce(links, s.mlp_sib_out, s.mlp_sib_in, s.mlp_far_out, s.mlp_far_in)

    def mlp_mine(part):
        def store(values):
            s.mlp_sib_out[1, part] = values[:, :HALF].astype(BF16)
            s.mlp_own[:, lanes(part)] += values[:, HALF:]

        return store

    for part in range(2):
        mlp_product(far_pair, part, split(s.mlp_sib_out, 0, part, s.keep_far))
        sum_mlp.to_sibling(0, part)
    for part in range(2):
        sum_mlp.make_far(s.keep_far, part)

    s.keep_own[...] = jnp.zeros((1024, 256), F32)
    s.keep_far[...] = jnp.zeros((1024, 256), F32)
    loads[17].wait()

    def dob(g, b, part):
        index = g * 4 + b
        return (4 + index // 4, pl.ds(2 * ((index // 2) % 2), 2), slice(None), pl.ds(pl.multiple_of((index % 2) * 512 + part * 256, 256), 256))

    def out_back(blocks, part):
        two = lanes(part, 256)
        every_grad = nn(s.h2[pl.ds(0, 512), :], pair(s.da, every, blocks, part))
        for g in range(2):
            grads = every_grad[256 * g : 256 * g + 256]
            for n, b in enumerate(blocks):
                columns = slice(HALF * n, HALF * n + HALF)
                both = jnp.concatenate([grads[:128, columns], grads[128:, columns]], axis=1) * s.inv[g, b, 0:1, two]
                outs = [s.ob[pl.ds(256 * g + 128 * k, 128), sub(b, part)] for k in range(2)]
                inner = jnp.sum(both * jnp.concatenate(outs, axis=1).astype(F32), axis=0, keepdims=True)
                s.inner[g, b, :, two] = jnp.broadcast_to(inner, (8, 256))
                s.t_gu[dob(g, b, part)] = both.astype(BF16).reshape(2, 64, 256)

    def attend_back(blocks, parts, groups):
        first, wide = 256 * parts[0], 256 * len(parts)
        cut = pl.ds(first, wide)
        chains = [(qb, g, 256 * (qb + 1)) for qb in blocks for g in groups]
        grads, weights, slopes, changes, key_parts, query_parts, value_parts = [], [], [], [], [], [], []
        for qb, g, keys in chains:
            index = g * 4 + qb
            at = (4 + index // 4, pl.ds(2 * ((index // 2) % 2), 2), slice(None), pl.ds((index % 2) * 512 + first, wide))
            grads.append(s.t_gu[at].reshape(128, wide))
            weights.append(s.p[p_slots(g, qb), :, :, cut].reshape(keys, wide))
        for (qb, g, keys), grad in zip(chains, grads):
            slopes.append(nn(s.v[g, pl.ds(0, keys), :], grad))
        for weight, grad in zip(weights, grads):
            value_parts.append(nt(weight, grad))
        for (qb, g, keys), weight, slope in zip(chains, weights, slopes):
            changes.append((weight.astype(F32) * (slope - s.inner[g, qb, 0:1, cut])).astype(BF16))
        for (qb, g, keys), change in zip(chains, changes):
            key_parts.append(nt(change, s.qs[g, qb, :, cut]))
            query_parts.append(nn(s.ks_t[pl.ds(128 * g, 128), pl.ds(0, keys)], change))
        for (qb, g, keys), value_part, key_part, query_part in zip(chains, value_parts, key_parts, query_parts):
            s.keep_own[pl.ds(0, keys), lanes(g)] += value_part
            s.keep_far[pl.ds(0, keys), lanes(g)] += key_part
            for n, part in enumerate(parts):
                columns = pl.ds(256 * qb + HALF * part, HALF)
                for k in range(2):
                    head = 3 * g + k
                    grad, gain_part = head_backward(
                        query_part[:, 256 * n + 128 * k : 256 * n + 128 * k + 128] * (1.0 / math.sqrt(HEAD)),
                        s.norm_qk[pl.ds(128 * head, 128), columns].astype(F32),
                        s.root_qk[pl.ds(head, 1), columns],
                        s.gain_q[...],
                        s.cosine[:, columns],
                        s.sine[:, columns],
                    )
                    s.t_qkv[pl.ds(512 * g + 128 * k, 128), columns] = grad.astype(BF16)
                    s.gain_q_sum[...] += gain_part

    def key_back(g):
        gain = twice(s.gain_k[...])

        def body(b):
            columns = span(b)
            grad, gain_part = head_backward(
                s.keep_far[columns, lanes(g)].T * math.log(2.0),
                s.norm_qk[pl.ds(384 * g + 256, 128), columns].astype(F32),
                s.root_qk[pl.ds(3 * g + 2, 1), columns],
                gain,
                s.cosine[:, columns],
                s.sine[:, columns],
            )
            s.t_qkv[pl.ds(512 * g + 256, 128), columns] = grad.astype(BF16)
            s.gain_k_sum[...] += gain_part
            s.t_qkv[pl.ds(512 * g + 384, 128), columns] = s.keep_own[columns, lanes(g)].T.astype(BF16)

        loop(4, body)

    def tell_ready():
        for k, name in enumerate(PARTNERS[2:]):
            pl.semaphore_signal(ready.at[k], inc=1, device_id=place.device(name), device_id_type=MESH)

    def wait_ready():
        for k in range(5):
            pl.semaphore_wait(ready.at[k], 1)

    def qkv_grad(g):
        values = nt(s.h1[...], s.t_qkv[pl.ds(512 * g, 512), :]).astype(BF16)
        s.attn_mix[:, :, :, pl.ds(512 * g, 512)] = values.reshape(4, 4, 64, 512)

    def out_grad():
        values = nt(s.da[...], s.ob[...]).astype(BF16)
        s.attn_mix[:, :, :, pl.ds(1024, 512)] = values.reshape(4, 4, 64, 512)

    for part in range(2):
        gather_da.near_ready(part)
        out_back(near_pair, part)
    gather_da.pass_on(0)
    both_roles(True, lambda blocks: attend_back(blocks, (0, 1), (0, 1)))
    gather_da.far_ready(0)
    out_back(far_pair, 0)
    gather_da.pass_on(1)
    sum_mlp.send_far(0)
    both_roles(False, lambda blocks: attend_back(blocks, (0,), (0, 1)))
    gather_da.far_ready(1)
    out_back(far_pair, 1)
    gather_dy.drain()
    dp_mlp.advance()
    both_roles(False, lambda blocks: attend_back(blocks, (1,), (0, 1)))
    tell_ready()
    for g in range(2):
        key_back(g)
    out_grad()
    for g in range(2):
        qkv_grad(g)
    wait_ready()
    dp_attn = DpSum(links, s, ATTN_STREAMS, s.p)
    dp_attn.start(0, 1, 2, 3)

    def in_back(blocks, part, store):
        values = nn(s.w_qkv[...], pair(s.t_qkv, every, blocks, part))
        product = values * pair(s.h1, every, blocks, part).astype(F32)
        s.gain_sum[...] += product[:, :HALF] + product[:, HALF:]
        store(values)

    sum_dh1 = Reduce(links, s.sib_out, s.sib_in, s.far_out, s.far_in)
    for part in range(2):
        in_back(far_pair, part, split(s.sib_out, 0, part, s.keep_far))
        sum_dh1.to_sibling(0, part)
    for part in range(2):
        sum_dh1.make_far(s.keep_far, part)
        sum_dh1.send_far(part)
    sum_mlp.send_far(1)
    dp_mlp.advance()
    for part in range(2):
        in_back(near_pair, part, split(s.sib_out, 1, part, s.keep_own))
        sum_dh1.to_sibling(1, part)
    for part in range(2):
        mlp_product(near_pair, part, mlp_mine(part))
        sum_mlp.to_sibling(1, part)
    put_gain(0, jnp.sum((s.gain_sum[...] / s.gain1[...]).T, axis=0, keepdims=True))
    both = s.gain_k_sum[:, lanes(0)] + s.gain_k_sum[:, lanes(1)]
    put_gain(16, jnp.sum(s.gain_q_sum[...].T, axis=0, keepdims=True))
    put_gain(17, jnp.sum(both.T, axis=0, keepdims=True))
    s.gain_own[pl.ds(18, 6), :] = jnp.zeros((6, 128), F32)
    gains = GainSum(links, s.gain_own, s.gain_parts)
    dp_attn.advance()
    dp_mlp.advance()
    gains.advance()
    dp_attn.advance()
    dp_mlp.advance()
    gains.advance()

    for part in range(2):
        sum_dh1.arrive(part)

        def inner_sum(i, total, part=part):
            grad = sum_dh1.total(s.keep_own, part, span(i))
            s.keep_own[span(i), lanes(part)] = grad
            normed = s.x_t[span(i), lanes(part)].astype(F32) * s.root1[0:1, lanes(part)]
            return total + fold(grad * normed * s.gain1[span(i), :])

        inner = lax.fori_loop(0, 4, inner_sum, jnp.zeros((8, HALF), F32))
        inner = jnp.sum(inner, axis=0, keepdims=True) / 1024.0

        def last_back(i, part=part, inner=inner):
            root = s.root1[0:1, lanes(part)]
            scaled = s.keep_own[span(i), lanes(part)] * s.gain1[span(i), :]
            normed = s.x_t[span(i), lanes(part)].astype(F32) * root
            s.resid[span(i), lanes(part)] += root * (scaled - normed * inner)

        loop(4, last_back)
        if part == 0:
            dp_attn.advance()
            gains.advance()
    load(s.resid, grad_x)

    for part in range(2):
        sum_mlp.arrive(part)

        def layer_out(i, part=part):
            s.stage[lanes(part), span(i)] = sum_mlp.total(s.mlp_own, part, span(i)).T.astype(BF16)

        loop(4, layer_out)
    load(s.stage, out)
    while dp_attn.phase < 5 or dp_mlp.phase < 5 or gains.step < 4:
        dp_attn.advance()
        gains.advance()
        dp_mlp.advance()
    load(s.sums, out_sums)
    s.gain_own[...] = gains.total
    load(s.gain_own, out_gains)

    for copy in loads[18:]:
        copy.wait()
    for exchange in (gather_h1, gather_da, sum_mlp, sum_dh1, dp_mlp, dp_attn, gains):
        exchange.drain()


def deliver_kernel(*refs):
    given, outs, held = refs[:4], refs[4:17], refs[17:21]
    turned, gain_rows, sems_in, sems_out = refs[21:]
    arrivals = [pltpu.make_async_copy(a, b, sems_in.at[k]) for k, (a, b) in enumerate(zip(given, held))]
    for copy in arrivals:
        copy.start()
    started = []

    def send(src, dst):
        copy = pltpu.make_async_copy(src, dst, sems_out.at[len(started)])
        copy.start()
        started.append(copy)

    arrivals[3].wait()
    gain_rows[0] = held[3][16:17]
    gain_rows[1] = held[3][17:18]
    send(held[3].at[pl.ds(0, 8)], outs[9])
    send(held[3].at[pl.ds(8, 8)], outs[10])
    send(gain_rows.at[0], outs[11])
    send(gain_rows.at[1], outs[12])
    arrivals[2].wait()
    sums = held[2]
    for g in range(2):
        for out, first, width in ((outs[2], 0, 256), (outs[3], 256, 128), (outs[4], 384, 128)):
            send(sums.at[:, pl.ds(512 * g + first, width)], out.at[:, pl.ds(width * g, width)])
    for out, first, width in ((outs[5], 1024, 512), (outs[6], 1536, 768), (outs[7], 2304, 768), (outs[8], 3072, 768)):
        send(sums.at[:, pl.ds(first, width)], out)
    arrivals[0].wait()
    send(held[0], outs[0])
    arrivals[1].wait()
    for i in range(4):
        turned[:, pl.ds(256 * i, 256)] = held[1][pl.ds(256 * i, 256), :].T
    send(turned, outs[1])
    for copy in started:
        copy.wait()


def shards(
    tokens,
    doc_starts,
    cotangent,
    w_query,
    key_matrix,
    value_matrix,
    w_out,
    w_gate,
    w_up,
    w_down,
    gain_attn,
    gain_mlp,
    gain_query,
    gain_key,
):
    frequency = ROPE_BASE ** (-(np.arange(64, dtype=np.float64) * 2.0) / HEAD)
    frequency = jnp.asarray(np.broadcast_to(frequency[:, None], (64, 128)).astype(np.float32))
    hbm = pl.BlockSpec(memory_space=pl.ANY)
    smem = pl.BlockSpec(memory_space=pltpu.SMEM)

    def shaped(*shape, kind=F32):
        return jax.ShapeDtypeStruct(shape, kind)

    gains = (shaped(8, 128), shaped(8, 128), shaped(1, 128), shaped(1, 128))
    given = (shaped(256, 1024, kind=BF16), shaped(1024, 256), shaped(32, 3840), shaped(24, 128))
    widths = (512, 256, 256, 512, 768, 768, 768)
    outs = pl.pallas_call(
        layer_kernel,
        out_shape=given,
        in_specs=[hbm, smem] + [hbm] * 13,
        out_specs=(hbm,) * 4,
        scratch_shapes=[pltpu.VMEM(shape, kind) for _, shape, kind in SCRATCH]
        + [
            pltpu.SemaphoreType.DMA((2, SEMAPHORES)),
            pltpu.SemaphoreType.DMA((24,)),
            pltpu.SemaphoreType.REGULAR((5,)),
        ],
        compiler_params=pltpu.CompilerParams(
            collective_id=0, has_side_effects=True, vmem_limit_bytes=64 * 2**20 - 2**16
        ),
        cost_estimate=pl.CostEstimate(flops=32 * 10**9, bytes_accessed=2**24, transcendentals=2**22),
        name="layer",
    )(
        tokens.reshape(256, 1024),
        doc_starts,
        cotangent.reshape(256, 1024),
        w_query,
        key_matrix,
        value_matrix,
        w_out,
        w_gate.reshape(4, 4, 64, 768),
        w_up.reshape(4, 4, 64, 768),
        w_down,
        gain_attn.reshape(1, 1024),
        gain_mlp.reshape(1, 1024),
        gain_query.reshape(1, 128),
        gain_key.reshape(1, 128),
        frequency,
    )
    outs = pl.pallas_call(
        deliver_kernel,
        out_shape=(given[0], shaped(256, 1024)) + tuple(shaped(32, width) for width in widths) + gains,
        in_specs=[hbm] * 4,
        out_specs=(hbm,) * 13,
        scratch_shapes=[pltpu.VMEM(one.shape, one.dtype) for one in given]
        + [
            pltpu.VMEM((256, 1024), F32),
            pltpu.VMEM((2, 1, 128), F32),
            pltpu.SemaphoreType.DMA((4,)),
            pltpu.SemaphoreType.DMA((16,)),
        ],
        name="deliver",
    )(*outs)
    return (
        outs[0].reshape(1, 256, 1024),
        outs[1].reshape(1, 256, 1024),
        *outs[2:5],
        outs[5].T,
        *outs[6:8],
        outs[8].T,
        *(gain.reshape(-1) for gain in outs[9:]),
    )


def solution(mesh):
    in_specs = (
        P("dp", "tensor", None),
        P("dp", None),
        P("dp", "tensor", None),
        P(None, "tensor"),
        P(None, "tensor"),
        P(None, "tensor"),
        P("tensor", None),
        P(None, "tensor"),
        P(None, "tensor"),
        P("tensor", None),
        P(),
        P(),
        P(),
        P(),
    )
    out_specs = (
        P("dp", "tensor", None),
        P("dp", "tensor", None),
        P("dp", "tensor"),
        P("dp", "tensor"),
        P("dp", "tensor"),
        P("tensor", "dp"),
        P("dp", "tensor"),
        P("dp", "tensor"),
        P("tensor", "dp"),
        P(),
        P(),
        P(),
        P(),
    )
    return jax.shard_map(shards, mesh=mesh, in_specs=in_specs, out_specs=out_specs, check_vma=False)
```

```python
import math

import jax
import jax.numpy as jnp
import numpy as np
from jax import lax
from jax.experimental import pallas as pl
from jax.experimental.pallas import tpu as pltpu
from jax.sharding import PartitionSpec as P

MESH = pl.DeviceIdType.MESH
BF16 = jnp.bfloat16
F32 = jnp.float32
EPSILON = 1e-06
ROPE_BASE = 1000000.0
BLOCK = 256
HALF = 128
HEAD = 128
QUERY_SCALE = math.log2(math.e) / math.sqrt(HEAD)
PARTNERS = ("core", "far", "y1", "y2", "z1", "z2", "x")
DIAGONALS = (("y", 2), ("z", 2), ("tensor", "far_core"))
ORDERS = (("y1", "y2", "z1", "z2"), ("y2", "y1", "z2", "z1"), ("z1", "z2", "y1", "y2"), ("z2", "z1", "y2", "y1"))
MLP_STREAMS = (
    ("mlp_mix", 0, 640, 0, 0, 0, 1536),
    ("mlp_mix", 640, 640, 4, 0, 1, 2176),
    ("mlp_mix", 1280, 256, 8, 0, 2, 2816),
    ("t_gu", 0, 256, 8, 256, 2, 3072),
    ("t_gu", 256, 512, 12, 0, 3, 3328),
)
ATTN_STREAMS = tuple(("attn_mix", 384 * k, 384, 4 * k, 0, k, 384 * k) for k in range(4))
GAIN_ORDER = ("y", "z", "tensor", "x")

SCRATCH = (
    ("w_qkv", (1024, 1024), BF16),
    ("t_qkv", (1024, 1024), BF16),
    ("w_down", (768, 1024), BF16),
    ("t_gu", (6, 4, 64, 1024), BF16),
    ("mlp_mix", (4, 4, 64, 2304), BF16),
    ("attn_mix", (4, 4, 64, 1536), BF16),
    ("h1", (1024, 1024), BF16),
    ("h2", (1024, 1024), BF16),
    ("da", (1024, 1024), BF16),
    ("norm_qk", (768, 1024), BF16),
    ("root_qk", (8, 1024), F32),
    ("ob", (512, 1024), BF16),
    ("qs", (2, 4, 128, 512), BF16),
    ("ks_t", (256, 1024), BF16),
    ("ks", (2, 1024, 128), BF16),
    ("v_t", (2, 144, 1024), BF16),
    ("v", (2, 1024, 128), BF16),
    ("p", (20, 4, 64, 512), BF16),
    ("inv", (2, 4, 8, 512), F32),
    ("inner", (2, 4, 8, 512), F32),
    ("hidden", (768, 1024), BF16),
    ("dgu", (1536, 1024), BF16),
    ("cosine", (64, 1024), F32),
    ("sine", (64, 1024), F32),
    ("x_t", (1024, 256), BF16),
    ("resid", (1024, 256), F32),
    ("gain1", (1024, 128), F32),
    ("gain2", (1024, 128), F32),
    ("gain_q", (128, 128), F32),
    ("gain_k", (128, 128), F32),
    ("gain_sum", (1024, 128), F32),
    ("gain_q_sum", (128, 128), F32),
    ("gain_k_sum", (128, 256), F32),
    ("root1", (8, 256), F32),
    ("root2", (8, 256), F32),
    ("keep", (2, 1024, 256), F32),
    ("sib_out", (2, 2, 1024, 128), BF16),
    ("sib_in", (2, 2, 1024, 128), BF16),
    ("far_out", (2, 1024, 128), BF16),
    ("far_in", (2, 1024, 128), BF16),
    ("mlp_own", (1024, 256), F32),
    ("mlp_sib_out", (2, 2, 1024, 128), BF16),
    ("mlp_sib_in", (2, 2, 1024, 128), BF16),
    ("mlp_far_out", (2, 1024, 128), BF16),
    ("mlp_far_in", (2, 1024, 128), BF16),
    ("mlp_halves", (16, 4, 64, 640), BF16),
    ("sums", (32, 3840), F32),
    ("stage", (256, 1024), BF16),
    ("x_in", (256, 1024), BF16),
    ("g1_in", (1, 1024), F32),
    ("g2_in", (1, 1024), F32),
    ("gq_in", (1, 128), F32),
    ("gk_in", (1, 128), F32),
    ("frequency", (64, 128), F32),
    ("gain_own", (24, 128), F32),
    ("gain_parts", (4, 4, 24, 128), F32),
)
SEMAPHORES = 160


class Box:
    pass


class Place:
    def __init__(self):
        dp = lax.axis_index("dp")
        tensor = lax.axis_index("tensor")
        self.z, self.y, self.x = dp // 8, (dp // 2) % 4, dp % 2
        self.far, self.core = tensor // 2, tensor % 2
        self.me = tensor
        self.sib = self.far * 2 + 1 - self.core
        self.across = (1 - self.far) * 2 + self.core
        self.across_sib = (1 - self.far) * 2 + 1 - self.core

    def near(self, name):
        return step_of(name, self.y if name[0] == "y" else self.z)

    def along(self, name):
        return {"y": self.y, "z": self.z, "x": self.x, "tensor": self.me}[name]

    def device(self, name):
        z, y, x, far, core = self.z, self.y, self.x, self.far, self.core
        if isinstance(name, tuple):
            axis, steps = name
            if axis == "tensor":
                if steps == "far_core":
                    far, core = 1 - far, 1 - core
                else:
                    turned = (self.me + steps) % 4
                    far, core = turned // 2, turned % 2
            elif axis == "y":
                y = (y + steps) % 4
            elif axis == "z":
                z = (z + steps) % 4
            else:
                x = 1 - x
        elif name[0] == "y":
            y = self.near(name)
        elif name[0] == "z":
            z = self.near(name)
        elif name == "x":
            x = 1 - x
        elif name == "far":
            far = 1 - far
        else:
            core = 1 - core
        return ((z * 4 + y) * 2 + x, far * 2 + core)


def step_of(name, value):
    return value + 1 - 2 * (value % 2) if name[1] == "1" else 3 - value


def nn(left, right):
    return lax.dot_general(left, right, (((1,), (0,)), ((), ())), preferred_element_type=F32)


def nt(left, right):
    return lax.dot_general(left, right, (((1,), (1,)), ((), ())), preferred_element_type=F32)


def span(index, size=BLOCK):
    return pl.ds(pl.multiple_of(index * size, size), size)


def loop(count, body):
    def step(index, carry):
        body(index)
        return carry

    lax.fori_loop(0, count, step, 0)


def twice(values):
    return jnp.concatenate([values, values], axis=1)


def fold(values):
    return jnp.sum(values.reshape(values.shape[0] // 8, 8, values.shape[1]), axis=0)


def sub(block, part):
    return pl.ds(pl.multiple_of(block * BLOCK + part * HALF, HALF), HALF)


def lanes(part, size=128):
    return pl.ds(part * size if isinstance(part, int) else pl.multiple_of(part * size, size), size)


def steps(count, body):
    def step(index, carry):
        body(index, lambda k, act: pl.when(index == k)(act))
        return carry

    lax.fori_loop(0, count, step, 0)


class Copy:
    def __init__(self, links, src, dst, name, index):
        self.links, self.src, self.dst, self.name, self.index = links, src, dst, name, index

    def make(self):
        return pltpu.make_async_remote_copy(
            src_ref=self.src(),
            dst_ref=self.dst(),
            send_sem=self.links.sems.at[0, self.index],
            recv_sem=self.links.sems.at[1, self.index],
            device_id=self.links.place.device(self.name),
            device_id_type=MESH,
        )

    def start(self):
        self.make().start()

    def wait_recv(self):
        self.make().wait_recv()

    def wait_send(self):
        self.make().wait_send()


class Links:
    def __init__(self, place, sems):
        self.place, self.sems, self.used, self.sent = place, sems, 0, []

    def copy(self, src, dst, name):
        self.used += 1
        return Copy(self, src, dst, name, self.used - 1)

    def send(self, src, dst, name):
        copy = self.copy(src, dst, name)
        copy.start()
        return copy


class Gather:
    def __init__(self, links, at):
        place = links.place

        def copies(block, name):
            halves = [lambda part=part: at(block, part) for part in range(2)]
            return [links.copy(half, half, name) for half in halves]

        self.far, self.sib = copies(place.me, "far"), copies(place.me, "core")
        self.passed = copies(place.across, "core")

    def send_far(self, part):
        self.far[part].start()

    def send_near(self, part):
        self.sib[part].start()

    def send(self, part):
        self.send_far(part)
        self.send_near(part)

    def pass_on(self, part):
        self.far[part].wait_recv()
        self.passed[part].start()

    def near_ready(self, part):
        self.sib[part].wait_recv()

    def far_ready(self, part):
        self.passed[part].wait_recv()

    def drain(self):
        for copy in self.far + self.sib + self.passed:
            copy.wait_send()


class Reduce:
    def __init__(self, links, sib_out, sib_in, far_out, far_in):
        self.sib_in, self.far_out, self.far_in = sib_in, far_out, far_in
        self.copies = {}
        for part in range(2):
            for index in range(2):
                src = lambda at=(index, part): sib_out.at[at]
                dst = lambda at=(index, part): sib_in.at[at]
                self.copies[index, part] = links.copy(src, dst, "core")
            src, dst = lambda part=part: far_out.at[part], lambda part=part: far_in.at[part]
            self.copies[2, part] = links.copy(src, dst, "far")

    def to_sibling(self, index, part):
        self.copies[index, part].start()

    def make_far(self, keep, part):
        self.copies[0, part].wait_recv()

        def body(i):
            rows = span(i, 512)
            summed = keep[rows, lanes(part)] + self.sib_in[0, part, rows, :].astype(F32)
            self.far_out[part, rows, :] = summed.astype(BF16)

        loop(2, body)

    def send_far(self, part):
        self.copies[2, part].start()

    def arrive(self, part):
        self.copies[1, part].wait_recv()
        self.copies[2, part].wait_recv()

    def total(self, keep, part, rows):
        near = keep[rows, lanes(part)] + self.sib_in[1, part, rows, :].astype(F32)
        return near + self.far_in[part, rows, :].astype(F32)

    def release(self, index, part):
        self.copies.pop((index, part)).wait_send()

    def drain(self):
        for copy in self.copies.values():
            copy.wait_send()


class DpSum:
    def __init__(self, links, box, streams, bufs):
        self.links, self.bufs, self.out = links, bufs, box.sums
        self.streams = [(getattr(box, name), *rest) for name, *rest in streams]
        self.phase = -1
        self.flying = [[] for _ in streams]
        self.sent = []

    def spot(self, stream, slot, *rest):
        _, _, w, at, column, _, _ = self.streams[stream]
        lead = pl.ds(at + slot.start, slot.size) if isinstance(slot, pl.Slice) else at + slot
        return (lead, *rest, pl.ds(column, w))

    def held(self, stream, phase):
        every = slice(None)
        if phase == 0:
            spot = self.spot(stream, pl.ds(0, 2), every, every)
        elif phase == 1:
            spot = self.spot(stream, 2, every, every)
        elif phase == 2:
            spot = self.spot(stream, 3, pl.ds(0, 2), every)
        elif phase == 3:
            spot = self.spot(stream, 3, 2, every)
        else:
            spot = self.spot(stream, 3, 3, pl.ds(0, 32))
        return self.bufs.at[spot]

    def begin(self, stream, phase):
        place = self.links.place
        source_ref, first, w, _, _, order, _ = self.streams[stream]
        order = ORDERS[order]
        name = "x" if phase == 4 else order[phase]

        def other(j):
            there = place.near(name)
            return there if j == 0 else step_of(order[phase + 1], there)

        def source(j):
            if phase == 4:
                return self.bufs.at[self.spot(stream, 3, 2, span(1 - place.x, 32))]
            if phase in (1, 3):
                return self.held(stream, phase - 1).at[1]
            if phase == 2:
                return self.held(stream, 1).at[other(j)]
            lead = (pl.ds(0, 4), other(j)) if name[0] == "y" else (other(j), slice(None))
            return source_ref.at[(*lead, slice(None), pl.ds(first, w))]

        def into(j):
            whole = self.held(stream, phase)
            return whole.at[j] if phase in (0, 2) else whole

        count = 2 if phase in (0, 2) else 1
        send = self.links.send
        return [send(lambda j=j: source(j), lambda j=j: into(j), name) for j in range(count)]

    def finish(self, stream, phase):
        place, spot, bufs = self.links.place, self.spot, self.bufs
        source_ref, first, w, _, _, order, out_first = self.streams[stream]
        order = ORDERS[order]
        every = slice(None)
        for copy in self.flying[stream]:
            copy.wait_recv()
        if phase == 4:
            mine = bufs[spot(stream, 3, 2, span(place.x, 32))].astype(F32)
            columns = pl.ds(out_first, w)
            self.out[:, columns] = bufs[spot(stream, 3, 3, pl.ds(0, 32))].astype(F32) + mine
        elif phase == 3:
            bufs[spot(stream, 3, 2, every)] += bufs[spot(stream, 3, 0, every)]
        elif phase == 1:
            for k in range(4):
                bufs[spot(stream, 2, k, every)] += bufs[spot(stream, 0, k, every)]
        else:
            name = order[phase]
            mine = place.y if name[0] == "y" else place.z
            for j, own in enumerate((mine, step_of(order[phase + 1], mine))):
                if phase == 2:
                    bufs[spot(stream, 3, j, every)] += bufs[spot(stream, 2, own, every)]
                    continue
                for k in range(4):
                    lead = (k, own) if name[0] == "y" else (own, k)
                    kept = source_ref[(*lead, every, pl.ds(first, w))]
                    bufs[spot(stream, j, k, every)] += kept

    def start(self, *streams):
        for stream in streams:
            self.flying[stream] = self.begin(stream, 0)
        self.phase = 0

    def advance(self):
        if self.phase == 5:
            return
        for stream in range(len(self.streams)):
            self.finish(stream, self.phase)
            self.sent += self.flying[stream]
            if self.phase < 4:
                self.flying[stream] = self.begin(stream, self.phase + 1)
        self.phase += 1

    def complete(self):
        while self.phase < 5:
            self.advance()

    def drain(self):
        for copy in self.sent:
            copy.wait_send()


class GainSum:
    def __init__(self, links, own, parts):
        self.links, self.parts, self.copies, self.step = links, parts, [], 0
        self.begin(own[...])

    def begin(self, values):
        place, name = self.links.place, GAIN_ORDER[self.step]
        mine = place.along(name)
        half = self.parts.at[self.step, mine]
        self.parts[self.step, mine] = values
        count = 2 if name == "x" else 4
        self.copies.append([self.links.send(lambda: half, lambda: half, (name, k)) for k in range(1, count)])

    def advance(self):
        if self.step == 4:
            return
        for copy in self.copies[self.step]:
            copy.wait_recv()
        parts = [self.parts[self.step, k] for k in range(len(self.copies[self.step]) + 1)]
        total = parts[0] + parts[1]
        if len(parts) == 4:
            total = total + (parts[2] + parts[3])
        self.step += 1
        if self.step < 4:
            self.begin(total)
        else:
            self.total = total

    def drain(self):
        for copies in self.copies:
            for copy in copies:
                copy.wait_send()


def head_forward(raw, gain, cosine, sine):
    root = lax.rsqrt(jnp.mean(raw * raw, axis=0, keepdims=True) + EPSILON)
    normed = raw * root
    scaled = normed * gain
    first, second = scaled[:64], scaled[64:]
    turned = jnp.concatenate([first * cosine - second * sine, second * cosine + first * sine], axis=0)
    return normed, root, turned


def head_backward(grad, normed, root, gain, cosine, sine):
    first, second = grad[:64], grad[64:]
    turned = jnp.concatenate([first * cosine + second * sine, second * cosine - first * sine], axis=0)
    scaled = turned * gain
    inner = jnp.mean(scaled * normed, axis=0, keepdims=True)
    return root * (scaled - normed * inner), turned * normed


def layer_kernel(
    x, starts, dy, wq, wk, wv, wo, wg, wu, wd, g1, g2, gq, gk, frequency,
    out, grad_x, out_sums, out_gains,
    *scratch,
):
    s = Box()
    for (name, _, _), ref in zip(SCRATCH, scratch):
        setattr(s, name, ref)
    s.keep_far, s.keep_own = s.keep.at[0], s.keep.at[1]
    link_sems, load_sems, ready = scratch[len(SCRATCH) :]
    place = Place()
    links = Links(place, link_sems)
    me, sib, across, across_sib = place.me, place.sib, place.across, place.across_sib

    barrier = pltpu.get_barrier_semaphore()
    for name in PARTNERS + DIAGONALS:
        pl.semaphore_signal(barrier, inc=1, device_id=place.device(name), device_id_type=MESH)

    loads = []

    def load(src, dst):
        copy = pltpu.make_async_copy(src, dst, load_sems.at[len(loads)])
        copy.start()
        loads.append(copy)

    load(x, s.x_in)
    load(g1, s.g1_in)
    for g in range(2):
        load(wq.at[:, pl.ds(256 * g, 256)], s.w_qkv.at[:, pl.ds(512 * g, 256)])
        load(wk.at[:, pl.ds(128 * g, 128)], s.w_qkv.at[:, pl.ds(512 * g + 256, 128)])
        load(wv.at[:, pl.ds(128 * g, 128)], s.w_qkv.at[:, pl.ds(512 * g + 384, 128)])
    load(wo, s.h2.at[pl.ds(0, 512)])
    load(wg, s.mlp_mix.at[:, :, :, pl.ds(0, 768)])
    load(wu, s.mlp_mix.at[:, :, :, pl.ds(768, 768)])
    load(wd, s.w_down)
    load(dy, s.da.at[pl.ds(0, 256)])
    load(g2, s.g2_in)
    load(gq, s.gq_in)
    load(gk, s.gk_in)
    load(frequency, s.frequency)

    near_pair, far_pair = (sib, me), (across_sib, across)

    def pair(ref, rows, blocks, part):
        return jnp.concatenate([ref[rows, sub(b, part)] for b in blocks], axis=1)

    def unpair(ref, rows, blocks, part, values):
        for n, b in enumerate(blocks):
            ref[rows, sub(b, part)] = values[:, HALF * n : HALF * n + HALF]

    every = pl.ds(0, 1024)

    loads[0].wait()
    loads[1].wait()
    gather_h1 = Gather(links, lambda b, part: s.h1.at[:, sub(b, part)])
    for part in range(2):

        def first_norm(i, part=part):
            rows = span(2 * part + i, 64)
            xs = s.x_in[rows, :].astype(F32)
            root = lax.rsqrt(jnp.mean(xs * xs, axis=1, keepdims=True) + EPSILON)
            s.stage[rows, :] = (xs * root * s.g1_in[...]).astype(BF16)

        loop(2, first_norm)
        for j in range(4):
            s.h1[pl.ds(256 * j, 256), sub(me, part)] = s.stage[lanes(part), pl.ds(256 * j, 256)].T
        if part == 0:
            pl.semaphore_wait(barrier, len(PARTNERS) + len(DIAGONALS))
        gather_h1.send(part)

    for k in range(2, 8):
        loads[k].wait()

    def turn_qkv(i):
        s.t_qkv[span(i), :] = s.w_qkv[:, span(i)].T

    loop(4, turn_qkv)

    for k in range(13, 17):
        loads[k].wait()
    place_row = lax.broadcasted_iota(jnp.int32, (8, 1024), 1)
    start_row = jnp.zeros((8, 1024), jnp.int32)
    for d in range(4):
        start_row = jnp.maximum(start_row, jnp.where(place_row >= starts[0, d], starts[0, d], 0))
    position = (place_row - start_row).astype(F32)
    for i in range(8):
        columns = pl.ds(128 * i, 128)
        angle = s.frequency[...] * position[0:1, 128 * i : 128 * i + 128]
        s.cosine[:, columns] = jnp.cos(angle)
        s.sine[:, columns] = jnp.sin(angle)
    for qb in range(4):
        first = start_row[0:1, qb * 256 : qb * 256 + 256]
        query = lax.broadcasted_iota(jnp.int32, (256, 256), 1) + qb * 256
        for kb in range(qb + 1):
            key = lax.broadcasted_iota(jnp.int32, (256, 256), 0) + kb * 256
            allowed = (key <= query) & (key >= first)
            s.dgu[pl.ds(256 * kb, 256), pl.ds(256 * qb, 256)] = jnp.where(allowed, 1.0, 0.0).astype(BF16)

    s.gain1[...] = jnp.broadcast_to(s.g1_in[...], (128, 1024)).T
    s.gain2[...] = jnp.broadcast_to(s.g2_in[...], (128, 1024)).T
    s.gain_q[...] = jnp.broadcast_to(s.gq_in[...], (128, 128)).T
    s.gain_k[...] = jnp.broadcast_to(s.gk_in[...], (128, 128)).T
    s.gain_q_sum[...] = jnp.zeros((128, 128), F32)
    s.gain_sum[...] = jnp.zeros((1024, 128), F32)
    s.gain_k_sum[...] = jnp.zeros((128, 256), F32)
    for g in range(2):
        s.v_t[g, pl.ds(128, 16), :] = jnp.ones((16, 1024), BF16)

    def x_in(i, total):
        turned = s.x_in[:, span(i)].astype(F32).T
        s.x_t[span(i), :] = turned.astype(BF16)
        return total + fold(turned * turned)

    square = lax.fori_loop(0, 4, x_in, jnp.zeros((8, BLOCK), F32))
    root = lax.rsqrt(jnp.sum(square, axis=0, keepdims=True) / 1024.0 + EPSILON)
    s.root1[...] = jnp.broadcast_to(root, (8, BLOCK))

    loads[8].wait()

    def turn_out(i):
        s.attn_mix[i, :, :, pl.ds(1024, 512)] = s.h2[pl.ds(0, 512), span(i)].T.reshape(4, 64, 512)

    loop(4, turn_out)
    loads[9].wait()
    loads[10].wait()

    def turn_gu(i):
        for z in range(4):
            turned = s.mlp_mix[z, :, :, span(i)].reshape(256, 256).T
            s.t_gu[i, :, :, pl.ds(256 * z, 256)] = turned.reshape(4, 64, 256)

    loop(6, turn_gu)
    loads[11].wait()

    def turn_down(i):
        s.mlp_mix[i, :, :, pl.ds(1536, 768)] = s.w_down[:, span(i)].T.reshape(4, 64, 768)

    loop(4, turn_down)

    def dy_in(i):
        s.attn_mix[i, :, :, span(me)] = s.da[pl.ds(0, 256), span(i)].T.reshape(4, 64, BLOCK)

    loads[12].wait()
    loop(4, dy_in)

    def project(blocks, part):
        cosine, sine = pair(s.cosine, pl.ds(0, 64), blocks, part), pair(s.sine, pl.ds(0, 64), blocks, part)
        query_gain = twice(s.gain_q[...] * QUERY_SCALE)
        key_gain = twice(s.gain_k[...])
        every_raw = nn(s.t_qkv[...], pair(s.h1, every, blocks, part))
        for g in range(2):
            raw = every_raw[512 * g : 512 * g + 512]
            for k in range(2):
                head = 3 * g + k
                normed, root, turned = head_forward(raw[128 * k : 128 * k + 128], query_gain, cosine, sine)
                unpair(s.norm_qk, pl.ds(128 * head, 128), blocks, part, normed.astype(BF16))
                unpair(s.root_qk, pl.ds(head, 1), blocks, part, root)
                turned = turned.astype(BF16)
                for n, b in enumerate(blocks):
                    s.qs[g, b, :, lanes(2 * part + k)] = turned[:, HALF * n : HALF * n + HALF]
            normed, root, turned = head_forward(raw[256:384], key_gain, cosine, sine)
            turned, values = turned.astype(BF16), raw[384:].astype(BF16)
            unpair(s.norm_qk, pl.ds(384 * g + 256, 128), blocks, part, normed.astype(BF16))
            unpair(s.root_qk, pl.ds(3 * g + 2, 1), blocks, part, root)
            unpair(s.ks_t, pl.ds(128 * g, 128), blocks, part, turned)
            for n, b in enumerate(blocks):
                s.v_t[g, pl.ds(0, 128), sub(b, part)] = values[:, HALF * n : HALF * n + HALF]
                s.ks[g, sub(b, part), :] = turned[:, HALF * n : HALF * n + HALF].T
                s.v[g, sub(b, part), :] = values[:, HALF * n : HALF * n + HALF].T

    def both_roles(own, body):
        for far in range(2):
            blocks = (2 * far, 2 * far + 1) if own else (2 - 2 * far, 3 - 2 * far)
            pl.when(place.far == far)(lambda blocks=blocks: body(blocks))

    def p_slots(g, qb):
        return pl.ds(g * 10 + qb * (qb + 1) // 2, qb + 1)

    def attend(blocks, parts):
        wide = 256 * len(parts)
        cut = lanes(parts[0], 256) if len(parts) == 1 else pl.ds(0, wide)
        chains = [(qb, g, 256 * (qb + 1)) for qb in blocks for g in range(2)]
        scores = [nn(s.ks[g, pl.ds(0, keys), :], s.qs[g, qb, :, cut]) for qb, g, keys in chains]
        weights = []
        for (qb, g, keys), score in zip(chains, scores):
            halves = [twice(s.dgu[pl.ds(0, keys), lanes(2 * qb + part)]) for part in parts]
            mask = halves[0] if len(parts) == 1 else jnp.concatenate(halves, axis=1)
            weights.append(jnp.exp2(score).astype(BF16) * mask)
        products = [nn(s.v_t[g, :, pl.ds(0, keys)], weight) for (qb, g, keys), weight in zip(chains, weights)]
        for (qb, g, keys), weight, product in zip(chains, weights, products):
            s.p[p_slots(g, qb), :, :, cut] = weight.reshape(qb + 1, 4, 64, wide)
            inverse = 1.0 / product[128:136]
            s.inv[g, qb, :, cut] = inverse
            attended = (product[:128] * inverse[0:1]).astype(BF16)
            for n, part in enumerate(parts):
                for k in range(2):
                    columns = slice(256 * n + 128 * k, 256 * n + 128 * k + 128)
                    s.ob[pl.ds(256 * g + 128 * k, 128), lanes(2 * qb + part)] = attended[:, columns]

    def out_product(blocks, part, store):
        attended = pair(s.ob, pl.ds(0, 512), blocks, part)
        store(nn(s.attn_mix[:, :, :, pl.ds(1024, 512)].reshape(1024, 512), attended))

    def split(sib_out, index, part, keep):
        def store(values):
            sib_out[index, part] = values[:, :HALF].astype(BF16)
            keep[:, lanes(part)] = values[:, HALF:]

        return store

    gather_dy = Gather(links, lambda b, part: s.attn_mix.at[:, :, :, sub(b, part)])

    def choose(far):
        return tuple(jnp.where(far, b, a) for a, b in zip(near_pair, far_pair))

    def project_step(k, when):
        when(0, lambda: gather_h1.near_ready(0))
        when(1, lambda: gather_h1.near_ready(1))

        def third():
            gather_h1.pass_on(0)
            gather_h1.far_ready(0)

        when(2, third)

        def fourth():
            gather_h1.pass_on(1)
            for part in range(2):
                gather_dy.send_near(part)
            gather_dy.send_far(0)
            gather_h1.far_ready(1)

        when(3, fourth)
        project(choose(k >= 2), k % 2)

    steps(4, project_step)

    sum_attn = Reduce(links, s.sib_out, s.sib_in, s.far_out, s.far_in)

    def attend_step(k, when):
        both_roles(False, lambda blocks: attend(blocks, (k,)))

        def second():
            sum_attn.make_far(s.keep_far, 0)
            sum_attn.send_far(0)

        when(1, second)
        out_product(far_pair, k, split(s.sib_out, 0, k, s.keep_far))
        when(0, lambda: sum_attn.to_sibling(0, 0))
        when(1, lambda: sum_attn.to_sibling(0, 1))

    steps(2, attend_step)
    both_roles(True, lambda blocks: attend(blocks, (0, 1)))
    sum_attn.make_far(s.keep_far, 1)
    sum_attn.send_far(1)
    loop(2, lambda part: out_product(near_pair, part, split(s.sib_out, 1, part, s.keep_own)))
    for part in range(2):
        sum_attn.to_sibling(1, part)
    for part in range(2):
        gather_dy.near_ready(part)
    gather_dy.pass_on(0)

    gather_h2 = Gather(links, lambda b, part: s.h2.at[:, sub(b, part)])

    def second_norm(part):
        sum_attn.arrive(part)

        def square(i, total):
            x1 = s.x_t[span(i), lanes(part)].astype(F32) + sum_attn.total(s.keep_own, part, span(i))
            s.resid[span(i), lanes(part)] = x1
            return total + fold(x1 * x1)

        total = lax.fori_loop(0, 4, square, jnp.zeros((8, HALF), F32))
        root = lax.rsqrt(jnp.sum(total, axis=0, keepdims=True) / 1024.0 + EPSILON)
        s.root2[:, lanes(part)] = jnp.broadcast_to(root, (8, HALF))

        def scale(i):
            normed = s.resid[span(i), lanes(part)] * s.root2[0:1, lanes(part)]
            s.h2[span(i), sub(me, part)] = (normed * s.gain2[span(i), :]).astype(BF16)

        loop(4, scale)
        gather_h2.send(part)

    def feed(blocks, part):
        def body(j):
            gate = nn(s.t_gu[j].reshape(256, 1024), pair(s.h2, every, blocks, part))
            up = nn(s.t_gu[3 + j].reshape(256, 1024), pair(s.h2, every, blocks, part))
            grads = [s.attn_mix[:, :, :, sub(b, part)].reshape(1024, HALF) for b in blocks]
            grad = nn(s.w_down[span(j), :], jnp.concatenate(grads, axis=1))
            open_gate = jax.nn.sigmoid(gate)
            silu = gate * open_gate
            unpair(s.hidden, span(j), blocks, part, (silu * up).astype(BF16))
            dgate = (grad * up * open_gate * (1.0 + gate * (1.0 - open_gate))).astype(BF16)
            unpair(s.dgu, span(j), blocks, part, dgate)
            unpair(s.dgu, span(3 + j), blocks, part, (grad * silu).astype(BF16))

        for j in range(3):
            body(j)

    def feed_back(blocks, part, store):
        grads = pair(s.dgu, pl.ds(0, 1536), blocks, part)
        store(nn(s.mlp_mix[:, :, :, pl.ds(0, 1536)].reshape(1024, 1536), grads))

    def mlp_product(blocks, part, store):
        hidden = pair(s.hidden, pl.ds(0, 768), blocks, part)
        store(nn(s.mlp_mix[:, :, :, pl.ds(1536, 768)].reshape(1024, 768), hidden))

    sum_dh2 = Reduce(links, s.sib_out, s.sib_in, s.far_out, s.far_in)

    def feed_step(k, when):
        def first():
            second_norm(0)
            sum_attn.release(1, 0)
            gather_h2.near_ready(0)

        when(0, first)

        def second():
            second_norm(1)
            sum_attn.drain()
            gather_h2.pass_on(0)
            gather_h2.near_ready(1)

        when(1, second)

        def third():
            gather_dy.far_ready(0)
            gather_h2.far_ready(0)

        when(2, third)

        def fourth():
            gather_h2.pass_on(1)
            gather_dy.pass_on(1)
            gather_h2.far_ready(1)
            gather_dy.far_ready(1)

        when(3, fourth)
        far, part = k >= 2, k % 2
        feed(choose(far), part)
        index = 1 - k // 2
        feed_back(choose(far), part, split(s.sib_out, index, part, s.keep.at[index]))
        when(0, lambda: sum_dh2.to_sibling(1, 0))

        def second_end():
            sum_dh2.to_sibling(1, 1)
            gather_dy.send_far(1)

        when(1, second_end)

        def third_end():
            sum_dh2.to_sibling(0, 0)
            sum_dh2.make_far(s.keep_far, 0)
            sum_dh2.send_far(0)

        when(2, third_end)
        when(3, lambda: sum_dh2.to_sibling(0, 1))

    steps(4, feed_step)

    dp_mlp = DpSum(links, s, MLP_STREAMS, s.mlp_halves)

    def feed_grad(stream):
        name, first, w, _, _, _, _ = MLP_STREAMS[stream]
        if name == "mlp_mix":
            values = nt(s.h2[...], s.dgu[pl.ds(first, w), :])
        else:
            values = nt(s.attn_mix[:, :, :, pl.ds(0, 1024)].reshape(1024, 1024), s.hidden[pl.ds(first, w), :])
        into = getattr(s, name)
        into[pl.ds(0, 4), :, :, pl.ds(first, w)] = values.astype(BF16).reshape(4, 4, 64, w)
        dp_mlp.start(stream)

    gather_da = Gather(links, lambda b, part: s.da.at[:, sub(b, part)])

    def norm_back(part):
        sum_dh2.arrive(part)

        def inner_sum(i, total):
            grad = sum_dh2.total(s.keep_own, part, span(i))
            s.keep_own[span(i), lanes(part)] = grad
            product = grad * (s.resid[span(i), lanes(part)] * s.root2[0:1, lanes(part)])
            s.gain_sum[span(i), :] += product
            return total + fold(product * s.gain2[span(i), :])

        inner = lax.fori_loop(0, 4, inner_sum, jnp.zeros((8, HALF), F32))
        inner = jnp.sum(inner, axis=0, keepdims=True) / 1024.0

        def body(i):
            root = s.root2[0:1, lanes(part)]
            scaled = s.keep_own[span(i), lanes(part)] * s.gain2[span(i), :]
            normed = s.resid[span(i), lanes(part)] * root
            own = s.attn_mix[i, :, :, sub(me, part)].reshape(256, HALF).astype(F32)
            s.da[span(i), sub(me, part)] = (own + root * (scaled - normed * inner)).astype(BF16)
            s.mlp_own[span(i), lanes(part)] = s.resid[span(i), lanes(part)]
            s.resid[span(i), lanes(part)] = own + root * (scaled - normed * inner)

        loop(4, body)
        gather_da.send(part)

    feed_grad(0)
    sum_dh2.make_far(s.keep_far, 1)
    sum_dh2.send_far(1)
    feed_grad(1)
    norm_back(0)
    feed_grad(4)
    feed_grad(2)
    feed_grad(3)
    gather_h2.drain()
    load(wo, s.h2.at[pl.ds(0, 512)])
    norm_back(1)
    sum_dh2.drain()

    def put_gain(first, row):
        for k in range(row.shape[1] // 128):
            s.gain_own[first + k : first + k + 1, :] = row[:, 128 * k : 128 * k + 128]

    put_gain(8, jnp.sum(s.gain_sum[...].T, axis=0, keepdims=True))
    s.gain_sum[...] = jnp.zeros((1024, 128), F32)

    sum_mlp = Reduce(links, s.mlp_sib_out, s.mlp_sib_in, s.mlp_far_out, s.mlp_far_in)

    def mlp_mine(part):
        def store(values):
            s.mlp_sib_out[1, part] = values[:, :HALF].astype(BF16)
            s.mlp_own[:, lanes(part)] += values[:, HALF:]

        return store

    loop(2, lambda part: mlp_product(far_pair, part, split(s.mlp_sib_out, 0, part, s.keep_far)))
    for part in range(2):
        sum_mlp.to_sibling(0, part)
    for part in range(2):
        sum_mlp.make_far(s.keep_far, part)

    s.keep[...] = jnp.zeros((2, 1024, 256), F32)
    loads[17].wait()

    def dob(g, b, part):
        index = g * 4 + b
        return (4 + index // 4, pl.ds(2 * ((index // 2) % 2), 2), slice(None), pl.ds(pl.multiple_of((index % 2) * 512 + part * 256, 256), 256))

    def out_back(blocks, part):
        two = lanes(part, 256)
        every_grad = nn(s.h2[pl.ds(0, 512), :], pair(s.da, every, blocks, part))
        for g in range(2):
            grads = every_grad[256 * g : 256 * g + 256]
            for n, b in enumerate(blocks):
                columns = slice(HALF * n, HALF * n + HALF)
                both = jnp.concatenate([grads[:128, columns], grads[128:, columns]], axis=1) * s.inv[g, b, 0:1, two]
                outs = [s.ob[pl.ds(256 * g + 128 * k, 128), sub(b, part)] for k in range(2)]
                inner = jnp.sum(both * jnp.concatenate(outs, axis=1).astype(F32), axis=0, keepdims=True)
                s.inner[g, b, :, two] = jnp.broadcast_to(inner, (8, 256))
                s.t_gu[dob(g, b, part)] = both.astype(BF16).reshape(2, 64, 256)

    def attend_back(blocks, parts, groups):
        wide = 256 * len(parts)
        cut = lanes(parts[0], 256) if len(parts) == 1 else pl.ds(0, wide)
        chains = [(qb, g, 256 * (qb + 1)) for qb in blocks for g in groups]
        grads, weights, slopes, changes, key_parts, query_parts, value_parts = [], [], [], [], [], [], []
        for qb, g, keys in chains:
            index = g * 4 + qb
            columns = lanes((index % 2) * 2 + parts[0], 256) if len(parts) == 1 else lanes(index % 2, 512)
            at = (4 + index // 4, pl.ds(2 * ((index // 2) % 2), 2), slice(None), columns)
            grads.append(s.t_gu[at].reshape(128, wide))
            weights.append(s.p[p_slots(g, qb), :, :, cut].reshape(keys, wide))
        for (qb, g, keys), grad in zip(chains, grads):
            slopes.append(nn(s.v[g, pl.ds(0, keys), :], grad))
        for weight, grad in zip(weights, grads):
            value_parts.append(nt(weight, grad))
        for (qb, g, keys), weight, slope in zip(chains, weights, slopes):
            changes.append((weight.astype(F32) * (slope - s.inner[g, qb, 0:1, cut])).astype(BF16))
        for (qb, g, keys), change in zip(chains, changes):
            key_parts.append(nt(change, s.qs[g, qb, :, cut]))
            query_parts.append(nn(s.ks_t[pl.ds(128 * g, 128), pl.ds(0, keys)], change))
        for (qb, g, keys), value_part, key_part, query_part in zip(chains, value_parts, key_parts, query_parts):
            s.keep_own[pl.ds(0, keys), lanes(g)] += value_part
            s.keep_far[pl.ds(0, keys), lanes(g)] += key_part
            for n, part in enumerate(parts):
                columns = lanes(2 * qb + part)
                for k in range(2):
                    head = 3 * g + k
                    grad, gain_part = head_backward(
                        query_part[:, 256 * n + 128 * k : 256 * n + 128 * k + 128] * (1.0 / math.sqrt(HEAD)),
                        s.norm_qk[pl.ds(128 * head, 128), columns].astype(F32),
                        s.root_qk[pl.ds(head, 1), columns],
                        s.gain_q[...],
                        s.cosine[:, columns],
                        s.sine[:, columns],
                    )
                    s.t_qkv[pl.ds(512 * g + 128 * k, 128), columns] = grad.astype(BF16)
                    s.gain_q_sum[...] += gain_part

    def key_back(g):
        gain = twice(s.gain_k[...])

        def body(b):
            columns = span(b)
            grad, gain_part = head_backward(
                s.keep_far[columns, lanes(g)].T * math.log(2.0),
                s.norm_qk[pl.ds(384 * g + 256, 128), columns].astype(F32),
                s.root_qk[pl.ds(3 * g + 2, 1), columns],
                gain,
                s.cosine[:, columns],
                s.sine[:, columns],
            )
            s.t_qkv[pl.ds(512 * g + 256, 128), columns] = grad.astype(BF16)
            s.gain_k_sum[...] += gain_part
            s.t_qkv[pl.ds(512 * g + 384, 128), columns] = s.keep_own[columns, lanes(g)].T.astype(BF16)

        loop(4, body)

    def tell_ready():
        for k, name in enumerate(PARTNERS[2:]):
            pl.semaphore_signal(ready.at[k], inc=1, device_id=place.device(name), device_id_type=MESH)

    def wait_ready():
        for k in range(5):
            pl.semaphore_wait(ready.at[k], 1)

    def qkv_grad(g):
        values = nt(s.h1[...], s.t_qkv[span(g, 512), :]).astype(BF16)
        s.attn_mix[:, :, :, span(g, 512)] = values.reshape(4, 4, 64, 512)

    def out_grad():
        values = nt(s.da[...], s.ob[...]).astype(BF16)
        s.attn_mix[:, :, :, pl.ds(1024, 512)] = values.reshape(4, 4, 64, 512)

    for part in range(2):
        gather_da.near_ready(part)
    loop(2, lambda part: out_back(near_pair, part))
    gather_da.pass_on(0)
    both_roles(True, lambda blocks: attend_back(blocks, (0, 1), (0, 1)))
    gather_dy.drain()

    def back_step(k, when):
        when(0, lambda: gather_da.far_ready(0))
        when(1, lambda: gather_da.far_ready(1))
        out_back(far_pair, k)

        def first():
            gather_da.pass_on(1)
            sum_mlp.send_far(0)

        when(0, first)
        when(1, dp_mlp.advance)
        both_roles(False, lambda blocks: attend_back(blocks, (k,), (0, 1)))

    steps(2, back_step)
    tell_ready()
    for g in range(2):
        key_back(g)
    out_grad()
    loop(2, qkv_grad)
    wait_ready()
    dp_attn = DpSum(links, s, ATTN_STREAMS, s.p)
    dp_attn.start(0, 1, 2, 3)

    def in_back(blocks, part, store):
        values = nn(s.w_qkv[...], pair(s.t_qkv, every, blocks, part))
        product = values * pair(s.h1, every, blocks, part).astype(F32)
        s.gain_sum[...] += product[:, :HALF] + product[:, HALF:]
        store(values)

    sum_dh1 = Reduce(links, s.sib_out, s.sib_in, s.far_out, s.far_in)
    loop(2, lambda part: in_back(far_pair, part, split(s.sib_out, 0, part, s.keep_far)))
    for part in range(2):
        sum_dh1.to_sibling(0, part)
    for part in range(2):
        sum_dh1.make_far(s.keep_far, part)
        sum_dh1.send_far(part)
    sum_mlp.send_far(1)
    dp_mlp.advance()
    loop(2, lambda part: in_back(near_pair, part, split(s.sib_out, 1, part, s.keep_own)))
    for part in range(2):
        sum_dh1.to_sibling(1, part)
    loop(2, lambda part: mlp_product(near_pair, part, mlp_mine(part)))
    for part in range(2):
        sum_mlp.to_sibling(1, part)
    put_gain(0, jnp.sum((s.gain_sum[...] / s.gain1[...]).T, axis=0, keepdims=True))
    both = s.gain_k_sum[:, lanes(0)] + s.gain_k_sum[:, lanes(1)]
    put_gain(16, jnp.sum(s.gain_q_sum[...].T, axis=0, keepdims=True))
    put_gain(17, jnp.sum(both.T, axis=0, keepdims=True))
    s.gain_own[pl.ds(18, 6), :] = jnp.zeros((6, 128), F32)
    gains = GainSum(links, s.gain_own, s.gain_parts)
    dp_attn.advance()
    dp_mlp.advance()
    gains.advance()
    dp_attn.advance()
    dp_mlp.advance()
    gains.advance()

    for part in range(2):
        sum_dh1.arrive(part)

        def inner_sum(i, total, part=part):
            grad = sum_dh1.total(s.keep_own, part, span(i))
            s.keep_own[span(i), lanes(part)] = grad
            normed = s.x_t[span(i), lanes(part)].astype(F32) * s.root1[0:1, lanes(part)]
            return total + fold(grad * normed * s.gain1[span(i), :])

        inner = lax.fori_loop(0, 4, inner_sum, jnp.zeros((8, HALF), F32))
        inner = jnp.sum(inner, axis=0, keepdims=True) / 1024.0

        def last_back(i, part=part, inner=inner):
            root = s.root1[0:1, lanes(part)]
            scaled = s.keep_own[span(i), lanes(part)] * s.gain1[span(i), :]
            normed = s.x_t[span(i), lanes(part)].astype(F32) * root
            s.resid[span(i), lanes(part)] += root * (scaled - normed * inner)

        loop(4, last_back)
        if part == 0:
            dp_attn.advance()
            gains.advance()
    load(s.resid, grad_x)

    for part in range(2):
        sum_mlp.arrive(part)

        def layer_out(i, part=part):
            s.stage[lanes(part), span(i)] = sum_mlp.total(s.mlp_own, part, span(i)).T.astype(BF16)

        loop(4, layer_out)
    load(s.stage, out)
    while dp_attn.phase < 5 or dp_mlp.phase < 5 or gains.step < 4:
        dp_attn.advance()
        gains.advance()
        dp_mlp.advance()
    load(s.sums, out_sums)
    s.gain_own[...] = gains.total
    load(s.gain_own, out_gains)

    for copy in loads[18:]:
        copy.wait()
    for exchange in (gather_h1, gather_da, sum_mlp, sum_dh1, dp_mlp, dp_attn, gains):
        exchange.drain()


def deliver_kernel(*refs):
    given, outs, held = refs[:4], refs[4:17], refs[17:21]
    turned, gain_rows, sems_in, sems_out = refs[21:]
    arrivals = [pltpu.make_async_copy(a, b, sems_in.at[k]) for k, (a, b) in enumerate(zip(given, held))]
    for copy in arrivals:
        copy.start()
    started = []

    def send(src, dst):
        copy = pltpu.make_async_copy(src, dst, sems_out.at[len(started)])
        copy.start()
        started.append(copy)

    arrivals[3].wait()
    gain_rows[0] = held[3][16:17]
    gain_rows[1] = held[3][17:18]
    send(held[3].at[pl.ds(0, 8)], outs[9])
    send(held[3].at[pl.ds(8, 8)], outs[10])
    send(gain_rows.at[0], outs[11])
    send(gain_rows.at[1], outs[12])
    arrivals[2].wait()
    sums = held[2]
    for g in range(2):
        for out, first, width in ((outs[2], 0, 256), (outs[3], 256, 128), (outs[4], 384, 128)):
            send(sums.at[:, pl.ds(512 * g + first, width)], out.at[:, pl.ds(width * g, width)])
    for out, first, width in ((outs[5], 1024, 512), (outs[6], 1536, 768), (outs[7], 2304, 768), (outs[8], 3072, 768)):
        send(sums.at[:, pl.ds(first, width)], out)
    arrivals[0].wait()
    send(held[0], outs[0])
    arrivals[1].wait()
    for i in range(4):
        turned[:, pl.ds(256 * i, 256)] = held[1][pl.ds(256 * i, 256), :].T
    send(turned, outs[1])
    for copy in started:
        copy.wait()


def shards(
    tokens,
    doc_starts,
    cotangent,
    w_query,
    key_matrix,
    value_matrix,
    w_out,
    w_gate,
    w_up,
    w_down,
    gain_attn,
    gain_mlp,
    gain_query,
    gain_key,
):
    frequency = ROPE_BASE ** (-(np.arange(64, dtype=np.float64) * 2.0) / HEAD)
    frequency = jnp.asarray(np.broadcast_to(frequency[:, None], (64, 128)).astype(np.float32))
    hbm = pl.BlockSpec(memory_space=pl.ANY)
    smem = pl.BlockSpec(memory_space=pltpu.SMEM)

    def shaped(*shape, kind=F32):
        return jax.ShapeDtypeStruct(shape, kind)

    gains = (shaped(8, 128), shaped(8, 128), shaped(1, 128), shaped(1, 128))
    given = (shaped(256, 1024, kind=BF16), shaped(1024, 256), shaped(32, 3840), shaped(24, 128))
    widths = (512, 256, 256, 512, 768, 768, 768)
    outs = pl.pallas_call(
        layer_kernel,
        out_shape=given,
        in_specs=[hbm, smem] + [hbm] * 13,
        out_specs=(hbm,) * 4,
        scratch_shapes=[pltpu.VMEM(shape, kind) for _, shape, kind in SCRATCH]
        + [
            pltpu.SemaphoreType.DMA((2, SEMAPHORES)),
            pltpu.SemaphoreType.DMA((24,)),
            pltpu.SemaphoreType.REGULAR((5,)),
        ],
        compiler_params=pltpu.CompilerParams(
            collective_id=0, has_side_effects=True, vmem_limit_bytes=64 * 2**20 - 2**16
        ),
        cost_estimate=pl.CostEstimate(flops=32 * 10**9, bytes_accessed=2**24, transcendentals=2**22),
        name="layer",
    )(
        tokens.reshape(256, 1024),
        doc_starts,
        cotangent.reshape(256, 1024),
        w_query,
        key_matrix,
        value_matrix,
        w_out,
        w_gate.reshape(4, 4, 64, 768),
        w_up.reshape(4, 4, 64, 768),
        w_down,
        gain_attn.reshape(1, 1024),
        gain_mlp.reshape(1, 1024),
        gain_query.reshape(1, 128),
        gain_key.reshape(1, 128),
        frequency,
    )
    outs = pl.pallas_call(
        deliver_kernel,
        out_shape=(given[0], shaped(256, 1024)) + tuple(shaped(32, width) for width in widths) + gains,
        in_specs=[hbm] * 4,
        out_specs=(hbm,) * 13,
        scratch_shapes=[pltpu.VMEM(one.shape, one.dtype) for one in given]
        + [
            pltpu.VMEM((256, 1024), F32),
            pltpu.VMEM((2, 1, 128), F32),
            pltpu.SemaphoreType.DMA((4,)),
            pltpu.SemaphoreType.DMA((16,)),
        ],
        name="deliver",
    )(*outs)
    return (
        outs[0].reshape(1, 256, 1024),
        outs[1].reshape(1, 256, 1024),
        *outs[2:5],
        outs[5].T,
        *outs[6:8],
        outs[8].T,
        *(gain.reshape(-1) for gain in outs[9:]),
    )


def solution(mesh):
    in_specs = (
        P("dp", "tensor", None),
        P("dp", None),
        P("dp", "tensor", None),
        P(None, "tensor"),
        P(None, "tensor"),
        P(None, "tensor"),
        P("tensor", None),
        P(None, "tensor"),
        P(None, "tensor"),
        P("tensor", None),
        P(),
        P(),
        P(),
        P(),
    )
    out_specs = (
        P("dp", "tensor", None),
        P("dp", "tensor", None),
        P("dp", "tensor"),
        P("dp", "tensor"),
        P("dp", "tensor"),
        P("tensor", "dp"),
        P("dp", "tensor"),
        P("dp", "tensor"),
        P("tensor", "dp"),
        P(),
        P(),
        P(),
        P(),
    )
    return jax.shard_map(shards, mesh=mesh, in_specs=in_specs, out_specs=out_specs, check_vma=False)
```

```python
import math

import jax
import jax.numpy as jnp
import numpy as np
from jax import lax
from jax.experimental import pallas as pl
from jax.experimental.pallas import tpu as pltpu
from jax.sharding import PartitionSpec as P

MESH = pl.DeviceIdType.MESH
BF16 = jnp.bfloat16
F32 = jnp.float32
EPSILON = 1e-06
ROPE_BASE = 1000000.0
BLOCK = 256
HALF = 128
HEAD = 128
QUERY_SCALE = math.log2(math.e) / math.sqrt(HEAD)
PARTNERS = ("core", "far", "y1", "y2", "z1", "z2", "x")
DIAGONALS = (("y", 2), ("z", 2), ("tensor", "far_core"))
ORDERS = (("y1", "y2", "z1", "z2"), ("y2", "y1", "z2", "z1"), ("z1", "z2", "y1", "y2"), ("z2", "z1", "y2", "y1"))
MLP_STREAMS = (
    ("mlp_mix", 0, 640, 0, 0, 0, 1536),
    ("mlp_mix", 640, 640, 4, 0, 1, 2176),
    ("mlp_mix", 1280, 256, 8, 0, 2, 2816),
    ("t_gu", 0, 256, 8, 256, 2, 3072),
    ("t_gu", 256, 512, 12, 0, 3, 3328),
)
ATTN_STREAMS = tuple(
    ("attn_mix", 512 + 256 * k, 256, 10 + 4 * (k // 2), 256 * (k % 2), k, 512 + 256 * k) for k in range(4)
) + tuple(("attn_mix", 128 * k, 128, 0, 128 * k, k, 128 * k) for k in range(4))
GAIN_ORDER = ("y", "z", "tensor", "x")

SCRATCH = (
    ("w_qkv", (1024, 1024), BF16),
    ("t_qkv", (1024, 1024), BF16),
    ("w_down", (768, 1024), BF16),
    ("t_gu", (6, 4, 64, 1024), BF16),
    ("mlp_mix", (4, 4, 64, 2304), BF16),
    ("attn_mix", (4, 4, 64, 1536), BF16),
    ("h1", (1024, 1024), BF16),
    ("h2", (1024, 1024), BF16),
    ("da", (1024, 1024), BF16),
    ("norm_qk", (768, 1024), BF16),
    ("root_qk", (8, 1024), F32),
    ("ob", (512, 1024), BF16),
    ("qs", (2, 4, 128, 512), BF16),
    ("ks_t", (256, 1024), BF16),
    ("ks", (2, 1024, 128), BF16),
    ("v_t", (2, 144, 1024), BF16),
    ("v", (2, 1024, 128), BF16),
    ("p", (20, 4, 64, 512), BF16),
    ("inv", (2, 4, 8, 512), F32),
    ("inner", (2, 4, 8, 512), F32),
    ("hidden", (768, 1024), BF16),
    ("dgu", (1536, 1024), BF16),
    ("cosine", (64, 1024), F32),
    ("sine", (64, 1024), F32),
    ("x_t", (1024, 256), BF16),
    ("resid", (1024, 256), F32),
    ("gain1", (1024, 128), F32),
    ("gain2", (1024, 128), F32),
    ("gain_q", (128, 128), F32),
    ("gain_k", (128, 128), F32),
    ("gain_sum", (1024, 128), F32),
    ("gain_q_sum", (128, 128), F32),
    ("gain_k_sum", (128, 256), F32),
    ("root1", (8, 256), F32),
    ("root2", (8, 256), F32),
    ("keep", (2, 1024, 256), F32),
    ("sib_out", (2, 2, 1024, 128), BF16),
    ("sib_in", (2, 2, 1024, 128), BF16),
    ("far_out", (2, 1024, 128), BF16),
    ("far_in", (2, 1024, 128), BF16),
    ("mlp_own", (1024, 256), F32),
    ("mlp_sib_out", (2, 2, 1024, 128), BF16),
    ("mlp_sib_in", (2, 2, 1024, 128), BF16),
    ("mlp_far_out", (2, 1024, 128), BF16),
    ("mlp_far_in", (2, 1024, 128), BF16),
    ("mlp_halves", (16, 4, 64, 640), BF16),
    ("sums", (32, 3840), F32),
    ("stage", (256, 1024), BF16),
    ("x_in", (256, 1024), BF16),
    ("g1_in", (1, 1024), F32),
    ("g2_in", (1, 1024), F32),
    ("gq_in", (1, 128), F32),
    ("gk_in", (1, 128), F32),
    ("frequency", (64, 128), F32),
    ("gain_own", (24, 128), F32),
    ("gain_parts", (4, 4, 24, 128), F32),
)
SEMAPHORES = 190


class Box:
    pass


class Place:
    def __init__(self):
        dp = lax.axis_index("dp")
        tensor = lax.axis_index("tensor")
        self.z, self.y, self.x = dp // 8, (dp // 2) % 4, dp % 2
        self.far, self.core = tensor // 2, tensor % 2
        self.me = tensor
        self.sib = self.far * 2 + 1 - self.core
        self.across = (1 - self.far) * 2 + self.core
        self.across_sib = (1 - self.far) * 2 + 1 - self.core

    def near(self, name):
        return step_of(name, self.y if name[0] == "y" else self.z)

    def along(self, name):
        return {"y": self.y, "z": self.z, "x": self.x, "tensor": self.me}[name]

    def device(self, name):
        z, y, x, far, core = self.z, self.y, self.x, self.far, self.core
        if isinstance(name, tuple):
            axis, steps = name
            if axis == "tensor":
                if steps == "far_core":
                    far, core = 1 - far, 1 - core
                else:
                    turned = (self.me + steps) % 4
                    far, core = turned // 2, turned % 2
            elif axis == "y":
                y = (y + steps) % 4
            elif axis == "z":
                z = (z + steps) % 4
            else:
                x = 1 - x
        elif name[0] == "y":
            y = self.near(name)
        elif name[0] == "z":
            z = self.near(name)
        elif name == "x":
            x = 1 - x
        elif name == "far":
            far = 1 - far
        else:
            core = 1 - core
        return ((z * 4 + y) * 2 + x, far * 2 + core)


def step_of(name, value):
    return value + 1 - 2 * (value % 2) if name[1] == "1" else 3 - value


def nn(left, right):
    return lax.dot_general(left, right, (((1,), (0,)), ((), ())), preferred_element_type=F32)


def nt(left, right):
    return lax.dot_general(left, right, (((1,), (1,)), ((), ())), preferred_element_type=F32)


def span(index, size=BLOCK):
    return pl.ds(pl.multiple_of(index * size, size), size)


def loop(count, body):
    def step(index, carry):
        body(index)
        return carry

    lax.fori_loop(0, count, step, 0)


def twice(values):
    return jnp.concatenate([values, values], axis=1)


def fold(values):
    return jnp.sum(values.reshape(values.shape[0] // 8, 8, values.shape[1]), axis=0)


def sub(block, part):
    return pl.ds(pl.multiple_of(block * BLOCK + part * HALF, HALF), HALF)


def lanes(part, size=128):
    return pl.ds(part * size if isinstance(part, int) else pl.multiple_of(part * size, size), size)


def steps(count, body):
    def step(index, carry):
        body(index, lambda k, act: pl.when(index == k)(act))
        return carry

    lax.fori_loop(0, count, step, 0)


class Copy:
    def __init__(self, links, src, dst, name, index):
        self.links, self.src, self.dst, self.name, self.index = links, src, dst, name, index

    def make(self):
        return pltpu.make_async_remote_copy(
            src_ref=self.src(),
            dst_ref=self.dst(),
            send_sem=self.links.sems.at[0, self.index],
            recv_sem=self.links.sems.at[1, self.index],
            device_id=self.links.place.device(self.name),
            device_id_type=MESH,
        )

    def start(self):
        self.make().start()

    def wait_recv(self):
        self.make().wait_recv()

    def wait_send(self):
        self.make().wait_send()


class Links:
    def __init__(self, place, sems):
        self.place, self.sems, self.used, self.sent = place, sems, 0, []

    def copy(self, src, dst, name):
        self.used += 1
        return Copy(self, src, dst, name, self.used - 1)

    def send(self, src, dst, name):
        copy = self.copy(src, dst, name)
        copy.start()
        return copy


class Gather:
    def __init__(self, links, at):
        place = links.place

        def copies(block, name):
            halves = [lambda part=part: at(block, part) for part in range(2)]
            return [links.copy(half, half, name) for half in halves]

        self.far, self.sib = copies(place.me, "far"), copies(place.me, "core")
        self.passed = copies(place.across, "core")

    def send_far(self, part):
        self.far[part].start()

    def send_near(self, part):
        self.sib[part].start()

    def send(self, part):
        self.send_far(part)
        self.send_near(part)

    def pass_on(self, part):
        self.far[part].wait_recv()
        self.passed[part].start()

    def near_ready(self, part):
        self.sib[part].wait_recv()

    def far_ready(self, part):
        self.passed[part].wait_recv()

    def drain(self):
        for copy in self.far + self.sib + self.passed:
            copy.wait_send()


class Reduce:
    def __init__(self, links, sib_out, sib_in, far_out, far_in):
        self.sib_in, self.far_out, self.far_in = sib_in, far_out, far_in
        self.copies = {}
        for part in range(2):
            for index in range(2):
                src = lambda at=(index, part): sib_out.at[at]
                dst = lambda at=(index, part): sib_in.at[at]
                self.copies[index, part] = links.copy(src, dst, "core")
            src, dst = lambda part=part: far_out.at[part], lambda part=part: far_in.at[part]
            self.copies[2, part] = links.copy(src, dst, "far")

    def to_sibling(self, index, part):
        self.copies[index, part].start()

    def make_far(self, keep, part):
        self.copies[0, part].wait_recv()

        def body(i):
            rows = span(i, 512)
            summed = keep[rows, lanes(part)] + self.sib_in[0, part, rows, :].astype(F32)
            self.far_out[part, rows, :] = summed.astype(BF16)

        loop(2, body)

    def send_far(self, part):
        self.copies[2, part].start()

    def arrive(self, part):
        self.copies[1, part].wait_recv()
        self.copies[2, part].wait_recv()

    def total(self, keep, part, rows):
        near = keep[rows, lanes(part)] + self.sib_in[1, part, rows, :].astype(F32)
        return near + self.far_in[part, rows, :].astype(F32)

    def release(self, index, part):
        self.copies.pop((index, part)).wait_send()

    def drain(self):
        for copy in self.copies.values():
            copy.wait_send()


class DpSum:
    def __init__(self, links, box, streams, bufs):
        self.links, self.bufs, self.out = links, bufs, box.sums
        self.streams = [(getattr(box, name), *rest) for name, *rest in streams]
        self.phases = [-1] * len(streams)
        self.flying = [[] for _ in streams]
        self.sent = []

    def spot(self, stream, slot, *rest):
        _, _, w, at, column, _, _ = self.streams[stream]
        lead = pl.ds(at + slot.start, slot.size) if isinstance(slot, pl.Slice) else at + slot
        return (lead, *rest, pl.ds(column, w))

    def held(self, stream, phase):
        every = slice(None)
        if phase == 0:
            spot = self.spot(stream, pl.ds(0, 2), every, every)
        elif phase == 1:
            spot = self.spot(stream, 2, every, every)
        elif phase == 2:
            spot = self.spot(stream, 3, pl.ds(0, 2), every)
        elif phase == 3:
            spot = self.spot(stream, 3, 2, every)
        else:
            spot = self.spot(stream, 3, 3, pl.ds(0, 32))
        return self.bufs.at[spot]

    def begin(self, stream, phase):
        place = self.links.place
        source_ref, first, w, _, _, order, _ = self.streams[stream]
        order = ORDERS[order]
        name = "x" if phase == 4 else order[phase]

        def other(j):
            there = place.near(name)
            return there if j == 0 else step_of(order[phase + 1], there)

        def source(j):
            if phase == 4:
                return self.bufs.at[self.spot(stream, 3, 2, span(1 - place.x, 32))]
            if phase in (1, 3):
                return self.held(stream, phase - 1).at[1]
            if phase == 2:
                return self.held(stream, 1).at[other(j)]
            lead = (pl.ds(0, 4), other(j)) if name[0] == "y" else (other(j), slice(None))
            return source_ref.at[(*lead, slice(None), pl.ds(first, w))]

        def into(j):
            whole = self.held(stream, phase)
            return whole.at[j] if phase in (0, 2) else whole

        count = 2 if phase in (0, 2) else 1
        send = self.links.send
        return [send(lambda j=j: source(j), lambda j=j: into(j), name) for j in range(count)]

    def finish(self, stream, phase):
        place, spot, bufs = self.links.place, self.spot, self.bufs
        source_ref, first, w, _, _, order, out_first = self.streams[stream]
        order = ORDERS[order]
        every = slice(None)
        for copy in self.flying[stream]:
            copy.wait_recv()
        if phase == 4:
            mine = bufs[spot(stream, 3, 2, span(place.x, 32))].astype(F32)
            columns = pl.ds(out_first, w)
            self.out[:, columns] = bufs[spot(stream, 3, 3, pl.ds(0, 32))].astype(F32) + mine
        elif phase == 3:
            bufs[spot(stream, 3, 2, every)] += bufs[spot(stream, 3, 0, every)]
        elif phase == 1:
            for k in range(4):
                bufs[spot(stream, 2, k, every)] += bufs[spot(stream, 0, k, every)]
        else:
            name = order[phase]
            mine = place.y if name[0] == "y" else place.z
            for j, own in enumerate((mine, step_of(order[phase + 1], mine))):
                if phase == 2:
                    bufs[spot(stream, 3, j, every)] += bufs[spot(stream, 2, own, every)]
                    continue
                for k in range(4):
                    lead = (k, own) if name[0] == "y" else (own, k)
                    kept = source_ref[(*lead, every, pl.ds(first, w))]
                    bufs[spot(stream, j, k, every)] += kept

    def start(self, *streams):
        for stream in streams:
            self.flying[stream] = self.begin(stream, 0)
            self.phases[stream] = 0

    def advance(self, *streams):
        for stream in streams or range(len(self.streams)):
            phase = self.phases[stream]
            if phase == 5:
                continue
            self.finish(stream, phase)
            self.sent += self.flying[stream]
            if phase < 4:
                self.flying[stream] = self.begin(stream, phase + 1)
            self.phases[stream] = phase + 1

    def drain(self):
        for copy in self.sent:
            copy.wait_send()


class GainSum:
    def __init__(self, links, own, parts):
        self.links, self.parts, self.copies, self.step = links, parts, [], 0
        self.begin(own[...])

    def begin(self, values):
        place, name = self.links.place, GAIN_ORDER[self.step]
        mine = place.along(name)
        half = self.parts.at[self.step, mine]
        self.parts[self.step, mine] = values
        count = 2 if name == "x" else 4
        self.copies.append([self.links.send(lambda: half, lambda: half, (name, k)) for k in range(1, count)])

    def advance(self):
        if self.step == 4:
            return
        for copy in self.copies[self.step]:
            copy.wait_recv()
        parts = [self.parts[self.step, k] for k in range(len(self.copies[self.step]) + 1)]
        total = parts[0] + parts[1]
        if len(parts) == 4:
            total = total + (parts[2] + parts[3])
        self.step += 1
        if self.step < 4:
            self.begin(total)
        else:
            self.total = total

    def drain(self):
        for copies in self.copies:
            for copy in copies:
                copy.wait_send()


def head_forward(raw, gain, cosine, sine):
    root = lax.rsqrt(jnp.mean(raw * raw, axis=0, keepdims=True) + EPSILON)
    normed = raw * root
    scaled = normed * gain
    first, second = scaled[:64], scaled[64:]
    turned = jnp.concatenate([first * cosine - second * sine, second * cosine + first * sine], axis=0)
    return normed, root, turned


def head_backward(grad, normed, root, gain, cosine, sine):
    first, second = grad[:64], grad[64:]
    turned = jnp.concatenate([first * cosine + second * sine, second * cosine - first * sine], axis=0)
    scaled = turned * gain
    inner = jnp.mean(scaled * normed, axis=0, keepdims=True)
    return root * (scaled - normed * inner), turned * normed


def layer_kernel(
    x, starts, dy, wq, wk, wv, wo, wg, wu, wd, g1, g2, gq, gk, frequency,
    out, grad_x, out_sums, out_gains,
    *scratch,
):
    s = Box()
    for (name, _, _), ref in zip(SCRATCH, scratch):
        setattr(s, name, ref)
    s.keep_far, s.keep_own = s.keep.at[0], s.keep.at[1]
    link_sems, load_sems, ready = scratch[len(SCRATCH) :]
    place = Place()
    links = Links(place, link_sems)
    me, sib, across, across_sib = place.me, place.sib, place.across, place.across_sib

    barrier = pltpu.get_barrier_semaphore()
    for name in PARTNERS + DIAGONALS:
        pl.semaphore_signal(barrier, inc=1, device_id=place.device(name), device_id_type=MESH)

    loads = []

    def load(src, dst):
        copy = pltpu.make_async_copy(src, dst, load_sems.at[len(loads)])
        copy.start()
        loads.append(copy)

    load(x, s.x_in)
    load(g1, s.g1_in)
    for g in range(2):
        load(wq.at[:, pl.ds(256 * g, 256)], s.w_qkv.at[:, pl.ds(512 * g, 256)])
        load(wk.at[:, pl.ds(128 * g, 128)], s.w_qkv.at[:, pl.ds(512 * g + 256, 128)])
        load(wv.at[:, pl.ds(128 * g, 128)], s.w_qkv.at[:, pl.ds(512 * g + 384, 128)])
    load(wo, s.h2.at[pl.ds(0, 512)])
    load(wg, s.mlp_mix.at[:, :, :, pl.ds(0, 768)])
    load(wu, s.mlp_mix.at[:, :, :, pl.ds(768, 768)])
    load(wd, s.w_down)
    load(dy, s.da.at[pl.ds(0, 256)])
    load(g2, s.g2_in)
    load(gq, s.gq_in)
    load(gk, s.gk_in)
    load(frequency, s.frequency)

    near_pair, far_pair = (sib, me), (across_sib, across)

    def pair(ref, rows, blocks, part):
        return jnp.concatenate([ref[rows, sub(b, part)] for b in blocks], axis=1)

    def unpair(ref, rows, blocks, part, values):
        for n, b in enumerate(blocks):
            ref[rows, sub(b, part)] = values[:, HALF * n : HALF * n + HALF]

    every = pl.ds(0, 1024)

    loads[0].wait()
    loads[1].wait()
    gather_h1 = Gather(links, lambda b, part: s.h1.at[:, sub(b, part)])
    for part in range(2):

        def first_norm(i, part=part):
            rows = span(2 * part + i, 64)
            xs = s.x_in[rows, :].astype(F32)
            root = lax.rsqrt(jnp.mean(xs * xs, axis=1, keepdims=True) + EPSILON)
            s.stage[rows, :] = (xs * root * s.g1_in[...]).astype(BF16)

        loop(2, first_norm)
        for j in range(4):
            s.h1[pl.ds(256 * j, 256), sub(me, part)] = s.stage[lanes(part), pl.ds(256 * j, 256)].T
        if part == 0:
            pl.semaphore_wait(barrier, len(PARTNERS) + len(DIAGONALS))
        gather_h1.send(part)

    for k in range(2, 8):
        loads[k].wait()

    def turn_qkv(i):
        s.t_qkv[span(i), :] = s.w_qkv[:, span(i)].T

    loop(4, turn_qkv)

    for k in range(13, 17):
        loads[k].wait()
    place_row = lax.broadcasted_iota(jnp.int32, (8, 1024), 1)
    start_row = jnp.zeros((8, 1024), jnp.int32)
    for d in range(4):
        start_row = jnp.maximum(start_row, jnp.where(place_row >= starts[0, d], starts[0, d], 0))
    position = (place_row - start_row).astype(F32)
    for i in range(8):
        columns = pl.ds(128 * i, 128)
        angle = s.frequency[...] * position[0:1, 128 * i : 128 * i + 128]
        s.cosine[:, columns] = jnp.cos(angle)
        s.sine[:, columns] = jnp.sin(angle)
    for qb in range(4):
        first = start_row[0:1, qb * 256 : qb * 256 + 256]
        query = lax.broadcasted_iota(jnp.int32, (256, 256), 1) + qb * 256
        for kb in range(qb + 1):
            key = lax.broadcasted_iota(jnp.int32, (256, 256), 0) + kb * 256
            allowed = (key <= query) & (key >= first)
            s.dgu[pl.ds(256 * kb, 256), pl.ds(256 * qb, 256)] = jnp.where(allowed, 1.0, 0.0).astype(BF16)

    s.gain1[...] = jnp.broadcast_to(s.g1_in[...], (128, 1024)).T
    s.gain2[...] = jnp.broadcast_to(s.g2_in[...], (128, 1024)).T
    s.gain_q[...] = jnp.broadcast_to(s.gq_in[...], (128, 128)).T
    s.gain_k[...] = jnp.broadcast_to(s.gk_in[...], (128, 128)).T
    s.gain_q_sum[...] = jnp.zeros((128, 128), F32)
    s.gain_sum[...] = jnp.zeros((1024, 128), F32)
    s.gain_k_sum[...] = jnp.zeros((128, 256), F32)
    for g in range(2):
        s.v_t[g, pl.ds(128, 16), :] = jnp.ones((16, 1024), BF16)

    def x_in(i, total):
        turned = s.x_in[:, span(i)].astype(F32).T
        s.x_t[span(i), :] = turned.astype(BF16)
        return total + fold(turned * turned)

    square = lax.fori_loop(0, 4, x_in, jnp.zeros((8, BLOCK), F32))
    root = lax.rsqrt(jnp.sum(square, axis=0, keepdims=True) / 1024.0 + EPSILON)
    s.root1[...] = jnp.broadcast_to(root, (8, BLOCK))

    loads[8].wait()

    def turn_out(i):
        s.attn_mix[i, :, :, pl.ds(1024, 512)] = s.h2[pl.ds(0, 512), span(i)].T.reshape(4, 64, 512)

    loop(4, turn_out)
    loads[9].wait()
    loads[10].wait()

    def turn_gu(i):
        for z in range(4):
            turned = s.mlp_mix[z, :, :, span(i)].reshape(256, 256).T
            s.t_gu[i, :, :, pl.ds(256 * z, 256)] = turned.reshape(4, 64, 256)

    loop(6, turn_gu)
    loads[11].wait()

    def turn_down(i):
        s.mlp_mix[i, :, :, pl.ds(1536, 768)] = s.w_down[:, span(i)].T.reshape(4, 64, 768)

    loop(4, turn_down)

    def dy_in(i):
        s.attn_mix[i, :, :, span(me)] = s.da[pl.ds(0, 256), span(i)].T.reshape(4, 64, BLOCK)

    loads[12].wait()
    loop(4, dy_in)

    def project(blocks, part):
        cosine, sine = pair(s.cosine, pl.ds(0, 64), blocks, part), pair(s.sine, pl.ds(0, 64), blocks, part)
        query_gain = twice(s.gain_q[...] * QUERY_SCALE)
        key_gain = twice(s.gain_k[...])
        every_raw = nn(s.t_qkv[...], pair(s.h1, every, blocks, part))
        for g in range(2):
            raw = every_raw[512 * g : 512 * g + 512]
            for k in range(2):
                head = 3 * g + k
                normed, root, turned = head_forward(raw[128 * k : 128 * k + 128], query_gain, cosine, sine)
                unpair(s.norm_qk, pl.ds(128 * head, 128), blocks, part, normed.astype(BF16))
                unpair(s.root_qk, pl.ds(head, 1), blocks, part, root)
                turned = turned.astype(BF16)
                for n, b in enumerate(blocks):
                    s.qs[g, b, :, lanes(2 * part + k)] = turned[:, HALF * n : HALF * n + HALF]
            normed, root, turned = head_forward(raw[256:384], key_gain, cosine, sine)
            turned, values = turned.astype(BF16), raw[384:].astype(BF16)
            unpair(s.norm_qk, pl.ds(384 * g + 256, 128), blocks, part, normed.astype(BF16))
            unpair(s.root_qk, pl.ds(3 * g + 2, 1), blocks, part, root)
            unpair(s.ks_t, pl.ds(128 * g, 128), blocks, part, turned)
            for n, b in enumerate(blocks):
                s.v_t[g, pl.ds(0, 128), sub(b, part)] = values[:, HALF * n : HALF * n + HALF]
                s.ks[g, sub(b, part), :] = turned[:, HALF * n : HALF * n + HALF].T
                s.v[g, sub(b, part), :] = values[:, HALF * n : HALF * n + HALF].T

    def both_roles(own, body):
        for far in range(2):
            blocks = (2 * far, 2 * far + 1) if own else (2 - 2 * far, 3 - 2 * far)
            pl.when(place.far == far)(lambda blocks=blocks: body(blocks))

    def p_slots(g, qb):
        return pl.ds(g * 10 + qb * (qb + 1) // 2, qb + 1)

    def attend(blocks, parts):
        wide = 256 * len(parts)
        cut = lanes(parts[0], 256) if len(parts) == 1 else pl.ds(0, wide)
        chains = [(qb, g, 256 * (qb + 1)) for qb in blocks for g in range(2)]
        scores = [nn(s.ks[g, pl.ds(0, keys), :], s.qs[g, qb, :, cut]) for qb, g, keys in chains]
        weights = []
        for (qb, g, keys), score in zip(chains, scores):
            halves = [twice(s.dgu[pl.ds(0, keys), lanes(2 * qb + part)]) for part in parts]
            mask = halves[0] if len(parts) == 1 else jnp.concatenate(halves, axis=1)
            weights.append(jnp.exp2(score).astype(BF16) * mask)
        products = [nn(s.v_t[g, :, pl.ds(0, keys)], weight) for (qb, g, keys), weight in zip(chains, weights)]
        for (qb, g, keys), weight, product in zip(chains, weights, products):
            s.p[p_slots(g, qb), :, :, cut] = weight.reshape(qb + 1, 4, 64, wide)
            inverse = 1.0 / product[128:136]
            s.inv[g, qb, :, cut] = inverse
            attended = (product[:128] * inverse[0:1]).astype(BF16)
            for n, part in enumerate(parts):
                for k in range(2):
                    columns = slice(256 * n + 128 * k, 256 * n + 128 * k + 128)
                    s.ob[pl.ds(256 * g + 128 * k, 128), lanes(2 * qb + part)] = attended[:, columns]

    def out_product(blocks, part, store):
        attended = pair(s.ob, pl.ds(0, 512), blocks, part)
        store(nn(s.attn_mix[:, :, :, pl.ds(1024, 512)].reshape(1024, 512), attended))

    def split(sib_out, index, part, keep):
        def store(values):
            sib_out[index, part] = values[:, :HALF].astype(BF16)
            keep[:, lanes(part)] = values[:, HALF:]

        return store

    gather_dy = Gather(links, lambda b, part: s.attn_mix.at[:, :, :, sub(b, part)])

    def choose(far):
        return tuple(jnp.where(far, b, a) for a, b in zip(near_pair, far_pair))

    def project_step(k, when):
        when(0, lambda: gather_h1.near_ready(0))
        when(1, lambda: gather_h1.near_ready(1))

        def third():
            gather_h1.pass_on(0)
            gather_h1.far_ready(0)

        when(2, third)

        def fourth():
            gather_h1.pass_on(1)
            for part in range(2):
                gather_dy.send_near(part)
            gather_dy.send_far(0)
            gather_h1.far_ready(1)

        when(3, fourth)
        project(choose(k >= 2), k % 2)

    steps(4, project_step)

    sum_attn = Reduce(links, s.sib_out, s.sib_in, s.far_out, s.far_in)

    def attend_step(k, when):
        both_roles(False, lambda blocks: attend(blocks, (k,)))

        def second():
            sum_attn.make_far(s.keep_far, 0)
            sum_attn.send_far(0)

        when(1, second)
        out_product(far_pair, k, split(s.sib_out, 0, k, s.keep_far))
        when(0, lambda: sum_attn.to_sibling(0, 0))
        when(1, lambda: sum_attn.to_sibling(0, 1))

    steps(2, attend_step)
    both_roles(True, lambda blocks: attend(blocks, (0, 1)))
    sum_attn.make_far(s.keep_far, 1)
    sum_attn.send_far(1)
    loop(2, lambda part: out_product(near_pair, part, split(s.sib_out, 1, part, s.keep_own)))
    for part in range(2):
        sum_attn.to_sibling(1, part)
    for part in range(2):
        gather_dy.near_ready(part)
    gather_dy.pass_on(0)

    gather_h2 = Gather(links, lambda b, part: s.h2.at[:, sub(b, part)])

    def second_norm(part):
        sum_attn.arrive(part)

        def square(i, total):
            x1 = s.x_t[span(i), lanes(part)].astype(F32) + sum_attn.total(s.keep_own, part, span(i))
            s.resid[span(i), lanes(part)] = x1
            return total + fold(x1 * x1)

        total = lax.fori_loop(0, 4, square, jnp.zeros((8, HALF), F32))
        root = lax.rsqrt(jnp.sum(total, axis=0, keepdims=True) / 1024.0 + EPSILON)
        s.root2[:, lanes(part)] = jnp.broadcast_to(root, (8, HALF))

        def scale(i):
            normed = s.resid[span(i), lanes(part)] * s.root2[0:1, lanes(part)]
            s.h2[span(i), sub(me, part)] = (normed * s.gain2[span(i), :]).astype(BF16)

        loop(4, scale)
        gather_h2.send(part)

    def feed(blocks, part):
        def body(j):
            gate = nn(s.t_gu[j].reshape(256, 1024), pair(s.h2, every, blocks, part))
            up = nn(s.t_gu[3 + j].reshape(256, 1024), pair(s.h2, every, blocks, part))
            grads = [s.attn_mix[:, :, :, sub(b, part)].reshape(1024, HALF) for b in blocks]
            grad = nn(s.w_down[span(j), :], jnp.concatenate(grads, axis=1))
            open_gate = jax.nn.sigmoid(gate)
            silu = gate * open_gate
            unpair(s.hidden, span(j), blocks, part, (silu * up).astype(BF16))
            dgate = (grad * up * open_gate * (1.0 + gate * (1.0 - open_gate))).astype(BF16)
            unpair(s.dgu, span(j), blocks, part, dgate)
            unpair(s.dgu, span(3 + j), blocks, part, (grad * silu).astype(BF16))

        for j in range(3):
            body(j)

    def feed_back(blocks, part, store):
        grads = pair(s.dgu, pl.ds(0, 1536), blocks, part)
        store(nn(s.mlp_mix[:, :, :, pl.ds(0, 1536)].reshape(1024, 1536), grads))

    def mlp_product(blocks, part, store):
        hidden = pair(s.hidden, pl.ds(0, 768), blocks, part)
        store(nn(s.mlp_mix[:, :, :, pl.ds(1536, 768)].reshape(1024, 768), hidden))

    sum_dh2 = Reduce(links, s.sib_out, s.sib_in, s.far_out, s.far_in)

    def feed_step(k, when):
        def first():
            second_norm(0)
            sum_attn.release(1, 0)
            gather_h2.near_ready(0)

        when(0, first)

        def second():
            second_norm(1)
            sum_attn.drain()
            gather_h2.pass_on(0)
            gather_h2.near_ready(1)

        when(1, second)

        def third():
            gather_dy.far_ready(0)
            gather_h2.far_ready(0)

        when(2, third)

        def fourth():
            gather_h2.pass_on(1)
            gather_dy.pass_on(1)
            gather_h2.far_ready(1)
            gather_dy.far_ready(1)

        when(3, fourth)
        far, part = k >= 2, k % 2
        feed(choose(far), part)
        index = 1 - k // 2
        feed_back(choose(far), part, split(s.sib_out, index, part, s.keep.at[index]))
        when(0, lambda: sum_dh2.to_sibling(1, 0))

        def second_end():
            sum_dh2.to_sibling(1, 1)
            gather_dy.send_far(1)

        when(1, second_end)

        def third_end():
            sum_dh2.to_sibling(0, 0)
            sum_dh2.make_far(s.keep_far, 0)
            sum_dh2.send_far(0)

        when(2, third_end)
        when(3, lambda: sum_dh2.to_sibling(0, 1))

    steps(4, feed_step)

    dp_mlp = DpSum(links, s, MLP_STREAMS, s.mlp_halves)

    def feed_grad(stream):
        name, first, w, _, _, _, _ = MLP_STREAMS[stream]
        if name == "mlp_mix":
            values = nt(s.h2[...], s.dgu[pl.ds(first, w), :])
        else:
            values = nt(s.attn_mix[:, :, :, pl.ds(0, 1024)].reshape(1024, 1024), s.hidden[pl.ds(first, w), :])
        into = getattr(s, name)
        into[pl.ds(0, 4), :, :, pl.ds(first, w)] = values.astype(BF16).reshape(4, 4, 64, w)
        dp_mlp.start(stream)

    gather_da = Gather(links, lambda b, part: s.da.at[:, sub(b, part)])

    def norm_back(part):
        sum_dh2.arrive(part)

        def inner_sum(i, total):
            grad = sum_dh2.total(s.keep_own, part, span(i))
            s.keep_own[span(i), lanes(part)] = grad
            product = grad * (s.resid[span(i), lanes(part)] * s.root2[0:1, lanes(part)])
            s.gain_sum[span(i), :] += product
            return total + fold(product * s.gain2[span(i), :])

        inner = lax.fori_loop(0, 4, inner_sum, jnp.zeros((8, HALF), F32))
        inner = jnp.sum(inner, axis=0, keepdims=True) / 1024.0

        def body(i):
            root = s.root2[0:1, lanes(part)]
            scaled = s.keep_own[span(i), lanes(part)] * s.gain2[span(i), :]
            normed = s.resid[span(i), lanes(part)] * root
            own = s.attn_mix[i, :, :, sub(me, part)].reshape(256, HALF).astype(F32)
            s.da[span(i), sub(me, part)] = (own + root * (scaled - normed * inner)).astype(BF16)
            s.mlp_own[span(i), lanes(part)] = s.resid[span(i), lanes(part)]
            s.resid[span(i), lanes(part)] = own + root * (scaled - normed * inner)

        loop(4, body)
        gather_da.send(part)

    feed_grad(0)
    sum_dh2.make_far(s.keep_far, 1)
    sum_dh2.send_far(1)
    feed_grad(1)
    norm_back(0)
    feed_grad(4)
    feed_grad(2)
    feed_grad(3)
    gather_h2.drain()
    load(wo, s.h2.at[pl.ds(0, 512)])
    norm_back(1)
    sum_dh2.drain()

    def put_gain(first, row):
        for k in range(row.shape[1] // 128):
            s.gain_own[first + k : first + k + 1, :] = row[:, 128 * k : 128 * k + 128]

    put_gain(8, jnp.sum(s.gain_sum[...].T, axis=0, keepdims=True))
    s.gain_sum[...] = jnp.zeros((1024, 128), F32)

    sum_mlp = Reduce(links, s.mlp_sib_out, s.mlp_sib_in, s.mlp_far_out, s.mlp_far_in)

    def mlp_mine(part):
        def store(values):
            s.mlp_sib_out[1, part] = values[:, :HALF].astype(BF16)
            s.mlp_own[:, lanes(part)] += values[:, HALF:]

        return store

    loop(2, lambda part: mlp_product(far_pair, part, split(s.mlp_sib_out, 0, part, s.keep_far)))
    for part in range(2):
        sum_mlp.to_sibling(0, part)
    for part in range(2):
        sum_mlp.make_far(s.keep_far, part)

    s.keep[...] = jnp.zeros((2, 1024, 256), F32)
    loads[17].wait()

    def dob(g, b, part):
        index = g * 4 + b
        return (4 + index // 4, pl.ds(2 * ((index // 2) % 2), 2), slice(None), pl.ds(pl.multiple_of((index % 2) * 512 + part * 256, 256), 256))

    def out_back(blocks, part):
        two = lanes(part, 256)
        every_grad = nn(s.h2[pl.ds(0, 512), :], pair(s.da, every, blocks, part))
        for g in range(2):
            grads = every_grad[256 * g : 256 * g + 256]
            for n, b in enumerate(blocks):
                columns = slice(HALF * n, HALF * n + HALF)
                both = jnp.concatenate([grads[:128, columns], grads[128:, columns]], axis=1) * s.inv[g, b, 0:1, two]
                outs = [s.ob[pl.ds(256 * g + 128 * k, 128), sub(b, part)] for k in range(2)]
                inner = jnp.sum(both * jnp.concatenate(outs, axis=1).astype(F32), axis=0, keepdims=True)
                s.inner[g, b, :, two] = jnp.broadcast_to(inner, (8, 256))
                s.t_gu[dob(g, b, part)] = both.astype(BF16).reshape(2, 64, 256)

    def attend_back(blocks, parts, groups):
        wide = 256 * len(parts)
        cut = lanes(parts[0], 256) if len(parts) == 1 else pl.ds(0, wide)
        chains = [(qb, g, 256 * (qb + 1)) for qb in blocks for g in groups]
        grads, weights, slopes, changes, key_parts, query_parts, value_parts = [], [], [], [], [], [], []
        for qb, g, keys in chains:
            index = g * 4 + qb
            columns = lanes((index % 2) * 2 + parts[0], 256) if len(parts) == 1 else lanes(index % 2, 512)
            at = (4 + index // 4, pl.ds(2 * ((index // 2) % 2), 2), slice(None), columns)
            grads.append(s.t_gu[at].reshape(128, wide))
            weights.append(s.p[p_slots(g, qb), :, :, cut].reshape(keys, wide))
        for (qb, g, keys), grad in zip(chains, grads):
            slopes.append(nn(s.v[g, pl.ds(0, keys), :], grad))
        for weight, grad in zip(weights, grads):
            value_parts.append(nt(weight, grad))
        for (qb, g, keys), weight, slope in zip(chains, weights, slopes):
            changes.append((weight.astype(F32) * (slope - s.inner[g, qb, 0:1, cut])).astype(BF16))
        for (qb, g, keys), change in zip(chains, changes):
            key_parts.append(nt(change, s.qs[g, qb, :, cut]))
            query_parts.append(nn(s.ks_t[pl.ds(128 * g, 128), pl.ds(0, keys)], change))
        for (qb, g, keys), value_part, key_part, query_part in zip(chains, value_parts, key_parts, query_parts):
            s.keep_own[pl.ds(0, keys), lanes(g)] += value_part
            s.keep_far[pl.ds(0, keys), lanes(g)] += key_part
            for n, part in enumerate(parts):
                columns = lanes(2 * qb + part)
                for k in range(2):
                    head = 3 * g + k
                    grad, gain_part = head_backward(
                        query_part[:, 256 * n + 128 * k : 256 * n + 128 * k + 128] * (1.0 / math.sqrt(HEAD)),
                        s.norm_qk[pl.ds(128 * head, 128), columns].astype(F32),
                        s.root_qk[pl.ds(head, 1), columns],
                        s.gain_q[...],
                        s.cosine[:, columns],
                        s.sine[:, columns],
                    )
                    s.t_qkv[pl.ds(512 * g + 128 * k, 128), columns] = grad.astype(BF16)
                    s.gain_q_sum[...] += gain_part

    def key_back(g):
        gain = twice(s.gain_k[...])

        def body(b):
            columns = span(b)
            grad, gain_part = head_backward(
                s.keep_far[columns, lanes(g)].T * math.log(2.0),
                s.norm_qk[pl.ds(384 * g + 256, 128), columns].astype(F32),
                s.root_qk[pl.ds(3 * g + 2, 1), columns],
                gain,
                s.cosine[:, columns],
                s.sine[:, columns],
            )
            s.t_qkv[pl.ds(512 * g + 256, 128), columns] = grad.astype(BF16)
            s.gain_k_sum[...] += gain_part
            s.t_qkv[pl.ds(512 * g + 384, 128), columns] = s.keep_own[columns, lanes(g)].T.astype(BF16)

        loop(4, body)

    def tell_ready():
        for k, name in enumerate(PARTNERS[2:]):
            pl.semaphore_signal(ready.at[k], inc=1, device_id=place.device(name), device_id_type=MESH)

    def wait_ready():
        for k in range(5):
            pl.semaphore_wait(ready.at[k], 1)

    def qkv_grad(g):
        values = nt(s.h1[...], s.t_qkv[span(g, 512), :]).astype(BF16)
        s.attn_mix[:, :, :, span(g, 512)] = values.reshape(4, 4, 64, 512)

    def out_grad():
        values = nt(s.da[...], s.ob[...]).astype(BF16)
        s.attn_mix[:, :, :, pl.ds(1024, 512)] = values.reshape(4, 4, 64, 512)

    for part in range(2):
        gather_da.near_ready(part)
    loop(2, lambda part: out_back(near_pair, part))
    gather_da.pass_on(0)
    both_roles(True, lambda blocks: attend_back(blocks, (0, 1), (0, 1)))
    gather_dy.drain()

    def back_step(k, when):
        when(0, lambda: gather_da.far_ready(0))
        when(1, lambda: gather_da.far_ready(1))
        out_back(far_pair, k)

        def first():
            gather_da.pass_on(1)
            sum_mlp.send_far(0)

        when(0, first)
        when(1, dp_mlp.advance)
        both_roles(False, lambda blocks: attend_back(blocks, (k,), (0, 1)))

    steps(2, back_step)
    tell_ready()
    out_grad()
    key_back(1)
    qkv_grad(1)
    wait_ready()
    dp_attn = DpSum(links, s, ATTN_STREAMS, s.p)
    dp_attn.start(0, 1, 2, 3)
    key_back(0)
    qkv_grad(0)
    dp_attn.start(4, 5, 6, 7)

    def in_back(blocks, part, store):
        values = nn(s.w_qkv[...], pair(s.t_qkv, every, blocks, part))
        product = values * pair(s.h1, every, blocks, part).astype(F32)
        s.gain_sum[...] += product[:, :HALF] + product[:, HALF:]
        store(values)

    sum_dh1 = Reduce(links, s.sib_out, s.sib_in, s.far_out, s.far_in)
    loop(2, lambda part: in_back(far_pair, part, split(s.sib_out, 0, part, s.keep_far)))
    for part in range(2):
        sum_dh1.to_sibling(0, part)
    for part in range(2):
        sum_dh1.make_far(s.keep_far, part)
        sum_dh1.send_far(part)
    sum_mlp.send_far(1)
    dp_mlp.advance()
    loop(2, lambda part: in_back(near_pair, part, split(s.sib_out, 1, part, s.keep_own)))
    for part in range(2):
        sum_dh1.to_sibling(1, part)
    loop(2, lambda part: mlp_product(near_pair, part, mlp_mine(part)))
    for part in range(2):
        sum_mlp.to_sibling(1, part)
    put_gain(0, jnp.sum((s.gain_sum[...] / s.gain1[...]).T, axis=0, keepdims=True))
    both = s.gain_k_sum[:, lanes(0)] + s.gain_k_sum[:, lanes(1)]
    put_gain(16, jnp.sum(s.gain_q_sum[...].T, axis=0, keepdims=True))
    put_gain(17, jnp.sum(both.T, axis=0, keepdims=True))
    s.gain_own[pl.ds(18, 6), :] = jnp.zeros((6, 128), F32)
    gains = GainSum(links, s.gain_own, s.gain_parts)
    dp_attn.advance()
    dp_mlp.advance()
    gains.advance()
    dp_attn.advance()
    dp_mlp.advance()
    gains.advance()

    for part in range(2):
        sum_dh1.arrive(part)

        def inner_sum(i, total, part=part):
            grad = sum_dh1.total(s.keep_own, part, span(i))
            s.keep_own[span(i), lanes(part)] = grad
            normed = s.x_t[span(i), lanes(part)].astype(F32) * s.root1[0:1, lanes(part)]
            return total + fold(grad * normed * s.gain1[span(i), :])

        inner = lax.fori_loop(0, 4, inner_sum, jnp.zeros((8, HALF), F32))
        inner = jnp.sum(inner, axis=0, keepdims=True) / 1024.0

        def last_back(i, part=part, inner=inner):
            root = s.root1[0:1, lanes(part)]
            scaled = s.keep_own[span(i), lanes(part)] * s.gain1[span(i), :]
            normed = s.x_t[span(i), lanes(part)].astype(F32) * root
            s.resid[span(i), lanes(part)] += root * (scaled - normed * inner)

        loop(4, last_back)
        if part == 0:
            dp_attn.advance()
            gains.advance()
    load(s.resid, grad_x)

    for part in range(2):
        sum_mlp.arrive(part)

        def layer_out(i, part=part):
            s.stage[lanes(part), span(i)] = sum_mlp.total(s.mlp_own, part, span(i)).T.astype(BF16)

        loop(4, layer_out)
    load(s.stage, out)
    while min(dp_attn.phases + dp_mlp.phases) < 5 or gains.step < 4:
        dp_attn.advance()
        gains.advance()
        dp_mlp.advance()
    load(s.sums, out_sums)
    s.gain_own[...] = gains.total
    load(s.gain_own, out_gains)

    for copy in loads[18:]:
        copy.wait()
    for exchange in (gather_h1, gather_da, sum_mlp, sum_dh1, dp_mlp, dp_attn, gains):
        exchange.drain()


def deliver_kernel(*refs):
    given, outs, held = refs[:4], refs[4:17], refs[17:21]
    turned, gain_rows, sems_in, sems_out = refs[21:]
    arrivals = {k: pltpu.make_async_copy(given[k], held[k], sems_in.at[k]) for k in (0, 2, 3)}
    pieces = []
    for i in range(4):
        rows = pl.ds(256 * i, 256)
        pieces.append(pltpu.make_async_copy(given[1].at[rows], held[1].at[rows], sems_in.at[4 + i]))
        pieces[i].start()
    for copy in arrivals.values():
        copy.start()
    started = []

    def send(src, dst):
        copy = pltpu.make_async_copy(src, dst, sems_out.at[len(started)])
        copy.start()
        started.append(copy)

    for i in range(4):
        columns = pl.ds(256 * i, 256)
        pieces[i].wait()
        turned[:, columns] = held[1][columns, :].T
        send(turned.at[:, columns], outs[1].at[:, columns])
    arrivals[3].wait()
    gain_rows[0] = held[3][16:17]
    gain_rows[1] = held[3][17:18]
    send(held[3].at[pl.ds(0, 8)], outs[9])
    send(held[3].at[pl.ds(8, 8)], outs[10])
    send(gain_rows.at[0], outs[11])
    send(gain_rows.at[1], outs[12])
    arrivals[2].wait()
    sums = held[2]
    for g in range(2):
        for out, first, width in ((outs[2], 0, 256), (outs[3], 256, 128), (outs[4], 384, 128)):
            send(sums.at[:, pl.ds(512 * g + first, width)], out.at[:, pl.ds(width * g, width)])
    for out, first, width in ((outs[5], 1024, 512), (outs[6], 1536, 768), (outs[7], 2304, 768), (outs[8], 3072, 768)):
        send(sums.at[:, pl.ds(first, width)], out)
    arrivals[0].wait()
    send(held[0], outs[0])
    for copy in started:
        copy.wait()


def shards(
    tokens,
    doc_starts,
    cotangent,
    w_query,
    key_matrix,
    value_matrix,
    w_out,
    w_gate,
    w_up,
    w_down,
    gain_attn,
    gain_mlp,
    gain_query,
    gain_key,
):
    frequency = ROPE_BASE ** (-(np.arange(64, dtype=np.float64) * 2.0) / HEAD)
    frequency = jnp.asarray(np.broadcast_to(frequency[:, None], (64, 128)).astype(np.float32))
    hbm = pl.BlockSpec(memory_space=pl.ANY)
    smem = pl.BlockSpec(memory_space=pltpu.SMEM)

    def shaped(*shape, kind=F32):
        return jax.ShapeDtypeStruct(shape, kind)

    gains = (shaped(8, 128), shaped(8, 128), shaped(1, 128), shaped(1, 128))
    given = (shaped(256, 1024, kind=BF16), shaped(1024, 256), shaped(32, 3840), shaped(24, 128))
    widths = (512, 256, 256, 512, 768, 768, 768)
    outs = pl.pallas_call(
        layer_kernel,
        out_shape=given,
        in_specs=[hbm, smem] + [hbm] * 13,
        out_specs=(hbm,) * 4,
        scratch_shapes=[pltpu.VMEM(shape, kind) for _, shape, kind in SCRATCH]
        + [
            pltpu.SemaphoreType.DMA((2, SEMAPHORES)),
            pltpu.SemaphoreType.DMA((24,)),
            pltpu.SemaphoreType.REGULAR((5,)),
        ],
        compiler_params=pltpu.CompilerParams(
            collective_id=0, has_side_effects=True, vmem_limit_bytes=64 * 2**20 - 2**16
        ),
        cost_estimate=pl.CostEstimate(flops=32 * 10**9, bytes_accessed=2**24, transcendentals=2**22),
        name="layer",
    )(
        tokens.reshape(256, 1024),
        doc_starts,
        cotangent.reshape(256, 1024),
        w_query,
        key_matrix,
        value_matrix,
        w_out,
        w_gate.reshape(4, 4, 64, 768),
        w_up.reshape(4, 4, 64, 768),
        w_down,
        gain_attn.reshape(1, 1024),
        gain_mlp.reshape(1, 1024),
        gain_query.reshape(1, 128),
        gain_key.reshape(1, 128),
        frequency,
    )
    outs = pl.pallas_call(
        deliver_kernel,
        out_shape=(given[0], shaped(256, 1024)) + tuple(shaped(32, width) for width in widths) + gains,
        in_specs=[hbm] * 4,
        out_specs=(hbm,) * 13,
        scratch_shapes=[pltpu.VMEM(one.shape, one.dtype) for one in given]
        + [
            pltpu.VMEM((256, 1024), F32),
            pltpu.VMEM((2, 1, 128), F32),
            pltpu.SemaphoreType.DMA((8,)),
            pltpu.SemaphoreType.DMA((20,)),
        ],
        name="deliver",
    )(*outs)
    return (
        outs[0].reshape(1, 256, 1024),
        outs[1].reshape(1, 256, 1024),
        *outs[2:5],
        outs[5].T,
        *outs[6:8],
        outs[8].T,
        *(gain.reshape(-1) for gain in outs[9:]),
    )


def solution(mesh):
    in_specs = (
        P("dp", "tensor", None),
        P("dp", None),
        P("dp", "tensor", None),
        P(None, "tensor"),
        P(None, "tensor"),
        P(None, "tensor"),
        P("tensor", None),
        P(None, "tensor"),
        P(None, "tensor"),
        P("tensor", None),
        P(),
        P(),
        P(),
        P(),
    )
    out_specs = (
        P("dp", "tensor", None),
        P("dp", "tensor", None),
        P("dp", "tensor"),
        P("dp", "tensor"),
        P("dp", "tensor"),
        P("tensor", "dp"),
        P("dp", "tensor"),
        P("dp", "tensor"),
        P("tensor", "dp"),
        P(),
        P(),
        P(),
        P(),
    )
    return jax.shard_map(shards, mesh=mesh, in_specs=in_specs, out_specs=out_specs, check_vma=False)
```

```python
import math

import jax
import jax.numpy as jnp
import numpy as np
from jax import lax
from jax.experimental import pallas as pl
from jax.experimental.pallas import tpu as pltpu
from jax.sharding import PartitionSpec as P

MESH = pl.DeviceIdType.MESH
BF16 = jnp.bfloat16
F32 = jnp.float32
EPSILON = 1e-06
ROPE_BASE = 1000000.0
BLOCK = 256
HALF = 128
HEAD = 128
QUERY_SCALE = math.log2(math.e) / math.sqrt(HEAD)
PARTNERS = ("core", "far", "y1", "y2", "z1", "z2", "x")
DIAGONALS = (("y", 2), ("z", 2), ("tensor", "far_core"))
ORDERS = (("y1", "y2", "z1", "z2"), ("y2", "y1", "z2", "z1"), ("z1", "z2", "y1", "y2"), ("z2", "z1", "y2", "y1"))
MLP_STREAMS = (
    ("mlp_mix", 0, 640, 0, 0, 0, 1536),
    ("mlp_mix", 640, 640, 4, 0, 1, 2176),
    ("mlp_mix", 1280, 256, 8, 0, 2, 2816),
    ("t_gu", 0, 256, 8, 256, 2, 3072),
    ("t_gu", 256, 512, 12, 0, 3, 3328),
)
ATTN_STREAMS = tuple(
    ("attn_mix", 512 + 256 * k, 256, 10 + 4 * (k // 2), 256 * (k % 2), k, 512 + 256 * k) for k in range(4)
) + tuple(("attn_mix", 128 * k, 128, 0, 128 * k, k, 128 * k) for k in range(4))
GAIN_ORDER = ("y", "z", "tensor", "x")

SCRATCH = (
    ("w_qkv", (1024, 1024), BF16),
    ("t_qkv", (1024, 1024), BF16),
    ("w_down", (768, 1024), BF16),
    ("t_gu", (6, 4, 64, 1024), BF16),
    ("mlp_mix", (4, 4, 64, 2304), BF16),
    ("attn_mix", (4, 4, 64, 1536), BF16),
    ("h1", (1024, 1024), BF16),
    ("h2", (1024, 1024), BF16),
    ("da", (1024, 1024), BF16),
    ("norm_qk", (768, 1024), BF16),
    ("root_qk", (8, 1024), F32),
    ("ob", (512, 1024), BF16),
    ("qs", (2, 4, 128, 512), BF16),
    ("ks_t", (256, 1024), BF16),
    ("ks", (2, 1024, 128), BF16),
    ("v_t", (2, 144, 1024), BF16),
    ("v", (2, 1024, 128), BF16),
    ("p", (20, 4, 64, 512), BF16),
    ("inv", (2, 4, 8, 512), F32),
    ("inner", (2, 4, 8, 512), F32),
    ("hidden", (768, 1024), BF16),
    ("dgu", (1536, 1024), BF16),
    ("cosine", (64, 1024), F32),
    ("sine", (64, 1024), F32),
    ("x_t", (1024, 256), BF16),
    ("resid", (1024, 256), F32),
    ("gain1", (1024, 128), F32),
    ("gain2", (1024, 128), F32),
    ("gain_q", (128, 128), F32),
    ("gain_k", (128, 128), F32),
    ("gain_sum", (1024, 128), F32),
    ("gain_q_sum", (128, 128), F32),
    ("gain_k_sum", (128, 256), F32),
    ("root1", (8, 256), F32),
    ("root2", (8, 256), F32),
    ("keep", (2, 1024, 256), F32),
    ("sib_out", (2, 2, 1024, 128), BF16),
    ("sib_in", (2, 2, 1024, 128), BF16),
    ("far_out", (2, 1024, 128), BF16),
    ("far_in", (2, 1024, 128), BF16),
    ("mlp_own", (1024, 256), F32),
    ("mlp_sib_out", (2, 2, 1024, 128), BF16),
    ("mlp_sib_in", (2, 2, 1024, 128), BF16),
    ("mlp_far_out", (2, 1024, 128), BF16),
    ("mlp_far_in", (2, 1024, 128), BF16),
    ("mlp_halves", (16, 4, 64, 640), BF16),
    ("sums", (32, 3840), F32),
    ("stage", (256, 1024), BF16),
    ("x_in", (256, 1024), BF16),
    ("g1_in", (1, 1024), F32),
    ("g2_in", (1, 1024), F32),
    ("gq_in", (1, 128), F32),
    ("gk_in", (1, 128), F32),
    ("frequency", (64, 128), F32),
    ("gain_own", (24, 128), F32),
    ("gain_parts", (4, 4, 24, 128), F32),
)
SEMAPHORES = 190


class Box:
    pass


class Place:
    def __init__(self):
        dp = lax.axis_index("dp")
        tensor = lax.axis_index("tensor")
        self.z, self.y, self.x = dp // 8, (dp // 2) % 4, dp % 2
        self.far, self.core = tensor // 2, tensor % 2
        self.me = tensor
        self.sib = self.far * 2 + 1 - self.core
        self.across = (1 - self.far) * 2 + self.core
        self.across_sib = (1 - self.far) * 2 + 1 - self.core

    def near(self, name):
        return step_of(name, self.y if name[0] == "y" else self.z)

    def along(self, name):
        return {"y": self.y, "z": self.z, "x": self.x, "tensor": self.me}[name]

    def device(self, name):
        z, y, x, far, core = self.z, self.y, self.x, self.far, self.core
        if isinstance(name, tuple):
            axis, steps = name
            if axis == "tensor":
                if steps == "far_core":
                    far, core = 1 - far, 1 - core
                else:
                    turned = (self.me + steps) % 4
                    far, core = turned // 2, turned % 2
            elif axis == "y":
                y = (y + steps) % 4
            elif axis == "z":
                z = (z + steps) % 4
            else:
                x = 1 - x
        elif name[0] == "y":
            y = self.near(name)
        elif name[0] == "z":
            z = self.near(name)
        elif name == "x":
            x = 1 - x
        elif name == "far":
            far = 1 - far
        else:
            core = 1 - core
        return ((z * 4 + y) * 2 + x, far * 2 + core)


def step_of(name, value):
    return value + 1 - 2 * (value % 2) if name[1] == "1" else 3 - value


def nn(left, right):
    return lax.dot_general(left, right, (((1,), (0,)), ((), ())), preferred_element_type=F32)


def nt(left, right):
    return lax.dot_general(left, right, (((1,), (1,)), ((), ())), preferred_element_type=F32)


def span(index, size=BLOCK):
    return pl.ds(pl.multiple_of(index * size, size), size)


def loop(count, body):
    def step(index, carry):
        body(index)
        return carry

    lax.fori_loop(0, count, step, 0)


def twice(values):
    return jnp.concatenate([values, values], axis=1)


def fold(values):
    return jnp.sum(values.reshape(values.shape[0] // 8, 8, values.shape[1]), axis=0)


def sub(block, part):
    return pl.ds(pl.multiple_of(block * BLOCK + part * HALF, HALF), HALF)


def lanes(part, size=128):
    return pl.ds(part * size if isinstance(part, int) else pl.multiple_of(part * size, size), size)


def steps(count, body):
    def step(index, carry):
        body(index, lambda k, act: pl.when(index == k)(act))
        return carry

    lax.fori_loop(0, count, step, 0)


class Copy:
    def __init__(self, links, src, dst, name, index):
        self.links, self.src, self.dst, self.name, self.index = links, src, dst, name, index

    def make(self):
        return pltpu.make_async_remote_copy(
            src_ref=self.src(),
            dst_ref=self.dst(),
            send_sem=self.links.sems.at[0, self.index],
            recv_sem=self.links.sems.at[1, self.index],
            device_id=self.links.place.device(self.name),
            device_id_type=MESH,
        )

    def start(self):
        self.make().start()

    def wait_recv(self):
        self.make().wait_recv()

    def wait_send(self):
        self.make().wait_send()


class Links:
    def __init__(self, place, sems):
        self.place, self.sems, self.used, self.sent = place, sems, 0, []

    def copy(self, src, dst, name):
        self.used += 1
        return Copy(self, src, dst, name, self.used - 1)

    def send(self, src, dst, name):
        copy = self.copy(src, dst, name)
        copy.start()
        return copy


class Gather:
    def __init__(self, links, at):
        place = links.place

        def copies(block, name):
            halves = [lambda part=part: at(block, part) for part in range(2)]
            return [links.copy(half, half, name) for half in halves]

        self.far, self.sib = copies(place.me, "far"), copies(place.me, "core")
        self.passed = copies(place.across, "core")

    def send_far(self, part):
        self.far[part].start()

    def send_near(self, part):
        self.sib[part].start()

    def send(self, part):
        self.send_far(part)
        self.send_near(part)

    def pass_on(self, part):
        self.far[part].wait_recv()
        self.passed[part].start()

    def near_ready(self, part):
        self.sib[part].wait_recv()

    def far_ready(self, part):
        self.passed[part].wait_recv()

    def drain(self):
        for copy in self.far + self.sib + self.passed:
            copy.wait_send()


class Reduce:
    def __init__(self, links, sib_out, sib_in, far_out, far_in):
        self.sib_in, self.far_out, self.far_in = sib_in, far_out, far_in
        self.copies = {}
        for part in range(2):
            for index in range(2):
                src = lambda at=(index, part): sib_out.at[at]
                dst = lambda at=(index, part): sib_in.at[at]
                self.copies[index, part] = links.copy(src, dst, "core")
            src, dst = lambda part=part: far_out.at[part], lambda part=part: far_in.at[part]
            self.copies[2, part] = links.copy(src, dst, "far")

    def to_sibling(self, index, part):
        self.copies[index, part].start()

    def make_far(self, keep, part):
        self.copies[0, part].wait_recv()

        def body(i):
            rows = span(i, 512)
            summed = keep[rows, lanes(part)] + self.sib_in[0, part, rows, :].astype(F32)
            self.far_out[part, rows, :] = summed.astype(BF16)

        loop(2, body)

    def send_far(self, part):
        self.copies[2, part].start()

    def arrive(self, part):
        self.copies[1, part].wait_recv()
        self.copies[2, part].wait_recv()

    def total(self, keep, part, rows):
        near = keep[rows, lanes(part)] + self.sib_in[1, part, rows, :].astype(F32)
        return near + self.far_in[part, rows, :].astype(F32)

    def release(self, index, part):
        self.copies.pop((index, part)).wait_send()

    def drain(self):
        for copy in self.copies.values():
            copy.wait_send()


class DpSum:
    def __init__(self, links, box, streams, bufs):
        self.links, self.bufs, self.out = links, bufs, box.sums
        self.streams = [(getattr(box, name), *rest) for name, *rest in streams]
        self.phases = [-1] * len(streams)
        self.flying = [[] for _ in streams]
        self.sent = []

    def spot(self, stream, slot, *rest):
        _, _, w, at, column, _, _ = self.streams[stream]
        lead = pl.ds(at + slot.start, slot.size) if isinstance(slot, pl.Slice) else at + slot
        return (lead, *rest, pl.ds(column, w))

    def held(self, stream, phase):
        every = slice(None)
        if phase == 0:
            spot = self.spot(stream, pl.ds(0, 2), every, every)
        elif phase == 1:
            spot = self.spot(stream, 2, every, every)
        elif phase == 2:
            spot = self.spot(stream, 3, pl.ds(0, 2), every)
        elif phase == 3:
            spot = self.spot(stream, 3, 2, every)
        else:
            spot = self.spot(stream, 3, 3, pl.ds(0, 32))
        return self.bufs.at[spot]

    def begin(self, stream, phase):
        place = self.links.place
        source_ref, first, w, _, _, order, _ = self.streams[stream]
        order = ORDERS[order]
        name = "x" if phase == 4 else order[phase]

        def other(j):
            there = place.near(name)
            return there if j == 0 else step_of(order[phase + 1], there)

        def source(j):
            if phase == 4:
                return self.bufs.at[self.spot(stream, 3, 2, span(1 - place.x, 32))]
            if phase in (1, 3):
                return self.held(stream, phase - 1).at[1]
            if phase == 2:
                return self.held(stream, 1).at[other(j)]
            lead = (pl.ds(0, 4), other(j)) if name[0] == "y" else (other(j), slice(None))
            return source_ref.at[(*lead, slice(None), pl.ds(first, w))]

        def into(j):
            whole = self.held(stream, phase)
            return whole.at[j] if phase in (0, 2) else whole

        count = 2 if phase in (0, 2) else 1
        send = self.links.send
        return [send(lambda j=j: source(j), lambda j=j: into(j), name) for j in range(count)]

    def finish(self, stream, phase):
        place, spot, bufs = self.links.place, self.spot, self.bufs
        source_ref, first, w, _, _, order, out_first = self.streams[stream]
        order = ORDERS[order]
        every = slice(None)
        for copy in self.flying[stream]:
            copy.wait_recv()
        if phase == 4:
            mine = bufs[spot(stream, 3, 2, span(place.x, 32))].astype(F32)
            columns = pl.ds(out_first, w)
            self.out[:, columns] = bufs[spot(stream, 3, 3, pl.ds(0, 32))].astype(F32) + mine
        elif phase == 3:
            bufs[spot(stream, 3, 2, every)] += bufs[spot(stream, 3, 0, every)]
        elif phase == 1:
            for k in range(4):
                bufs[spot(stream, 2, k, every)] += bufs[spot(stream, 0, k, every)]
        else:
            name = order[phase]
            mine = place.y if name[0] == "y" else place.z
            for j, own in enumerate((mine, step_of(order[phase + 1], mine))):
                if phase == 2:
                    bufs[spot(stream, 3, j, every)] += bufs[spot(stream, 2, own, every)]
                    continue
                for k in range(4):
                    lead = (k, own) if name[0] == "y" else (own, k)
                    kept = source_ref[(*lead, every, pl.ds(first, w))]
                    bufs[spot(stream, j, k, every)] += kept

    def start(self, *streams):
        for stream in streams:
            self.flying[stream] = self.begin(stream, 0)
            self.phases[stream] = 0

    def advance(self, *streams):
        for stream in streams or range(len(self.streams)):
            phase = self.phases[stream]
            if phase == 5:
                continue
            self.finish(stream, phase)
            self.sent += self.flying[stream]
            if phase < 4:
                self.flying[stream] = self.begin(stream, phase + 1)
            self.phases[stream] = phase + 1

    def drain(self):
        for copy in self.sent:
            copy.wait_send()


class GainSum:
    def __init__(self, links, own, parts):
        self.links, self.parts, self.copies, self.step = links, parts, [], 0
        self.begin(own[...])

    def begin(self, values):
        place, name = self.links.place, GAIN_ORDER[self.step]
        mine = place.along(name)
        half = self.parts.at[self.step, mine]
        self.parts[self.step, mine] = values
        count = 2 if name == "x" else 4
        self.copies.append([self.links.send(lambda: half, lambda: half, (name, k)) for k in range(1, count)])

    def advance(self):
        if self.step == 4:
            return
        for copy in self.copies[self.step]:
            copy.wait_recv()
        parts = [self.parts[self.step, k] for k in range(len(self.copies[self.step]) + 1)]
        total = parts[0] + parts[1]
        if len(parts) == 4:
            total = total + (parts[2] + parts[3])
        self.step += 1
        if self.step < 4:
            self.begin(total)
        else:
            self.total = total

    def drain(self):
        for copies in self.copies:
            for copy in copies:
                copy.wait_send()


def head_forward(raw, gain, cosine, sine):
    root = lax.rsqrt(jnp.mean(raw * raw, axis=0, keepdims=True) + EPSILON)
    normed = raw * root
    scaled = normed * gain
    first, second = scaled[:64], scaled[64:]
    turned = jnp.concatenate([first * cosine - second * sine, second * cosine + first * sine], axis=0)
    return normed, root, turned


def head_backward(grad, normed, root, gain, cosine, sine):
    first, second = grad[:64], grad[64:]
    turned = jnp.concatenate([first * cosine + second * sine, second * cosine - first * sine], axis=0)
    scaled = turned * gain
    inner = jnp.mean(scaled * normed, axis=0, keepdims=True)
    return root * (scaled - normed * inner), turned * normed


def layer_kernel(
    x, starts, dy, wq, wk, wv, wo, wg, wu, wd, g1, g2, gq, gk, frequency,
    out, grad_x, out_sums, out_gains,
    *scratch,
):
    s = Box()
    for (name, _, _), ref in zip(SCRATCH, scratch):
        setattr(s, name, ref)
    s.keep_far, s.keep_own = s.keep.at[0], s.keep.at[1]
    link_sems, load_sems, ready = scratch[len(SCRATCH) :]
    place = Place()
    links = Links(place, link_sems)
    me, sib, across, across_sib = place.me, place.sib, place.across, place.across_sib

    barrier = pltpu.get_barrier_semaphore()
    for name in PARTNERS + DIAGONALS:
        pl.semaphore_signal(barrier, inc=1, device_id=place.device(name), device_id_type=MESH)

    loads = []

    def load(src, dst):
        copy = pltpu.make_async_copy(src, dst, load_sems.at[len(loads)])
        copy.start()
        loads.append(copy)

    load(x, s.x_in)
    load(g1, s.g1_in)
    for g in range(2):
        load(wq.at[:, pl.ds(256 * g, 256)], s.w_qkv.at[:, pl.ds(512 * g, 256)])
        load(wk.at[:, pl.ds(128 * g, 128)], s.w_qkv.at[:, pl.ds(512 * g + 256, 128)])
        load(wv.at[:, pl.ds(128 * g, 128)], s.w_qkv.at[:, pl.ds(512 * g + 384, 128)])
    load(wo, s.h2.at[pl.ds(0, 512)])
    load(wg, s.mlp_mix.at[:, :, :, pl.ds(0, 768)])
    load(wu, s.mlp_mix.at[:, :, :, pl.ds(768, 768)])
    load(wd, s.w_down)
    load(dy, s.da.at[pl.ds(0, 256)])
    load(g2, s.g2_in)
    load(gq, s.gq_in)
    load(gk, s.gk_in)
    load(frequency, s.frequency)

    near_pair, far_pair = (sib, me), (across_sib, across)

    def pair(ref, rows, blocks, part):
        return jnp.concatenate([ref[rows, sub(b, part)] for b in blocks], axis=1)

    def unpair(ref, rows, blocks, part, values):
        for n, b in enumerate(blocks):
            ref[rows, sub(b, part)] = values[:, HALF * n : HALF * n + HALF]

    every = pl.ds(0, 1024)

    loads[0].wait()
    loads[1].wait()
    gather_h1 = Gather(links, lambda b, part: s.h1.at[:, sub(b, part)])
    for part in range(2):

        def first_norm(i, part=part):
            rows = span(2 * part + i, 64)
            xs = s.x_in[rows, :].astype(F32)
            root = lax.rsqrt(jnp.mean(xs * xs, axis=1, keepdims=True) + EPSILON)
            s.stage[rows, :] = (xs * root * s.g1_in[...]).astype(BF16)

        loop(2, first_norm)
        for j in range(4):
            s.h1[pl.ds(256 * j, 256), sub(me, part)] = s.stage[lanes(part), pl.ds(256 * j, 256)].T
        if part == 0:
            pl.semaphore_wait(barrier, len(PARTNERS) + len(DIAGONALS))
        gather_h1.send(part)

    for k in range(2, 8):
        loads[k].wait()

    def turn_qkv(i):
        s.t_qkv[span(i), :] = s.w_qkv[:, span(i)].T

    loop(4, turn_qkv)

    for k in range(13, 17):
        loads[k].wait()
    place_row = lax.broadcasted_iota(jnp.int32, (8, 1024), 1)
    start_row = jnp.zeros((8, 1024), jnp.int32)
    for d in range(4):
        start_row = jnp.maximum(start_row, jnp.where(place_row >= starts[0, d], starts[0, d], 0))
    position = (place_row - start_row).astype(F32)
    for i in range(8):
        columns = pl.ds(128 * i, 128)
        angle = s.frequency[...] * position[0:1, 128 * i : 128 * i + 128]
        s.cosine[:, columns] = jnp.cos(angle)
        s.sine[:, columns] = jnp.sin(angle)
    for qb in range(4):
        first = start_row[0:1, qb * 256 : qb * 256 + 256]
        query = lax.broadcasted_iota(jnp.int32, (256, 256), 1) + qb * 256
        for kb in range(qb + 1):
            key = lax.broadcasted_iota(jnp.int32, (256, 256), 0) + kb * 256
            allowed = (key <= query) & (key >= first)
            s.dgu[pl.ds(256 * kb, 256), pl.ds(256 * qb, 256)] = jnp.where(allowed, 1.0, 0.0).astype(BF16)

    s.gain1[...] = jnp.broadcast_to(s.g1_in[...], (128, 1024)).T
    s.gain2[...] = jnp.broadcast_to(s.g2_in[...], (128, 1024)).T
    s.gain_q[...] = jnp.broadcast_to(s.gq_in[...], (128, 128)).T
    s.gain_k[...] = jnp.broadcast_to(s.gk_in[...], (128, 128)).T
    s.gain_q_sum[...] = jnp.zeros((128, 128), F32)
    s.gain_sum[...] = jnp.zeros((1024, 128), F32)
    s.gain_k_sum[...] = jnp.zeros((128, 256), F32)
    for g in range(2):
        s.v_t[g, pl.ds(128, 16), :] = jnp.ones((16, 1024), BF16)

    def x_in(i, total):
        turned = s.x_in[:, span(i)].astype(F32).T
        s.x_t[span(i), :] = turned.astype(BF16)
        return total + fold(turned * turned)

    square = lax.fori_loop(0, 4, x_in, jnp.zeros((8, BLOCK), F32))
    root = lax.rsqrt(jnp.sum(square, axis=0, keepdims=True) / 1024.0 + EPSILON)
    s.root1[...] = jnp.broadcast_to(root, (8, BLOCK))

    loads[8].wait()

    def turn_out(i):
        s.attn_mix[i, :, :, pl.ds(1024, 512)] = s.h2[pl.ds(0, 512), span(i)].T.reshape(4, 64, 512)

    loop(4, turn_out)
    loads[9].wait()
    loads[10].wait()

    def turn_gu(i):
        for z in range(4):
            turned = s.mlp_mix[z, :, :, span(i)].reshape(256, 256).T
            s.t_gu[i, :, :, pl.ds(256 * z, 256)] = turned.reshape(4, 64, 256)

    loop(6, turn_gu)
    loads[11].wait()

    def turn_down(i):
        s.mlp_mix[i, :, :, pl.ds(1536, 768)] = s.w_down[:, span(i)].T.reshape(4, 64, 768)

    loop(4, turn_down)

    def dy_in(i):
        s.attn_mix[i, :, :, span(me)] = s.da[pl.ds(0, 256), span(i)].T.reshape(4, 64, BLOCK)

    loads[12].wait()
    loop(4, dy_in)

    def project(blocks, part):
        cosine, sine = pair(s.cosine, pl.ds(0, 64), blocks, part), pair(s.sine, pl.ds(0, 64), blocks, part)
        query_gain = twice(s.gain_q[...] * QUERY_SCALE)
        key_gain = twice(s.gain_k[...])
        every_raw = nn(s.t_qkv[...], pair(s.h1, every, blocks, part))
        for g in range(2):
            raw = every_raw[512 * g : 512 * g + 512]
            for k in range(2):
                head = 3 * g + k
                normed, root, turned = head_forward(raw[128 * k : 128 * k + 128], query_gain, cosine, sine)
                unpair(s.norm_qk, pl.ds(128 * head, 128), blocks, part, normed.astype(BF16))
                unpair(s.root_qk, pl.ds(head, 1), blocks, part, root)
                turned = turned.astype(BF16)
                for n, b in enumerate(blocks):
                    s.qs[g, b, :, lanes(2 * part + k)] = turned[:, HALF * n : HALF * n + HALF]
            normed, root, turned = head_forward(raw[256:384], key_gain, cosine, sine)
            turned, values = turned.astype(BF16), raw[384:].astype(BF16)
            unpair(s.norm_qk, pl.ds(384 * g + 256, 128), blocks, part, normed.astype(BF16))
            unpair(s.root_qk, pl.ds(3 * g + 2, 1), blocks, part, root)
            unpair(s.ks_t, pl.ds(128 * g, 128), blocks, part, turned)
            for n, b in enumerate(blocks):
                s.v_t[g, pl.ds(0, 128), sub(b, part)] = values[:, HALF * n : HALF * n + HALF]
                s.ks[g, sub(b, part), :] = turned[:, HALF * n : HALF * n + HALF].T
                s.v[g, sub(b, part), :] = values[:, HALF * n : HALF * n + HALF].T

    def both_roles(own, body):
        for far in range(2):
            blocks = (2 * far, 2 * far + 1) if own else (2 - 2 * far, 3 - 2 * far)
            pl.when(place.far == far)(lambda blocks=blocks: body(blocks))

    def p_slots(g, qb):
        return pl.ds(g * 10 + qb * (qb + 1) // 2, qb + 1)

    def attend(blocks, parts):
        wide = 256 * len(parts)
        cut = lanes(parts[0], 256) if len(parts) == 1 else pl.ds(0, wide)
        chains = [(qb, g, 256 * (qb + 1)) for qb in blocks for g in range(2)]
        scores = [nn(s.ks[g, pl.ds(0, keys), :], s.qs[g, qb, :, cut]) for qb, g, keys in chains]
        weights = []
        for (qb, g, keys), score in zip(chains, scores):
            halves = [twice(s.dgu[pl.ds(0, keys), lanes(2 * qb + part)]) for part in parts]
            mask = halves[0] if len(parts) == 1 else jnp.concatenate(halves, axis=1)
            weights.append(jnp.exp2(score).astype(BF16) * mask)
        products = [nn(s.v_t[g, :, pl.ds(0, keys)], weight) for (qb, g, keys), weight in zip(chains, weights)]
        for (qb, g, keys), weight, product in zip(chains, weights, products):
            s.p[p_slots(g, qb), :, :, cut] = weight.reshape(qb + 1, 4, 64, wide)
            inverse = 1.0 / product[128:136]
            s.inv[g, qb, :, cut] = inverse
            attended = (product[:128] * inverse[0:1]).astype(BF16)
            for n, part in enumerate(parts):
                for k in range(2):
                    columns = slice(256 * n + 128 * k, 256 * n + 128 * k + 128)
                    s.ob[pl.ds(256 * g + 128 * k, 128), lanes(2 * qb + part)] = attended[:, columns]

    def out_product(blocks, part, store):
        attended = pair(s.ob, pl.ds(0, 512), blocks, part)
        store(nn(s.attn_mix[:, :, :, pl.ds(1024, 512)].reshape(1024, 512), attended))

    def split(sib_out, index, part, keep):
        def store(values):
            sib_out[index, part] = values[:, :HALF].astype(BF16)
            keep[:, lanes(part)] = values[:, HALF:]

        return store

    gather_dy = Gather(links, lambda b, part: s.attn_mix.at[:, :, :, sub(b, part)])

    def choose(far):
        return tuple(jnp.where(far, b, a) for a, b in zip(near_pair, far_pair))

    def project_step(k, when):
        when(0, lambda: gather_h1.near_ready(0))
        when(1, lambda: gather_h1.near_ready(1))

        def third():
            gather_h1.pass_on(0)
            gather_h1.far_ready(0)

        when(2, third)

        def fourth():
            gather_h1.pass_on(1)
            for part in range(2):
                gather_dy.send_near(part)
            gather_dy.send_far(0)
            gather_h1.far_ready(1)

        when(3, fourth)
        project(choose(k >= 2), k % 2)

    steps(4, project_step)

    sum_attn = Reduce(links, s.sib_out, s.sib_in, s.far_out, s.far_in)

    def attend_step(k, when):
        both_roles(False, lambda blocks: attend(blocks, (k,)))

        def second():
            sum_attn.make_far(s.keep_far, 0)
            sum_attn.send_far(0)

        when(1, second)
        out_product(far_pair, k, split(s.sib_out, 0, k, s.keep_far))
        when(0, lambda: sum_attn.to_sibling(0, 0))
        when(1, lambda: sum_attn.to_sibling(0, 1))

    steps(2, attend_step)
    both_roles(True, lambda blocks: attend(blocks, (0, 1)))
    sum_attn.make_far(s.keep_far, 1)
    sum_attn.send_far(1)
    loop(2, lambda part: out_product(near_pair, part, split(s.sib_out, 1, part, s.keep_own)))
    for part in range(2):
        sum_attn.to_sibling(1, part)
    for part in range(2):
        gather_dy.near_ready(part)
    gather_dy.pass_on(0)

    gather_h2 = Gather(links, lambda b, part: s.h2.at[:, sub(b, part)])

    def second_norm(part):
        sum_attn.arrive(part)

        def square(i, total):
            x1 = s.x_t[span(i), lanes(part)].astype(F32) + sum_attn.total(s.keep_own, part, span(i))
            s.resid[span(i), lanes(part)] = x1
            return total + fold(x1 * x1)

        total = lax.fori_loop(0, 4, square, jnp.zeros((8, HALF), F32))
        root = lax.rsqrt(jnp.sum(total, axis=0, keepdims=True) / 1024.0 + EPSILON)
        s.root2[:, lanes(part)] = jnp.broadcast_to(root, (8, HALF))

        def scale(i):
            normed = s.resid[span(i), lanes(part)] * s.root2[0:1, lanes(part)]
            s.h2[span(i), sub(me, part)] = (normed * s.gain2[span(i), :]).astype(BF16)

        loop(4, scale)
        gather_h2.send(part)

    def feed(blocks, part):
        def body(j):
            gate = nn(s.t_gu[j].reshape(256, 1024), pair(s.h2, every, blocks, part))
            up = nn(s.t_gu[3 + j].reshape(256, 1024), pair(s.h2, every, blocks, part))
            grads = [s.attn_mix[:, :, :, sub(b, part)].reshape(1024, HALF) for b in blocks]
            grad = nn(s.w_down[span(j), :], jnp.concatenate(grads, axis=1))
            open_gate = jax.nn.sigmoid(gate)
            silu = gate * open_gate
            unpair(s.hidden, span(j), blocks, part, (silu * up).astype(BF16))
            dgate = (grad * up * open_gate * (1.0 + gate * (1.0 - open_gate))).astype(BF16)
            unpair(s.dgu, span(j), blocks, part, dgate)
            unpair(s.dgu, span(3 + j), blocks, part, (grad * silu).astype(BF16))

        for j in range(3):
            body(j)

    def feed_back(blocks, part, store):
        grads = pair(s.dgu, pl.ds(0, 1536), blocks, part)
        store(nn(s.mlp_mix[:, :, :, pl.ds(0, 1536)].reshape(1024, 1536), grads))

    def mlp_product(blocks, part, store):
        hidden = pair(s.hidden, pl.ds(0, 768), blocks, part)
        store(nn(s.mlp_mix[:, :, :, pl.ds(1536, 768)].reshape(1024, 768), hidden))

    sum_dh2 = Reduce(links, s.sib_out, s.sib_in, s.far_out, s.far_in)

    def feed_step(k, when):
        def first():
            second_norm(0)
            sum_attn.release(1, 0)
            gather_h2.near_ready(0)

        when(0, first)

        def second():
            second_norm(1)
            sum_attn.drain()
            gather_h2.pass_on(0)
            gather_h2.near_ready(1)

        when(1, second)

        def third():
            gather_dy.far_ready(0)
            gather_h2.far_ready(0)

        when(2, third)

        def fourth():
            gather_h2.pass_on(1)
            gather_dy.pass_on(1)
            gather_h2.far_ready(1)
            gather_dy.far_ready(1)

        when(3, fourth)
        far, part = k >= 2, k % 2
        feed(choose(far), part)
        index = 1 - k // 2
        feed_back(choose(far), part, split(s.sib_out, index, part, s.keep.at[index]))
        when(0, lambda: sum_dh2.to_sibling(1, 0))

        def second_end():
            sum_dh2.to_sibling(1, 1)
            gather_dy.send_far(1)

        when(1, second_end)

        def third_end():
            sum_dh2.to_sibling(0, 0)
            sum_dh2.make_far(s.keep_far, 0)
            sum_dh2.send_far(0)

        when(2, third_end)
        when(3, lambda: sum_dh2.to_sibling(0, 1))

    steps(4, feed_step)

    dp_mlp = DpSum(links, s, MLP_STREAMS, s.mlp_halves)

    def feed_grad(stream):
        name, first, w, _, _, _, _ = MLP_STREAMS[stream]
        if name == "mlp_mix":
            values = nt(s.h2[...], s.dgu[pl.ds(first, w), :])
        else:
            values = nt(s.attn_mix[:, :, :, pl.ds(0, 1024)].reshape(1024, 1024), s.hidden[pl.ds(first, w), :])
        into = getattr(s, name)
        into[pl.ds(0, 4), :, :, pl.ds(first, w)] = values.astype(BF16).reshape(4, 4, 64, w)
        dp_mlp.start(stream)

    gather_da = Gather(links, lambda b, part: s.da.at[:, sub(b, part)])

    def norm_back(part):
        sum_dh2.arrive(part)

        def inner_sum(i, total):
            grad = sum_dh2.total(s.keep_own, part, span(i))
            s.keep_own[span(i), lanes(part)] = grad
            product = grad * (s.resid[span(i), lanes(part)] * s.root2[0:1, lanes(part)])
            s.gain_sum[span(i), :] += product
            return total + fold(product * s.gain2[span(i), :])

        inner = lax.fori_loop(0, 4, inner_sum, jnp.zeros((8, HALF), F32))
        inner = jnp.sum(inner, axis=0, keepdims=True) / 1024.0

        def body(i):
            root = s.root2[0:1, lanes(part)]
            scaled = s.keep_own[span(i), lanes(part)] * s.gain2[span(i), :]
            normed = s.resid[span(i), lanes(part)] * root
            own = s.attn_mix[i, :, :, sub(me, part)].reshape(256, HALF).astype(F32)
            s.da[span(i), sub(me, part)] = (own + root * (scaled - normed * inner)).astype(BF16)
            s.mlp_own[span(i), lanes(part)] = s.resid[span(i), lanes(part)]
            s.resid[span(i), lanes(part)] = own + root * (scaled - normed * inner)

        loop(4, body)
        gather_da.send(part)

    feed_grad(0)
    sum_dh2.make_far(s.keep_far, 1)
    sum_dh2.send_far(1)
    feed_grad(1)
    norm_back(0)
    feed_grad(4)
    feed_grad(2)
    feed_grad(3)
    gather_h2.drain()
    load(wo, s.h2.at[pl.ds(0, 512)])
    norm_back(1)
    sum_dh2.drain()

    def put_gain(first, row):
        for k in range(row.shape[1] // 128):
            s.gain_own[first + k : first + k + 1, :] = row[:, 128 * k : 128 * k + 128]

    put_gain(8, jnp.sum(s.gain_sum[...].T, axis=0, keepdims=True))
    s.gain_sum[...] = jnp.zeros((1024, 128), F32)

    sum_mlp = Reduce(links, s.mlp_sib_out, s.mlp_sib_in, s.mlp_far_out, s.mlp_far_in)

    def mlp_mine(part):
        def store(values):
            s.mlp_sib_out[1, part] = values[:, :HALF].astype(BF16)
            s.mlp_own[:, lanes(part)] += values[:, HALF:]

        return store

    loop(2, lambda part: mlp_product(far_pair, part, split(s.mlp_sib_out, 0, part, s.keep_far)))
    for part in range(2):
        sum_mlp.to_sibling(0, part)
    for part in range(2):
        sum_mlp.make_far(s.keep_far, part)

    s.keep[...] = jnp.zeros((2, 1024, 256), F32)
    loads[17].wait()

    def dob(g, b, part):
        index = g * 4 + b
        return (4 + index // 4, pl.ds(2 * ((index // 2) % 2), 2), slice(None), pl.ds(pl.multiple_of((index % 2) * 512 + part * 256, 256), 256))

    def out_back(blocks, part):
        two = lanes(part, 256)
        every_grad = nn(s.h2[pl.ds(0, 512), :], pair(s.da, every, blocks, part))
        for g in range(2):
            grads = every_grad[256 * g : 256 * g + 256]
            for n, b in enumerate(blocks):
                columns = slice(HALF * n, HALF * n + HALF)
                both = jnp.concatenate([grads[:128, columns], grads[128:, columns]], axis=1) * s.inv[g, b, 0:1, two]
                outs = [s.ob[pl.ds(256 * g + 128 * k, 128), sub(b, part)] for k in range(2)]
                inner = jnp.sum(both * jnp.concatenate(outs, axis=1).astype(F32), axis=0, keepdims=True)
                s.inner[g, b, :, two] = jnp.broadcast_to(inner, (8, 256))
                s.t_gu[dob(g, b, part)] = both.astype(BF16).reshape(2, 64, 256)

    def attend_back(blocks, parts, groups):
        wide = 256 * len(parts)
        cut = lanes(parts[0], 256) if len(parts) == 1 else pl.ds(0, wide)
        chains = [(qb, g, 256 * (qb + 1)) for qb in blocks for g in groups]
        grads, weights, slopes, changes, key_parts, query_parts, value_parts = [], [], [], [], [], [], []
        for qb, g, keys in chains:
            index = g * 4 + qb
            columns = lanes((index % 2) * 2 + parts[0], 256) if len(parts) == 1 else lanes(index % 2, 512)
            at = (4 + index // 4, pl.ds(2 * ((index // 2) % 2), 2), slice(None), columns)
            grads.append(s.t_gu[at].reshape(128, wide))
            weights.append(s.p[p_slots(g, qb), :, :, cut].reshape(keys, wide))
        for (qb, g, keys), grad in zip(chains, grads):
            slopes.append(nn(s.v[g, pl.ds(0, keys), :], grad))
        for weight, grad in zip(weights, grads):
            value_parts.append(nt(weight, grad))
        for (qb, g, keys), weight, slope in zip(chains, weights, slopes):
            changes.append((weight.astype(F32) * (slope - s.inner[g, qb, 0:1, cut])).astype(BF16))
        for (qb, g, keys), change in zip(chains, changes):
            key_parts.append(nt(change, s.qs[g, qb, :, cut]))
            query_parts.append(nn(s.ks_t[pl.ds(128 * g, 128), pl.ds(0, keys)], change))
        for (qb, g, keys), value_part, key_part, query_part in zip(chains, value_parts, key_parts, query_parts):
            s.keep_own[pl.ds(0, keys), lanes(g)] += value_part
            s.keep_far[pl.ds(0, keys), lanes(g)] += key_part
            for n, part in enumerate(parts):
                columns = lanes(2 * qb + part)
                for k in range(2):
                    head = 3 * g + k
                    grad, gain_part = head_backward(
                        query_part[:, 256 * n + 128 * k : 256 * n + 128 * k + 128] * (1.0 / math.sqrt(HEAD)),
                        s.norm_qk[pl.ds(128 * head, 128), columns].astype(F32),
                        s.root_qk[pl.ds(head, 1), columns],
                        s.gain_q[...],
                        s.cosine[:, columns],
                        s.sine[:, columns],
                    )
                    s.t_qkv[pl.ds(512 * g + 128 * k, 128), columns] = grad.astype(BF16)
                    s.gain_q_sum[...] += gain_part

    def key_back(g):
        gain = twice(s.gain_k[...])

        def body(b):
            columns = span(b)
            grad, gain_part = head_backward(
                s.keep_far[columns, lanes(g)].T * math.log(2.0),
                s.norm_qk[pl.ds(384 * g + 256, 128), columns].astype(F32),
                s.root_qk[pl.ds(3 * g + 2, 1), columns],
                gain,
                s.cosine[:, columns],
                s.sine[:, columns],
            )
            s.t_qkv[pl.ds(512 * g + 256, 128), columns] = grad.astype(BF16)
            s.gain_k_sum[...] += gain_part
            s.t_qkv[pl.ds(512 * g + 384, 128), columns] = s.keep_own[columns, lanes(g)].T.astype(BF16)

        loop(4, body)

    def tell_ready():
        for k, name in enumerate(PARTNERS[2:]):
            pl.semaphore_signal(ready.at[k], inc=1, device_id=place.device(name), device_id_type=MESH)

    def wait_ready():
        for k in range(5):
            pl.semaphore_wait(ready.at[k], 1)

    def qkv_grad(g):
        values = nt(s.h1[...], s.t_qkv[span(g, 512), :]).astype(BF16)
        s.attn_mix[:, :, :, span(g, 512)] = values.reshape(4, 4, 64, 512)

    def out_grad():
        values = nt(s.da[...], s.ob[...]).astype(BF16)
        s.attn_mix[:, :, :, pl.ds(1024, 512)] = values.reshape(4, 4, 64, 512)

    for part in range(2):
        gather_da.near_ready(part)
    loop(2, lambda part: out_back(near_pair, part))
    gather_da.pass_on(0)
    both_roles(True, lambda blocks: attend_back(blocks, (0, 1), (0, 1)))
    gather_dy.drain()

    def back_step(k, when):
        when(0, lambda: gather_da.far_ready(0))
        when(1, lambda: gather_da.far_ready(1))
        out_back(far_pair, k)

        def first():
            gather_da.pass_on(1)
            sum_mlp.send_far(0)

        when(0, first)
        when(1, dp_mlp.advance)
        both_roles(False, lambda blocks: attend_back(blocks, (k,), (0, 1)))

    steps(2, back_step)
    tell_ready()
    out_grad()
    key_back(1)
    qkv_grad(1)
    wait_ready()
    dp_attn = DpSum(links, s, ATTN_STREAMS, s.p)
    dp_attn.start(0, 1, 2, 3)
    key_back(0)
    qkv_grad(0)
    dp_attn.start(4, 5, 6, 7)

    def in_back(blocks, part, store):
        values = nn(s.w_qkv[...], pair(s.t_qkv, every, blocks, part))
        product = values * pair(s.h1, every, blocks, part).astype(F32)
        s.gain_sum[...] += product[:, :HALF] + product[:, HALF:]
        store(values)

    sum_dh1 = Reduce(links, s.sib_out, s.sib_in, s.far_out, s.far_in)
    loop(2, lambda part: in_back(far_pair, part, split(s.sib_out, 0, part, s.keep_far)))
    for part in range(2):
        sum_dh1.to_sibling(0, part)
    for part in range(2):
        sum_dh1.make_far(s.keep_far, part)
        sum_dh1.send_far(part)
    sum_mlp.send_far(1)
    dp_mlp.advance()
    loop(2, lambda part: in_back(near_pair, part, split(s.sib_out, 1, part, s.keep_own)))
    for part in range(2):
        sum_dh1.to_sibling(1, part)
    loop(2, lambda part: mlp_product(near_pair, part, mlp_mine(part)))
    for part in range(2):
        sum_mlp.to_sibling(1, part)
    dp_attn.advance(0, 1, 2, 3)
    put_gain(0, jnp.sum((s.gain_sum[...] / s.gain1[...]).T, axis=0, keepdims=True))
    both = s.gain_k_sum[:, lanes(0)] + s.gain_k_sum[:, lanes(1)]
    put_gain(16, jnp.sum(s.gain_q_sum[...].T, axis=0, keepdims=True))
    put_gain(17, jnp.sum(both.T, axis=0, keepdims=True))
    s.gain_own[pl.ds(18, 6), :] = jnp.zeros((6, 128), F32)
    gains = GainSum(links, s.gain_own, s.gain_parts)
    dp_attn.advance()
    dp_mlp.advance()
    gains.advance()
    dp_attn.advance()
    dp_mlp.advance()
    gains.advance()

    for part in range(2):
        sum_dh1.arrive(part)

        def inner_sum(i, total, part=part):
            grad = sum_dh1.total(s.keep_own, part, span(i))
            s.keep_own[span(i), lanes(part)] = grad
            normed = s.x_t[span(i), lanes(part)].astype(F32) * s.root1[0:1, lanes(part)]
            return total + fold(grad * normed * s.gain1[span(i), :])

        inner = lax.fori_loop(0, 4, inner_sum, jnp.zeros((8, HALF), F32))
        inner = jnp.sum(inner, axis=0, keepdims=True) / 1024.0

        def last_back(i, part=part, inner=inner):
            root = s.root1[0:1, lanes(part)]
            scaled = s.keep_own[span(i), lanes(part)] * s.gain1[span(i), :]
            normed = s.x_t[span(i), lanes(part)].astype(F32) * root
            s.resid[span(i), lanes(part)] += root * (scaled - normed * inner)

        loop(4, last_back)
        if part == 0:
            dp_attn.advance()
            gains.advance()
    load(s.resid, grad_x)

    for part in range(2):
        sum_mlp.arrive(part)

        def layer_out(i, part=part):
            s.stage[lanes(part), span(i)] = sum_mlp.total(s.mlp_own, part, span(i)).T.astype(BF16)

        loop(4, layer_out)
    load(s.stage, out)
    while min(dp_attn.phases + dp_mlp.phases) < 5 or gains.step < 4:
        dp_attn.advance()
        gains.advance()
        dp_mlp.advance()
    load(s.sums, out_sums)
    s.gain_own[...] = gains.total
    load(s.gain_own, out_gains)

    for copy in loads[18:]:
        copy.wait()
    for exchange in (gather_h1, gather_da, sum_mlp, sum_dh1, dp_mlp, dp_attn, gains):
        exchange.drain()


def deliver_kernel(*refs):
    given, outs, held = refs[:4], refs[4:17], refs[17:21]
    turned, gain_rows, sems_in, sems_out = refs[21:]
    arrivals = {k: pltpu.make_async_copy(given[k], held[k], sems_in.at[k]) for k in (0, 2, 3)}
    pieces = []
    for i in range(4):
        rows = pl.ds(256 * i, 256)
        pieces.append(pltpu.make_async_copy(given[1].at[rows], held[1].at[rows], sems_in.at[4 + i]))
        pieces[i].start()
    for copy in arrivals.values():
        copy.start()
    started = []

    def send(src, dst):
        copy = pltpu.make_async_copy(src, dst, sems_out.at[len(started)])
        copy.start()
        started.append(copy)

    for i in range(4):
        columns = pl.ds(256 * i, 256)
        pieces[i].wait()
        turned[:, columns] = held[1][columns, :].T
        send(turned.at[:, columns], outs[1].at[:, columns])
    arrivals[3].wait()
    gain_rows[0] = held[3][16:17]
    gain_rows[1] = held[3][17:18]
    send(held[3].at[pl.ds(0, 8)], outs[9])
    send(held[3].at[pl.ds(8, 8)], outs[10])
    send(gain_rows.at[0], outs[11])
    send(gain_rows.at[1], outs[12])
    arrivals[2].wait()
    sums = held[2]
    for g in range(2):
        for out, first, width in ((outs[2], 0, 256), (outs[3], 256, 128), (outs[4], 384, 128)):
            send(sums.at[:, pl.ds(512 * g + first, width)], out.at[:, pl.ds(width * g, width)])
    for out, first, width in ((outs[5], 1024, 512), (outs[6], 1536, 768), (outs[7], 2304, 768), (outs[8], 3072, 768)):
        send(sums.at[:, pl.ds(first, width)], out)
    arrivals[0].wait()
    send(held[0], outs[0])
    for copy in started:
        copy.wait()


def shards(
    tokens,
    doc_starts,
    cotangent,
    w_query,
    key_matrix,
    value_matrix,
    w_out,
    w_gate,
    w_up,
    w_down,
    gain_attn,
    gain_mlp,
    gain_query,
    gain_key,
):
    frequency = ROPE_BASE ** (-(np.arange(64, dtype=np.float64) * 2.0) / HEAD)
    frequency = jnp.asarray(np.broadcast_to(frequency[:, None], (64, 128)).astype(np.float32))
    hbm = pl.BlockSpec(memory_space=pl.ANY)
    smem = pl.BlockSpec(memory_space=pltpu.SMEM)

    def shaped(*shape, kind=F32):
        return jax.ShapeDtypeStruct(shape, kind)

    gains = (shaped(8, 128), shaped(8, 128), shaped(1, 128), shaped(1, 128))
    given = (shaped(256, 1024, kind=BF16), shaped(1024, 256), shaped(32, 3840), shaped(24, 128))
    widths = (512, 256, 256, 512, 768, 768, 768)
    outs = pl.pallas_call(
        layer_kernel,
        out_shape=given,
        in_specs=[hbm, smem] + [hbm] * 13,
        out_specs=(hbm,) * 4,
        scratch_shapes=[pltpu.VMEM(shape, kind) for _, shape, kind in SCRATCH]
        + [
            pltpu.SemaphoreType.DMA((2, SEMAPHORES)),
            pltpu.SemaphoreType.DMA((24,)),
            pltpu.SemaphoreType.REGULAR((5,)),
        ],
        compiler_params=pltpu.CompilerParams(
            collective_id=0, has_side_effects=True, vmem_limit_bytes=64 * 2**20 - 2**16
        ),
        cost_estimate=pl.CostEstimate(flops=32 * 10**9, bytes_accessed=2**24, transcendentals=2**22),
        name="layer",
    )(
        tokens.reshape(256, 1024),
        doc_starts,
        cotangent.reshape(256, 1024),
        w_query,
        key_matrix,
        value_matrix,
        w_out,
        w_gate.reshape(4, 4, 64, 768),
        w_up.reshape(4, 4, 64, 768),
        w_down,
        gain_attn.reshape(1, 1024),
        gain_mlp.reshape(1, 1024),
        gain_query.reshape(1, 128),
        gain_key.reshape(1, 128),
        frequency,
    )
    outs = pl.pallas_call(
        deliver_kernel,
        out_shape=(given[0], shaped(256, 1024)) + tuple(shaped(32, width) for width in widths) + gains,
        in_specs=[hbm] * 4,
        out_specs=(hbm,) * 13,
        scratch_shapes=[pltpu.VMEM(one.shape, one.dtype) for one in given]
        + [
            pltpu.VMEM((256, 1024), F32),
            pltpu.VMEM((2, 1, 128), F32),
            pltpu.SemaphoreType.DMA((8,)),
            pltpu.SemaphoreType.DMA((20,)),
        ],
        name="deliver",
    )(*outs)
    return (
        outs[0].reshape(1, 256, 1024),
        outs[1].reshape(1, 256, 1024),
        *outs[2:5],
        outs[5].T,
        *outs[6:8],
        outs[8].T,
        *(gain.reshape(-1) for gain in outs[9:]),
    )


def solution(mesh):
    in_specs = (
        P("dp", "tensor", None),
        P("dp", None),
        P("dp", "tensor", None),
        P(None, "tensor"),
        P(None, "tensor"),
        P(None, "tensor"),
        P("tensor", None),
        P(None, "tensor"),
        P(None, "tensor"),
        P("tensor", None),
        P(),
        P(),
        P(),
        P(),
    )
    out_specs = (
        P("dp", "tensor", None),
        P("dp", "tensor", None),
        P("dp", "tensor"),
        P("dp", "tensor"),
        P("dp", "tensor"),
        P("tensor", "dp"),
        P("dp", "tensor"),
        P("dp", "tensor"),
        P("tensor", "dp"),
        P(),
        P(),
        P(),
        P(),
    )
    return jax.shard_map(shards, mesh=mesh, in_specs=in_specs, out_specs=out_specs, check_vma=False)
```
